32 devices in a mesh: dp: 2 (over core), row: 4 (over z), col: 4 (over y, x).
Axes of the slice: x: 2, y: 2, z: 4, core: 2. Of those that a mesh axis runs over, the one named last changes fastest.
Arguments:
- inputs: bfloat16 [1024, 6144], P(('dp', 'row'), 'col'), may hold values from -6 to 6
- up_weight: bfloat16 [6144, 24576], P('col', ('dp', 'row')), may hold values from -0.078125 to 0.078125
- down_weight: bfloat16 [24576, 6144], P(('dp', 'row'), 'col'), may hold values from -0.0390625 to 0.0390625
- cotangent: bfloat16 [1024, 6144], P(('dp', 'row'), 'col'), may hold values from -3 to 3
Outputs:
- input_grad: bfloat16 [1024, 6144], P(('dp', 'row'), 'col')
- up_grad: bfloat16 [6144, 24576], P('col', ('dp', 'row'))
- down_grad: bfloat16 [24576, 6144], P(('dp', 'row'), 'col')
The draws below stay inside these ranges and needn't reach their ends.
All inputs are finite; a program needn't handle non-finite values.
Results may differ from the reference program's by a relative error of at most 0.0049.
Values may be sent and summed in bfloat16 or wider, within the bound.
No kernel may reach another device: no remote copies, remote signals or barrier semaphores. Data moves between devices by JAX's collectives and lax.ppermute only.
A program may use at most 128 MiB of HBM per device.

```python
import math
import jax
import jax.numpy as jnp
from jax import lax

D = 6144
FF = 24576
TOKENS = 1024
N_DP = 2


def level_of(key, dims, split, low, top_value):
    def one(axis_at, shards_of):
        steps = jax.random.uniform(jax.random.fold_in(jax.random.fold_in(key, 6), axis_at), (shards_of,), jnp.float32, low / len(split), top_value / len(split))
        return jnp.repeat(jnp.exp(steps), dims[axis_at] // shards_of).reshape((-1,) + (1,) * (len(dims) - axis_at - 1))

    factor_of = one(*split[0])
    for cut in split[1:]:
        factor_of = factor_of * one(*cut)
    return factor_of


def normal_values(own_key, shape, scale, limit, split=(), kind=jnp.bfloat16):
    entries = jax.random.normal(own_key, shape, jnp.float32) * scale
    if len(split) > 0:
        entries = level_of(own_key, shape, split, -0.22, 0.18) * entries
    return jnp.clip(entries, min=-limit, max=limit).astype(kind)


def setup_inputs(seed: int = 0) -> dict:
    splits = jax.random.split(jax.random.key(seed), 5)
    return {
        "inputs": normal_values(splits[0], (TOKENS, D), 1.0, 6.0, ((0, 8), (1, 4))),
        "up_weight": normal_values(splits[1], (D, FF), D ** -0.5, 0.078125, ((0, 4), (1, 8))),
        "down_weight": normal_values(splits[2], (FF, D), FF ** -0.5, 0.0390625, ((0, 8), (1, 4))),
        "cotangent": normal_values(splits[3], (TOKENS, D), 0.5, 3.0, ((0, 8), (1, 4))),
    }


gelu_const = math.sqrt(2.0 / math.pi)

def gelu_tanh(value):
    inner = gelu_const * (value + 0.044715 * value * value * value)
    return 0.5 * value * (1.0 + jnp.tanh(inner))

def gelu_slope(value):
    tangent = jnp.tanh(gelu_const * (value + 0.044715 * value * value * value))
    return 0.5 * (1.0 + tangent) + 0.5 * value * (1.0 - tangent * tangent) * gelu_const * (1.0 + 3.0 * 0.044715 * value * value)

def reference(inputs, up_weight, down_weight, cotangent):
    hidden = jnp.dot(inputs, up_weight, preferred_element_type=jnp.float32)
    active = gelu_tanh(hidden).astype(jnp.bfloat16)
    delta_act = lax.dot_general(cotangent, down_weight, (((1,), (1,)), ((), ())), preferred_element_type=jnp.float32)
    delta = (delta_act * gelu_slope(hidden)).astype(jnp.bfloat16)
    input_grad = lax.dot_general(delta, up_weight, (((1,), (1,)), ((), ())), preferred_element_type=jnp.float32).astype(jnp.bfloat16)
    up_total = lax.dot_general(inputs, delta, (((0,), (0,)), ((), ())), preferred_element_type=jnp.float32)
    down_total = lax.dot_general(active, cotangent, (((0,), (0,)), ((), ())), preferred_element_type=jnp.float32)
    up_grad = (up_total / N_DP).astype(jnp.bfloat16)
    down_grad = (down_total / N_DP).astype(jnp.bfloat16)
    return (input_grad, up_grad, down_grad)
```

```python
import math

import jax
import jax.numpy as jnp
from jax import lax
from jax.sharding import PartitionSpec as P

gelu_const = math.sqrt(2.0 / math.pi)


def gelu_both(value):
    square = value * value
    tangent = jnp.tanh(gelu_const * (value + 0.044715 * square * value))
    half = 0.5 * (1.0 + tangent)
    slope = half + 0.5 * value * (1.0 - tangent * tangent) * gelu_const * (1.0 + 3.0 * 0.044715 * square)
    return value * half, slope


def contract(left, right, at_left, at_right):
    return lax.dot_general(
        left, right, (((at_left,), (at_right,)), ((), ())), preferred_element_type=jnp.float32
    )


def shards(inputs, up_weight, down_weight, cotangent):
    n_row = lax.axis_size("row")
    replicas = lax.axis_size("dp")
    n_col = lax.axis_size("col")
    assert replicas == 2 and n_col == 4 and n_row % 4 in (0, n_row)
    rows, width = inputs.shape
    quarter = rows // n_col
    own = lax.axis_index("col")
    f32, b16 = jnp.float32, jnp.bfloat16

    def swap_x(a):
        return lax.ppermute(a, "col", [(i, i ^ 1) for i in range(n_col)])

    def swap_y(a):
        return lax.ppermute(a, "col", [(i, i ^ 2) for i in range(n_col)])

    def swap_dp(a):
        return lax.ppermute(a, "dp", [(0, 1), (1, 0)])

    def pass_row(a):
        return lax.ppermute(a, "row", [(i, (i + 1) % n_row) for i in range(n_row)])

    def reorder(a, order):
        blocks = [lax.dynamic_slice_in_dim(a, (own ^ bits) * quarter, quarter, 0) for bits in order]
        return jnp.concatenate(blocks, axis=0)

    x_outer, y_outer = (0, 2, 1, 3), (0, 1, 2, 3)
    moving = jnp.concatenate([reorder(inputs, x_outer), reorder(cotangent, y_outer)], axis=0)

    group = max(1, n_row // 4)
    tall = group * rows
    inputs_of, cotangent_of, active_of, delta_of = [], [], [], []
    input_own, running = None, None
    for first in range(0, n_row, group):
        blocks = []
        for step in range(first, first + group):
            blocks += [moving, swap_dp(moving)]
            if step + 1 < n_row:
                moving = pass_row(moving)
        both = jnp.stack([block.reshape(2 * n_col, quarter, width) for block in blocks], axis=1)
        both = both.reshape(2, 2 * tall, width)
        chunk_in, chunk_cot = both[0], both[1]
        hidden_sent = swap_x(contract(chunk_in[tall:], up_weight, 1, 0).astype(b16))
        act_sent = swap_y(contract(chunk_cot[tall:], down_weight, 1, 1).astype(b16))
        hidden = contract(chunk_in[:tall], up_weight, 1, 0)
        delta_act = contract(chunk_cot[:tall], down_weight, 1, 1)
        hidden = hidden + hidden_sent.astype(f32)
        delta_act = delta_act + act_sent.astype(f32)
        half = tall // 2
        hidden = hidden[:half] + swap_y(hidden[half:].astype(b16)).astype(f32)
        delta_act = delta_act[:half] + swap_x(delta_act[half:].astype(b16)).astype(f32)
        value, slope = gelu_both(hidden)
        active = value.astype(b16)
        delta = (delta_act * slope).astype(b16)
        delta = jnp.concatenate([delta, swap_y(delta)], axis=0)
        active = jnp.concatenate([active, swap_x(active)], axis=0)
        delta = jnp.concatenate([delta, swap_x(delta)], axis=0)
        active = jnp.concatenate([active, swap_y(active)], axis=0)
        inputs_of.append(chunk_in)
        cotangent_of.append(chunk_cot)
        active_of.append(active)
        delta_of.append(delta)
        parts = contract(delta, up_weight, 1, 1).reshape(n_col, group, 2, quarter, width)
        parts = parts[:, :, 0] + swap_dp(parts[:, :, 1])
        for step in range(first, first + group):
            part = parts[:, step - first].reshape(rows, width)
            if step == 0:
                input_own = part
            else:
                running = pass_row(part if running is None else running + part)

    input_grad = (input_own if running is None else input_own + running).astype(b16)
    input_grad = reorder(input_grad.reshape(2, 2, quarter, width).transpose(1, 0, 2, 3).reshape(rows, width), y_outer)

    def grad(left, right):
        total = contract(left[-1], right[-1], 0, 0)
        if n_row > 1:
            total = total + contract(jnp.concatenate(left[:-1]), jnp.concatenate(right[:-1]), 0, 0)
        return (total / replicas).astype(b16)

    return (input_grad, grad(inputs_of, delta_of), grad(active_of, cotangent_of))


def solution(mesh):
    tokens = P(("dp", "row"), "col")
    up, down = P("col", ("dp", "row")), P(("dp", "row"), "col")
    return jax.shard_map(
        shards,
        mesh=mesh,
        in_specs=(tokens, up, down, tokens),
        out_specs=(tokens, up, down),
        check_vma=False,
    )
```

```python
import math

import jax
import jax.numpy as jnp
from jax import lax
from jax.experimental import pallas as pl
from jax.experimental.pallas import tpu as pltpu
from jax.sharding import PartitionSpec as P

gelu_const = math.sqrt(2.0 / math.pi)
f32, b16 = jnp.float32, jnp.bfloat16
VMEM_LIMIT = 50 * 2**20


def gelu_both(value):
    square = value * value
    tangent = jnp.tanh(gelu_const * (value + 0.044715 * square * value))
    half = 0.5 * (1.0 + tangent)
    slope = half + 0.5 * value * (1.0 - tangent * tangent) * gelu_const * (1.0 + 3.0 * 0.044715 * square)
    return value * half, slope


def contract(left, right, at_left, at_right):
    return lax.dot_general(
        left, right, (((at_left,), (at_right,)), ((), ())), preferred_element_type=f32
    )


def tile_of(size, most):
    return max(t for t in range(128, most + 1, 128) if size % t == 0)


def call(body, operands, in_specs, outs, out_specs, grid, after=(), scratch=(), aliases=None, name=None):
    count = len(operands)

    def kernel(*refs):
        body(*refs[:count], *refs[count + len(after):])

    return pl.pallas_call(
        kernel,
        grid=grid,
        in_specs=list(in_specs) + [pl.BlockSpec(memory_space=pl.ANY)] * len(after),
        out_specs=out_specs,
        out_shape=outs,
        scratch_shapes=list(scratch),
        input_output_aliases=aliases or {},
        compiler_params=pltpu.CompilerParams(vmem_limit_bytes=VMEM_LIMIT),
        cost_estimate=pl.CostEstimate(flops=1000, bytes_accessed=1000, transcendentals=0),
        name=name,
    )(*operands, *after)


def shape(dims, dtype):
    return jax.ShapeDtypeStruct(dims, dtype)


def first_product(chunk, weight, weight_dim, store, at, chunks, after, name):
    tokens, width = chunk.shape
    hidden = weight.shape[1 - weight_dim]
    half = tokens // 2
    tile = tile_of(hidden, 512)

    def body(*refs):
        chunk_ref, weight_ref = refs[:2]
        sent_ref, kept_ref, store_ref = refs[-3:]
        total = contract(chunk_ref[...], weight_ref[...], 1, weight_dim)
        kept_ref[...] = total[:half]
        sent_ref[...] = total[half:].astype(b16)

        @pl.when(pl.program_id(0) == 0)
        def _():
            store_ref[...] = chunk_ref[...]

    weight_spec = (
        pl.BlockSpec((width, tile), lambda i: (0, i)) if weight_dim == 0 else pl.BlockSpec((tile, width), lambda i: (i, 0))
    )
    operands = [chunk, weight]
    in_specs = [pl.BlockSpec((tokens, width), lambda i: (0, 0)), weight_spec]
    aliases = None
    if store is not None:
        operands.append(store)
        in_specs.append(pl.BlockSpec(memory_space=pl.ANY))
        aliases = {2: 2}
    return call(
        body,
        operands,
        in_specs,
        [shape((half, hidden), b16), shape((half, hidden), f32), shape((chunks * tokens, width), b16)],
        [
            pl.BlockSpec((half, tile), lambda i: (0, i)),
            pl.BlockSpec((half, tile), lambda i: (0, i)),
            pl.BlockSpec((tokens, width), lambda i: (at, 0)),
        ],
        (hidden // tile,),
        after,
        aliases=aliases,
        name=name,
    )


def add_halves(kept_h, came_h, kept_g, came_g, after):
    tokens, hidden = kept_h.shape
    half = tokens // 2
    tile = tile_of(hidden, 768)

    def body(kh, ch, kg, cg, sent_h, next_h, sent_g, next_g):
        for kept, came, sent, rest in ((kh, ch, sent_h, next_h), (kg, cg, sent_g, next_g)):
            total = kept[...] + came[...].astype(f32)
            rest[...] = total[:half]
            sent[...] = total[half:].astype(b16)

    block = pl.BlockSpec((tokens, tile), lambda i: (0, i))
    part = pl.BlockSpec((half, tile), lambda i: (0, i))
    return call(
        body,
        [kept_h, came_h, kept_g, came_g],
        [block] * 4,
        [shape((half, hidden), b16), shape((half, hidden), f32)] * 2,
        [part] * 4,
        (hidden // tile,),
        after,
        name="add_halves",
    )


def activate(kept_h, came_h, kept_g, came_g, after):
    tokens, hidden = kept_h.shape
    tile = tile_of(hidden, 768)

    def body(kh, ch, kg, cg, active_ref, delta_ref):
        value, slope = gelu_both(kh[...] + ch[...].astype(f32))
        active_ref[...] = value.astype(b16)
        delta_ref[...] = ((kg[...] + cg[...].astype(f32)) * slope).astype(b16)

    block = pl.BlockSpec((tokens, tile), lambda i: (0, i))
    return call(
        body,
        [kept_h, came_h, kept_g, came_g],
        [block] * 4,
        [shape((tokens, hidden), b16)] * 2,
        [block] * 2,
        (hidden // tile,),
        after,
        name="activate",
    )


def input_product(deltas, up_weight, actives, stores, at, chunks, after):
    quarter, hidden = deltas[0].shape
    width = up_weight.shape[0]
    tokens = 4 * quarter
    tile = tile_of(width, 256)

    def body(*refs):
        delta_refs, weight_ref, active_refs = refs[:4], refs[4], refs[5:9]
        part_ref, delta_store, active_store = refs[-3:]

        @pl.when(pl.program_id(0) == 0)
        def _():
            for i in range(4):
                delta_store[pl.ds(i * quarter, quarter), :] = delta_refs[i][...]
                active_store[pl.ds(i * quarter, quarter), :] = active_refs[i][...]

        part_ref[...] = contract(delta_store[...], weight_ref[...], 1, 1)

    piece = pl.BlockSpec((quarter, hidden), lambda i: (0, 0))
    operands = [*deltas, up_weight, *actives]
    in_specs = [piece] * 4 + [pl.BlockSpec((tile, hidden), lambda i: (i, 0))] + [piece] * 4
    aliases = None
    if stores is not None:
        operands += stores
        in_specs += [pl.BlockSpec(memory_space=pl.ANY)] * 2
        aliases = {9: 1, 10: 2}
    stored = pl.BlockSpec((tokens, hidden), lambda i: (at, 0))
    return call(
        body,
        operands,
        in_specs,
        [shape((tokens, width), f32)] + [shape((chunks * tokens, hidden), b16)] * 2,
        [pl.BlockSpec((tokens, tile), lambda i: (0, i)), stored, stored],
        (width // tile,),
        after,
        aliases=aliases,
        name="input_product",
    )


def weight_product(left, right, tokens, at, partial, scale, most, after, name):
    rows, columns = left.shape[1], right.shape[1]
    tile = tile_of(rows, most)

    def body(*refs):
        total = contract(refs[0][...], refs[1][...], 0, 0)
        if partial is not None:
            total = total + refs[2][...]
        refs[-1][...] = (total if scale is None else total * scale).astype(refs[-1].dtype)

    block = pl.BlockSpec((tile, columns), lambda i: (i, 0))
    operands = [left, right] + ([] if partial is None else [partial])
    return call(
        body,
        operands,
        [pl.BlockSpec((tokens, tile), lambda i: (at, i)), pl.BlockSpec((tokens, columns), lambda i: (at, 0))]
        + [block] * (partial is not None),
        shape((rows, columns), f32 if scale is None else b16),
        block,
        (rows // tile,),
        after,
        name=name,
    )


def shards(inputs, up_weight, down_weight, cotangent):
    n_row = lax.axis_size("row")
    replicas = lax.axis_size("dp")
    n_col = lax.axis_size("col")
    assert replicas == 2 and n_col == 4 and n_row % 4 == 0
    rows, width = inputs.shape
    quarter = rows // n_col
    own = lax.axis_index("col")

    def swap_x(a):
        return lax.ppermute(a, "col", [(i, i ^ 1) for i in range(n_col)])

    def swap_y(a):
        return lax.ppermute(a, "col", [(i, i ^ 2) for i in range(n_col)])

    def swap_dp(a):
        return lax.ppermute(a, "dp", [(0, 1), (1, 0)])

    def pass_row(a):
        return lax.ppermute(a, "row", [(i, (i + 1) % n_row) for i in range(n_row)])

    def reorder(a, order):
        blocks = [lax.dynamic_slice_in_dim(a, (own ^ bits) * quarter, quarter, 0) for bits in order]
        return jnp.concatenate(blocks, axis=0)

    x_outer, y_outer = (0, 2, 1, 3), (0, 1, 2, 3)

    def reorder_both():
        def body(own_ref, inputs_ref, cotangent_ref, out_ref):
            for i in range(n_col):
                for ref, order, base in ((inputs_ref, x_outer, 0), (cotangent_ref, y_outer, rows)):
                    source = pl.multiple_of((own_ref[0] ^ order[i]) * quarter, quarter)
                    out_ref[pl.ds(base + i * quarter, quarter), :] = ref[pl.ds(source, quarter), :]

        whole = pl.BlockSpec(memory_space=pltpu.VMEM)
        return call(
            body,
            [own.astype(jnp.int32).reshape(1), inputs, cotangent],
            [pl.BlockSpec(memory_space=pltpu.SMEM), whole, whole],
            shape((2 * rows, width), b16),
            whole,
            (),
            name="reorder",
        )

    if quarter % 16 == 0:
        moving = reorder_both()
    else:
        moving = jnp.concatenate([reorder(inputs, x_outer), reorder(cotangent, y_outer)], axis=0)

    group = n_row // 4
    chunks = n_row // group
    work = [{} for _ in range(chunks)]
    stores = {"inputs": None, "cotangent": None, "gathered": None}
    last = ()

    def bring(at):
        nonlocal moving
        blocks = []
        for step in range(at * group, (at + 1) * group):
            blocks += [moving, swap_dp(moving)]
            if step + 1 < n_row:
                moving = pass_row(moving)
        both = jnp.stack([block.reshape(2 * n_col, quarter, width) for block in blocks], axis=1)
        return both.reshape(2, 2 * group * rows, width)

    def stage_a(at):
        nonlocal last
        both, w = bring(at), work[at]
        sent, w["h"], stores["inputs"] = first_product(
            both[0], up_weight, 0, stores["inputs"], at, chunks, last, "hidden_product"
        )
        w["h_came"] = swap_x(sent)
        sent, w["g"], stores["cotangent"] = first_product(
            both[1], down_weight, 1, stores["cotangent"], at, chunks, (sent,), "delta_act_product"
        )
        w["g_came"] = swap_y(sent)
        last = (sent,)

    def stage_b(at):
        nonlocal last
        w = work[at]
        sent_h, w["h"], sent_g, w["g"] = add_halves(w["h"], w["h_came"], w["g"], w["g_came"], last)
        w["h_came"], w["g_came"] = swap_y(sent_h), swap_x(sent_g)
        last = (sent_h,)

    def stage_c(at):
        nonlocal last
        w = work[at]
        active, delta = activate(w["h"], w["h_came"], w["g"], w["g_came"], last)
        delta_y, active_x = swap_y(delta), swap_x(active)
        delta_x, active_y = swap_x(delta), swap_y(active)
        w["delta"] = [delta, delta_y, delta_x, swap_x(delta_y)]
        w["active"] = [active, active_x, active_y, swap_y(active_x)]
        last = (delta,)

    input_own, running = None, None

    def stage_d(at):
        nonlocal last, input_own, running
        w = work[at]
        after = last if running is None else (*last, running)
        parts, *stores["gathered"] = input_product(
            w["delta"], up_weight, w["active"], stores["gathered"], at, chunks, after
        )
        last = (parts,)
        parts = parts.reshape(n_col, group, 2, quarter, width)
        parts = parts[:, :, 0] + swap_dp(parts[:, :, 1])
        for step in range(at * group, (at + 1) * group):
            part = parts[:, step - at * group].reshape(rows, width)
            if step == 0:
                input_own = part
            else:
                running = pass_row(part if running is None else running + part)

    for stage, at in (
        (stage_a, 0), (stage_b, 0), (stage_a, 1), (stage_c, 0), (stage_a, 2), (stage_b, 1), (stage_a, 3),
        (stage_c, 1), (stage_b, 2), (stage_d, 0), (stage_c, 2), (stage_b, 3), (stage_d, 1), (stage_c, 3), (stage_d, 2),
    ):
        stage(at)
    tall = 2 * group * rows
    delta_all, active_all = stores["gathered"]
    early = (chunks - 1) * tall
    up_partial = weight_product(stores["inputs"], delta_all, early, 0, None, None, 256, last, "up_grad_early")
    down_partial = weight_product(active_all, stores["cotangent"], early, 0, None, None, 512, (up_partial,), "down_grad_early")
    last = (down_partial,)
    stage_d(3)
    delta_all, active_all = stores["gathered"]
    up_grad = weight_product(
        stores["inputs"], delta_all, tall, chunks - 1, up_partial, 1.0 / replicas, 256, last, "up_grad"
    )
    down_grad = weight_product(
        active_all, stores["cotangent"], tall, chunks - 1, down_partial, 1.0 / replicas, 512, (up_grad,), "down_grad"
    )

    input_grad = (input_own + running).astype(b16)
    input_grad = reorder(input_grad.reshape(2, 2, quarter, width).transpose(1, 0, 2, 3).reshape(rows, width), y_outer)
    return (input_grad, up_grad, down_grad)


def solution(mesh):
    tokens = P(("dp", "row"), "col")
    up, down = P("col", ("dp", "row")), P(("dp", "row"), "col")
    return jax.shard_map(
        shards,
        mesh=mesh,
        in_specs=(tokens, up, down, tokens),
        out_specs=(tokens, up, down),
        check_vma=False,
    )
```

```python
import math

import jax
import jax.numpy as jnp
from jax import lax
from jax.experimental import pallas as pl
from jax.experimental.pallas import tpu as pltpu
from jax.sharding import PartitionSpec as P

gelu_const = math.sqrt(2.0 / math.pi)
f32, b16 = jnp.float32, jnp.bfloat16


def gelu_both(value):
    square = value * value
    tangent = jnp.tanh(gelu_const * (value + 0.044715 * square * value))
    half = 0.5 * (1.0 + tangent)
    slope = half + 0.5 * value * (1.0 - tangent * tangent) * gelu_const * (1.0 + 3.0 * 0.044715 * square)
    return value * half, slope


def contract(left, right, at_left, at_right):
    return lax.dot_general(
        left, right, (((at_left,), (at_right,)), ((), ())), preferred_element_type=f32
    )


def shards(inputs, up_weight, down_weight, cotangent):
    n_row = lax.axis_size("row")
    replicas = lax.axis_size("dp")
    n_col = lax.axis_size("col")
    assert replicas == 2 and n_col == 4 and n_row % 4 == 0
    rows, width = inputs.shape
    quarter = rows // n_col
    own = lax.axis_index("col")

    def swap_x(a):
        return lax.ppermute(a, "col", [(i, i ^ 1) for i in range(n_col)])

    def swap_y(a):
        return lax.ppermute(a, "col", [(i, i ^ 2) for i in range(n_col)])

    def swap_dp(a):
        return lax.ppermute(a, "dp", [(0, 1), (1, 0)])

    def pass_row(a):
        return lax.ppermute(a, "row", [(i, (i + 1) % n_row) for i in range(n_row)])

    def reorder(a, order):
        blocks = [lax.dynamic_slice_in_dim(a, (own ^ bits) * quarter, quarter, 0) for bits in order]
        return jnp.concatenate(blocks, axis=0)

    x_outer, y_outer = (0, 2, 1, 3), (0, 1, 2, 3)

    def reorder_both():
        def body(own_ref, inputs_ref, cotangent_ref, out_ref):
            for i in range(n_col):
                for ref, order, base in ((inputs_ref, x_outer, 0), (cotangent_ref, y_outer, rows)):
                    source = pl.multiple_of((own_ref[0] ^ order[i]) * quarter, quarter)
                    out_ref[pl.ds(base + i * quarter, quarter), :] = ref[pl.ds(source, quarter), :]

        whole = pl.BlockSpec(memory_space=pltpu.VMEM)
        return pl.pallas_call(
            body,
            in_specs=[pl.BlockSpec(memory_space=pltpu.SMEM), whole, whole],
            out_specs=whole,
            out_shape=jax.ShapeDtypeStruct((2 * rows, width), b16),
            name="reorder",
        )(own.astype(jnp.int32).reshape(1), inputs, cotangent)

    if quarter % 16 == 0:
        moving = reorder_both()
    else:
        moving = jnp.concatenate([reorder(inputs, x_outer), reorder(cotangent, y_outer)], axis=0)

    group = n_row // 4
    tall = group * rows
    half = tall // 2
    work = [{} for _ in range(4)]
    blocks = {0: [moving]}

    token = ()

    def after(*values):
        tied = lax.optimization_barrier((*values, *token))[: len(values)]
        return tied if len(values) > 1 else tied[0]

    def fetch(at):
        if at > 0:
            blocks[at] = [pass_row(after(blocks[at - 1][-1]))]
        while len(blocks[at]) < group:
            blocks[at].append(pass_row(blocks[at][-1]))

    def mirror(at):
        work[at]["mine"] = jnp.stack(blocks[at])
        work[at]["other"] = swap_dp(after(work[at]["mine"]))

    def build(at):
        nonlocal token
        w = work[at]
        pair = [a.reshape(group, 2 * n_col, quarter, width) for a in after(w["mine"], w["other"])]
        both = jnp.stack([a.transpose(1, 0, 2, 3) for a in pair], axis=2).reshape(2, 2 * tall, width)
        w["in"], w["cot"] = both[0], both[1]
        token = (both,)

    def products(at, first):
        nonlocal token
        w = work[at]
        w_in, w_cot = after(w["in"], w["cot"])
        span = slice(tall, None) if first else slice(0, tall)
        hidden = contract(w_in[span], up_weight, 1, 0)
        delta_act = contract(w_cot[span], down_weight, 1, 1)
        if first:
            hidden, delta_act = hidden.astype(b16), delta_act.astype(b16)
        names = ("h_out", "g_out") if first else ("h", "g")
        w[names[0]], w[names[1]] = token = (hidden, delta_act)

    def reduce_first(at, before=()):
        w = work[at]
        h_out, g_out, *_ = after(w["h_out"], w["g_out"], *before)
        w["h_came"], w["g_came"] = swap_x(h_out), swap_y(g_out)

    def reduce_second(at):
        nonlocal token
        w = work[at]
        kept_h, kept_g, h_came, g_came = after(w["h"], w["g"], w["h_came"], w["g_came"])
        hidden, delta_act = kept_h + h_came.astype(f32), kept_g + g_came.astype(f32)
        w["h"], w["g"] = hidden[:half], delta_act[:half]
        token = (hidden[half:].astype(b16), delta_act[half:].astype(b16))
        w["h_came"], w["g_came"] = swap_y(token[0]), swap_x(token[1])

    def gather_first(at):
        nonlocal token
        w = work[at]
        kept_h, kept_g, h_came, g_came = after(w["h"], w["g"], w["h_came"], w["g_came"])
        value, slope = gelu_both(kept_h + h_came.astype(f32))
        w["active"] = value.astype(b16)
        w["delta"] = ((kept_g + g_came.astype(f32)) * slope).astype(b16)
        token = (w["delta"], w["active"])
        w["delta_came"], w["active_came"] = swap_y(w["delta"]), swap_x(w["active"])

    def join(at):
        nonlocal token
        w = work[at]
        own_d, came_d, own_a, came_a = after(w["delta"], w["delta_came"], w["active"], w["active_came"])
        w["delta"], w["active"] = token = (jnp.concatenate([own_d, came_d]), jnp.concatenate([own_a, came_a]))

    def gather_second(at):
        w = work[at]
        join(at)
        w["delta_came"], w["active_came"] = swap_x(w["delta"]), swap_y(w["active"])

    def share(at):
        nonlocal token
        w = work[at]
        parts = contract(after(w["delta"]), up_weight, 1, 1).reshape(n_col, group, 2, quarter, width)
        w["part"] = parts[:, :, 0]
        token = (parts[:, :, 1],)
        w["part_came"] = swap_dp(token[0])

    def share_sum(at):
        nonlocal token
        w = work[at]
        part, came = after(w["part"], w["part_came"])
        w["part"] = part + came
        token = (w["part"],)

    def early_grads(names):
        nonlocal token
        left, right = (jnp.concatenate(after(work[0][k], work[1][k])) for k in names)
        token = (contract(left, right, 0, 0),)
        return token[0]

    def late_grads(names, partial):
        nonlocal token
        left, right = (jnp.concatenate(after(work[2][k], work[3][k])) for k in names)
        token = (((partial + contract(left, right, 0, 0)) / replicas).astype(b16),)
        return token[0]

    def step_part(step):
        return work[step // group]["part"][:, step % group].reshape(rows, width)

    fetch(0)
    mirror(0)
    fetch(1)
    build(0)
    products(0, True)
    reduce_first(0)
    mirror(1)
    fetch(2)
    build(1)
    products(1, True)
    reduce_first(1)
    products(0, False)
    reduce_second(0)
    products(1, False)
    reduce_second(1)
    mirror(2)
    gather_first(0)
    fetch(3)
    gather_first(1)
    build(2)
    products(2, True)
    gather_second(0)
    products(2, False)
    mirror(3)
    gather_second(1)
    build(3)
    products(3, True)
    reduce_first(2, (work[0]["delta_came"], work[0]["active_came"]))
    products(3, False)
    join(0)
    reduce_first(3, (work[1]["delta_came"], work[1]["active_came"]))
    join(1)
    up_partial = early_grads(("in", "delta"))
    reduce_second(2)
    share(0)
    reduce_second(3)
    share_sum(0)
    share(1)
    gather_first(2)
    share_sum(1)
    gather_first(3)
    gather_second(2)
    gather_second(3)
    down_partial = early_grads(("active", "cot"))
    join(2)
    share(2)
    share_sum(2)
    join(3)
    share(3)
    up_grad = late_grads(("in", "delta"), up_partial)
    share_sum(3)
    down_grad = late_grads(("active", "cot"), down_partial)

    if group == 1:
        two = pass_row(step_part(1)) + step_part(2)
        two = lax.ppermute(two, "row", [(i, (i + 2) % n_row) for i in range(n_row)])
        input_grad = step_part(0) + two + pass_row(step_part(3).astype(b16)).astype(f32)
    else:
        running = pass_row(step_part(1))
        for step in range(2, n_row):
            running = pass_row(running + step_part(step))
        input_grad = step_part(0) + running
    input_grad = input_grad.astype(b16).reshape(2, 2, quarter, width).transpose(1, 0, 2, 3).reshape(rows, width)
    return (reorder(input_grad, y_outer), up_grad, down_grad)


def solution(mesh):
    tokens = P(("dp", "row"), "col")
    up, down = P("col", ("dp", "row")), P(("dp", "row"), "col")
    return jax.shard_map(
        shards,
        mesh=mesh,
        in_specs=(tokens, up, down, tokens),
        out_specs=(tokens, up, down),
        check_vma=False,
    )
```

```python
import math

import jax
import jax.numpy as jnp
from jax import lax
from jax.experimental import pallas as pl
from jax.experimental.pallas import tpu as pltpu
from jax.sharding import PartitionSpec as P

gelu_const = math.sqrt(2.0 / math.pi)
f32, b16 = jnp.float32, jnp.bfloat16


def gelu_both(value):
    square = value * value
    tangent = jnp.tanh(gelu_const * (value + 0.044715 * square * value))
    half = 0.5 * (1.0 + tangent)
    slope = half + 0.5 * value * (1.0 - tangent * tangent) * gelu_const * (1.0 + 3.0 * 0.044715 * square)
    return value * half, slope


def contract(left, right, at_left, at_right):
    return lax.dot_general(
        left, right, (((at_left,), (at_right,)), ((), ())), preferred_element_type=f32
    )


def call(body, operands, in_specs, outs, out_specs, grid, name, limit=16 * 2**20):
    return pl.pallas_call(
        body,
        grid=grid,
        in_specs=in_specs,
        out_specs=out_specs,
        out_shape=outs,
        compiler_params=pltpu.CompilerParams(vmem_limit_bytes=limit),
        cost_estimate=pl.CostEstimate(flops=1000, bytes_accessed=1000, transcendentals=0),
        name=name,
    )(*operands)


def shape(dims, dtype):
    return jax.ShapeDtypeStruct(dims, dtype)


def tile_of(size, most):
    return max(t for t in range(128, most + 1, 128) if size % t == 0)


whole = pl.BlockSpec(memory_space=pltpu.VMEM)


def first_product(chunk, weight, weight_dim, name):
    tokens = chunk.shape[0]
    hidden = weight.shape[1 - weight_dim]
    half = tokens // 2
    tile = tile_of(hidden, 512)

    def body(chunk_ref, weight_ref, sent_ref, kept_ref):
        for start in range(0, hidden, tile):
            span = pl.ds(start, tile)
            block = weight_ref[:, span] if weight_dim == 0 else weight_ref[span, :]
            total = contract(chunk_ref[...], block, 1, weight_dim)
            kept_ref[:, span] = total[:half]
            sent_ref[:, span] = total[half:].astype(b16)

    return call(
        body, [chunk, weight], [whole] * 2, [shape((half, hidden), b16), shape((half, hidden), f32)], [whole] * 2, (), name
    )


def add_halves(kept_h, came_h, kept_g, came_g):
    tokens, hidden = kept_h.shape
    half = tokens // 2
    tile = tile_of(hidden, 768)

    def body(kh, ch, kg, cg, sent_h, next_h, sent_g, next_g):
        for kept, came, sent, rest in ((kh, ch, sent_h, next_h), (kg, cg, sent_g, next_g)):
            total = kept[...] + came[...].astype(f32)
            rest[...] = total[:half]
            sent[...] = total[half:].astype(b16)

    block = pl.BlockSpec((tokens, tile), lambda i: (0, i))
    part = pl.BlockSpec((half, tile), lambda i: (0, i))
    return call(
        body,
        [kept_h, came_h, kept_g, came_g],
        [block] * 4,
        [shape((half, hidden), b16), shape((half, hidden), f32)] * 2,
        [part] * 4,
        (hidden // tile,),
        "add_halves",
    )


def activate(kept_h, came_h, kept_g, came_g):
    tokens, hidden = kept_h.shape
    tile = tile_of(hidden, 768)

    def body(kh, ch, kg, cg, active_ref, delta_ref):
        value, slope = gelu_both(kh[...] + ch[...].astype(f32))
        active_ref[...] = value.astype(b16)
        delta_ref[...] = ((kg[...] + cg[...].astype(f32)) * slope).astype(b16)

    block = pl.BlockSpec((tokens, tile), lambda i: (0, i))
    return call(
        body, [kept_h, came_h, kept_g, came_g], [block] * 4, [shape((tokens, hidden), b16)] * 2, [block] * 2,
        (hidden // tile,), "activate",
    )


def join_pairs(*arrays):
    rows, columns = arrays[0].shape
    tile = tile_of(columns, 1536)

    def body(*refs):
        for i, out in enumerate(refs[len(arrays):]):
            out[pl.ds(0, rows), :] = refs[2 * i][...]
            out[pl.ds(rows, rows), :] = refs[2 * i + 1][...]

    return call(
        body,
        arrays,
        [pl.BlockSpec((rows, tile), lambda i: (0, i))] * len(arrays),
        [shape((2 * rows, columns), arrays[0].dtype)] * (len(arrays) // 2),
        [pl.BlockSpec((2 * rows, tile), lambda i: (0, i))] * (len(arrays) // 2),
        (columns // tile,),
        "join_pairs",
    )


def input_product(delta, up_weight, core, quarter):
    tokens = delta.shape[0]
    width = up_weight.shape[0]
    tile = tile_of(width, 512)
    half = tokens // 2
    pairs = range(tokens // (2 * quarter))

    def body(*refs):
        delta_ref, weight_ref = refs[:2]
        for start in range(0, width, tile):
            span = pl.ds(start, tile)
            total = contract(delta_ref[...], weight_ref[span, :], 1, 1)
            for i in pairs:
                for other in range(2):
                    rows = total[(2 * i + other) * quarter : (2 * i + other + 1) * quarter]
                    if core is None:
                        refs[2 + other][pl.ds(i * quarter, quarter), span] = rows
                    else:
                        base = pl.multiple_of((refs[2][0] ^ other) * half, half)
                        refs[3][pl.ds(base + i * quarter, quarter), span] = rows

    if core is None:
        return call(body, [delta, up_weight], [whole] * 2, [shape((half, width), f32)] * 2, [whole] * 2, (), "input_product")
    return call(
        body,
        [delta, up_weight, core],
        [whole] * 2 + [pl.BlockSpec(memory_space=pltpu.SMEM)],
        shape((tokens, width), f32),
        whole,
        (),
        "input_product",
    )


def weight_product(lefts, rights, partial, scale, most, name):
    tokens, rows = lefts[0].shape
    columns = rights[0].shape[1]
    tile = tile_of(rows, most)
    count = len(lefts)

    def body(*refs):
        total = contract(refs[0][...], refs[count][...], 0, 0)
        for i in range(1, count):
            total = total + contract(refs[i][...], refs[count + i][...], 0, 0)
        if partial is not None:
            total = total + refs[2 * count][...]
        refs[-1][...] = (total if scale is None else total * scale).astype(refs[-1].dtype)

    block = pl.BlockSpec((tile, columns), lambda i: (i, 0))
    return call(
        body,
        [*lefts, *rights] + ([] if partial is None else [partial]),
        [pl.BlockSpec((tokens, tile), lambda i: (0, i))] * count
        + [pl.BlockSpec((tokens, columns), lambda i: (0, 0))] * count
        + [block] * (partial is not None),
        shape((rows, columns), f32 if scale is None else b16),
        block,
        (rows // tile,),
        name,
        32 * 2**20,
    )


def shards(inputs, up_weight, down_weight, cotangent):
    n_row = lax.axis_size("row")
    replicas = lax.axis_size("dp")
    n_col = lax.axis_size("col")
    assert replicas == 2 and n_col == 4 and n_row % 4 == 0
    rows, width = inputs.shape
    quarter = rows // n_col
    own = lax.axis_index("col")

    def swap_x(a):
        return lax.ppermute(a, "col", [(i, i ^ 1) for i in range(n_col)])

    def swap_y(a):
        return lax.ppermute(a, "col", [(i, i ^ 2) for i in range(n_col)])

    def swap_dp(a):
        return lax.ppermute(a, "dp", [(0, 1), (1, 0)])

    def pass_row(a):
        return lax.ppermute(a, "row", [(i, (i + 1) % n_row) for i in range(n_row)])

    def reorder(a, order):
        blocks = [lax.dynamic_slice_in_dim(a, (own ^ bits) * quarter, quarter, 0) for bits in order]
        return jnp.concatenate(blocks, axis=0)

    x_outer, y_outer = (0, 2, 1, 3), (0, 1, 2, 3)

    def reorder_both():
        def body(own_ref, inputs_ref, cotangent_ref, out_ref):
            for i in range(n_col):
                for ref, order, base in ((inputs_ref, x_outer, 0), (cotangent_ref, y_outer, rows)):
                    source = pl.multiple_of((own_ref[0] ^ order[i]) * quarter, quarter)
                    out_ref[pl.ds(base + i * quarter, quarter), :] = ref[pl.ds(source, quarter), :]

        return pl.pallas_call(
            body,
            in_specs=[pl.BlockSpec(memory_space=pltpu.SMEM), whole, whole],
            out_specs=whole,
            out_shape=jax.ShapeDtypeStruct((2 * rows, width), b16),
            name="reorder",
        )(own.astype(jnp.int32).reshape(1), inputs, cotangent)

    if quarter % 16 == 0:
        moving = reorder_both()
    else:
        moving = jnp.concatenate([reorder(inputs, x_outer), reorder(cotangent, y_outer)], axis=0)

    group = n_row // 4
    tall = group * rows
    work = [{} for _ in range(4)]
    blocks = {0: [moving]}
    aligned = group == 1 and quarter % 16 == 0

    token = ()

    def after(*values):
        tied = lax.optimization_barrier((*values, *token))[: len(values)]
        return tied if len(values) > 1 else tied[0]

    def fetch(at):
        if at > 0:
            blocks[at] = [pass_row(after(blocks[at - 1][-1]))]
        while len(blocks[at]) < group:
            blocks[at].append(pass_row(blocks[at][-1]))

    def mirror(at):
        w = work[at]
        w["mine"] = blocks[at][0] if group == 1 else jnp.concatenate(blocks[at])
        mine = after(w["mine"])
        if at == 1:
            w["other"] = [swap_dp(part) for part in jnp.split(mine, 2)]
        elif at == 0:
            w["other"] = [swap_dp(mine)]
        else:
            pair = lax.all_gather(mine, "dp")
            w["other"] = [lax.dynamic_index_in_dim(pair, 1 - lax.axis_index("dp"), 0, keepdims=False)]

    def arrived(at):
        nonlocal token
        blocks[at][-1] = after(blocks[at][-1])
        token = (*token, blocks[at][-1])

    def build_kernel(mine, *others):
        def body(mine_ref, *refs):
            for part, out in enumerate(refs[-2:]):
                for i in range(n_col):
                    span = pl.ds(part * rows + i * quarter, quarter)
                    out[pl.ds(2 * i * quarter, quarter), :] = mine_ref[span, :]
                    if len(refs) == 3:
                        out[pl.ds((2 * i + 1) * quarter, quarter), :] = refs[0][span, :]
                    else:
                        out[pl.ds((2 * i + 1) * quarter, quarter), :] = refs[part][pl.ds(i * quarter, quarter), :]

        return call(
            body, [mine, *others], [whole] * (1 + len(others)), [shape((2 * rows, width), b16)] * 2, [whole] * 2, (), "build"
        )

    def build(at):
        nonlocal token
        w = work[at]
        mine, *others = after(w["mine"], *w["other"])
        if aligned:
            w["in"], w["cot"] = build_kernel(mine, *others)
        else:
            other = jnp.concatenate(others)
            pair = [a.reshape(group, 2 * n_col, quarter, width).transpose(1, 0, 2, 3) for a in (mine, other)]
            w["in"], w["cot"] = jnp.stack(pair, axis=2).reshape(2, 2 * tall, width)
        token = (w["in"], w["cot"])

    def products(at):
        nonlocal token
        w = work[at]
        w["h_out"], w["h"] = token = first_product(after(w["in"]), up_weight, 0, "hidden_product")
        w["g_out"], w["g"] = token = first_product(after(w["cot"]), down_weight, 1, "delta_act_product")

    def reduce_first(at):
        w = work[at]
        if at < 2:
            w["h_came"], w["g_came"] = swap_x(w["h_out"]), swap_y(w["g_out"])
        else:
            h_out, g_out = after(w["h_out"], w["g_out"])
            w["h_came"], w["g_came"] = swap_x(h_out), swap_y(g_out)

    def reduce_second(at):
        nonlocal token
        w = work[at]
        sent_h, w["h"], sent_g, w["g"] = token = add_halves(*after(w["h"], w["h_came"], w["g"], w["g_came"]))
        w["h_came"], w["g_came"] = swap_y(sent_h), swap_x(sent_g)

    def gather_first(at):
        nonlocal token
        w = work[at]
        w["active"], w["delta"] = token = activate(*after(w["h"], w["h_came"], w["g"], w["g_came"]))
        w["delta_came"], w["active_came"] = swap_y(w["delta"]), swap_x(w["active"])

    def join(at):
        nonlocal token
        w = work[at]
        w["delta"], w["active"] = token = join_pairs(
            *after(w["delta"], w["delta_came"], w["active"], w["active_came"])
        )

    def gather_second(at):
        w = work[at]
        join(at)
        w["delta_came"], w["active_came"] = swap_x(w["delta"]), swap_y(w["active"])

    def add_kernel(dtype, *arrays):
        height = arrays[0].shape[0]
        step = tile_of(height, 128) if height % 128 == 0 else height

        def body(*refs):
            total = refs[0][...]
            for ref in refs[1:-1]:
                total = total + ref[...]
            refs[-1][...] = total.astype(dtype)

        block = pl.BlockSpec((step, tile_of(width, 768)), lambda i, j: (i, j))
        grid = (height // step, width // tile_of(width, 768))
        return call(body, arrays, [block] * len(arrays), shape((height, width), dtype), block, grid, "add")

    def share(at):
        nonlocal token
        w = work[at]
        delta = after(w["delta"])
        if not aligned:
            parts = contract(delta, up_weight, 1, 1).reshape(n_col, group, 2, quarter, width)
            token = (parts,)
            w["part"], w["part_came"] = parts[:, :, 0], swap_dp(parts[:, :, 1])
        elif at < 2:
            parts = input_product(delta, up_weight, lax.axis_index("dp").astype(jnp.int32).reshape(1), quarter)
            token = (parts,)
            w["both"] = lax.psum_scatter(parts, "dp", scatter_dimension=0, tiled=True)
        else:
            w["part"], sent = token = input_product(delta, up_weight, None, quarter)
            w["part_came"] = swap_dp(sent)

    running = None

    def share_sum(at):
        nonlocal token, running
        w = work[at]
        if not aligned:
            part = w["part"] + w["part_came"]
            for step in range(at * group, (at + 1) * group):
                one = part[:, step - at * group].reshape(rows, width)
                if step == 0:
                    w["part"] = one
                else:
                    running = pass_row(one if running is None else running + one)
        elif at < 2:
            w["part"] = w["both"]
            if at == 1:
                running = pass_row(after(w["both"]))
        else:
            total = add_kernel(b16 if at == 3 else f32, *after(w["part"], w["part_came"], running))
            token = (total,)
            running = pass_row(total)

    def grads(chunks, names, partial, most, name):
        nonlocal token
        values = after(*(work[at][k] for k in names for at in chunks))
        count = len(chunks)
        scale = None if partial is None else 1.0 / replicas
        token = (weight_product(values[:count], values[count:], partial, scale, most, name),)
        return token[0]

    fetch(0)
    mirror(0)
    fetch(1)
    build(0)
    products(0)
    reduce_first(0)
    mirror(1)
    fetch(2)
    build(1)
    products(1)
    reduce_first(1)
    reduce_second(0)
    arrived(2)
    reduce_second(1)
    fetch(3)
    mirror(2)
    gather_first(0)
    gather_first(1)
    build(2)
    products(2)
    arrived(3)
    gather_second(0)
    mirror(3)
    gather_second(1)
    build(3)
    products(3)
    join(0)
    reduce_first(2)
    share(0)
    join(1)
    reduce_first(3)
    share(1)
    up_partial = grads((0, 1), ("in", "delta"), None, 256, "up_grad_early")
    reduce_second(2)
    reduce_second(3)
    share_sum(0)
    gather_first(2)
    gather_first(3)
    share_sum(1)
    gather_second(2)
    gather_second(3)
    down_partial = grads((0, 1), ("active", "cot"), None, 512, "down_grad_early")
    join(2)
    share(2)
    join(3)
    share_sum(2)
    share(3)
    up_grad = grads((2, 3), ("in", "delta"), up_partial, 256, "up_grad")
    share_sum(3)
    down_grad = grads((2, 3), ("active", "cot"), down_partial, 512, "down_grad")

    def end_kernel(part, came):
        tile = tile_of(width, 768)

        def body(own_ref, part_ref, came_ref, out_ref):
            total = (part_ref[...] + came_ref[...].astype(f32)).astype(b16)
            for i in range(n_col):
                target = pl.multiple_of((own_ref[0] ^ x_outer[i]) * quarter, quarter)
                out_ref[pl.ds(target, quarter), :] = total[i * quarter : (i + 1) * quarter]

        block = pl.BlockSpec((rows, tile), lambda i: (0, i))
        return call(
            body,
            [own.astype(jnp.int32).reshape(1), part, came],
            [pl.BlockSpec(memory_space=pltpu.SMEM), block, block],
            shape((rows, width), b16),
            block,
            (width // tile,),
            "end",
        )

    if aligned:
        return (end_kernel(work[0]["part"], running), up_grad, down_grad)
    input_grad = work[0]["part"] + running.astype(f32)
    input_grad = input_grad.astype(b16).reshape(2, 2, quarter, width).transpose(1, 0, 2, 3).reshape(rows, width)
    return (reorder(input_grad, y_outer), up_grad, down_grad)


def solution(mesh):
    tokens = P(("dp", "row"), "col")
    up, down = P("col", ("dp", "row")), P(("dp", "row"), "col")
    return jax.shard_map(
        shards,
        mesh=mesh,
        in_specs=(tokens, up, down, tokens),
        out_specs=(tokens, up, down),
        check_vma=False,
    )
```

```python
import math

import jax
import jax.numpy as jnp
from jax import lax
from jax.experimental import pallas as pl
from jax.experimental.pallas import tpu as pltpu
from jax.sharding import PartitionSpec as P

gelu_const = math.sqrt(2.0 / math.pi)
f32, b16 = jnp.float32, jnp.bfloat16


def gelu_both(value):
    square = value * value
    tangent = jnp.tanh(gelu_const * (value + 0.044715 * square * value))
    half = 0.5 * (1.0 + tangent)
    slope = half + 0.5 * value * (1.0 - tangent * tangent) * gelu_const * (1.0 + 3.0 * 0.044715 * square)
    return value * half, slope


def contract(left, right, at_left, at_right):
    return lax.dot_general(
        left, right, (((at_left,), (at_right,)), ((), ())), preferred_element_type=f32
    )


def call(body, operands, in_specs, outs, out_specs, grid, name, limit=8 * 2**20):
    return pl.pallas_call(
        body,
        grid=grid,
        in_specs=in_specs,
        out_specs=out_specs,
        out_shape=outs,
        compiler_params=pltpu.CompilerParams(vmem_limit_bytes=limit),
        cost_estimate=pl.CostEstimate(flops=1000, bytes_accessed=1000, transcendentals=0),
        name=name,
    )(*operands)


def shape(dims, dtype):
    return jax.ShapeDtypeStruct(dims, dtype)


def tile_of(size, most):
    return max(t for t in range(128, most + 1, 128) if size % t == 0)


whole = pl.BlockSpec(memory_space=pltpu.VMEM)


def first_product(chunk, weight, weight_dim, name):
    tokens = chunk.shape[0]
    hidden = weight.shape[1 - weight_dim]
    half = tokens // 2
    tile = tile_of(hidden, 512)

    def body(chunk_ref, weight_ref, sent_ref, kept_ref):
        for start in range(0, hidden, tile):
            span = pl.ds(start, tile)
            block = weight_ref[:, span] if weight_dim == 0 else weight_ref[span, :]
            total = contract(chunk_ref[...], block, 1, weight_dim)
            kept_ref[:, span] = total[:half]
            sent_ref[:, span] = total[half:].astype(b16)

    return call(
        body, [chunk, weight], [whole] * 2, [shape((half, hidden), b16), shape((half, hidden), f32)], [whole] * 2, (), name
    )


def add_halves(kept_h, came_h, kept_g, came_g):
    tokens, hidden = kept_h.shape
    half = tokens // 2
    tile = tile_of(hidden, 768)

    def body(kh, ch, kg, cg, sent_h, next_h, sent_g, next_g):
        for kept, came, sent, rest in ((kh, ch, sent_h, next_h), (kg, cg, sent_g, next_g)):
            total = kept[...] + came[...].astype(f32)
            rest[...] = total[:half]
            sent[...] = total[half:].astype(b16)

    block = pl.BlockSpec((tokens, tile), lambda i: (0, i))
    part = pl.BlockSpec((half, tile), lambda i: (0, i))
    return call(
        body,
        [kept_h, came_h, kept_g, came_g],
        [block] * 4,
        [shape((half, hidden), b16), shape((half, hidden), f32)] * 2,
        [part] * 4,
        (hidden // tile,),
        "add_halves",
    )


def activate(kept_h, came_h, kept_g, came_g):
    tokens, hidden = kept_h.shape
    tile = tile_of(hidden, 768)

    def body(kh, ch, kg, cg, active_ref, delta_ref):
        value, slope = gelu_both(kh[...] + ch[...].astype(f32))
        active_ref[...] = value.astype(b16)
        delta_ref[...] = ((kg[...] + cg[...].astype(f32)) * slope).astype(b16)

    block = pl.BlockSpec((tokens, tile), lambda i: (0, i))
    return call(
        body, [kept_h, came_h, kept_g, came_g], [block] * 4, [shape((tokens, hidden), b16)] * 2, [block] * 2,
        (hidden // tile,), "activate",
    )


def join_pairs(*arrays):
    rows, columns = arrays[0].shape
    tile = tile_of(columns, 1536)

    def body(*refs):
        for i, out in enumerate(refs[len(arrays):]):
            out[pl.ds(0, rows), :] = refs[2 * i][...]
            out[pl.ds(rows, rows), :] = refs[2 * i + 1][...]

    return call(
        body,
        arrays,
        [pl.BlockSpec((rows, tile), lambda i: (0, i))] * len(arrays),
        [shape((2 * rows, columns), arrays[0].dtype)] * (len(arrays) // 2),
        [pl.BlockSpec((2 * rows, tile), lambda i: (0, i))] * (len(arrays) // 2),
        (columns // tile,),
        "join_pairs",
    )


def input_product(delta, up_weight, quarter):
    tokens = delta.shape[0]
    width = up_weight.shape[0]
    tile = tile_of(width, 512)

    def body(delta_ref, weight_ref, *outs):
        for start in range(0, width, tile):
            span = pl.ds(start, tile)
            total = contract(delta_ref[...], weight_ref[span, :], 1, 1)
            for i in range(tokens // quarter):
                outs[i % 2][pl.ds(i // 2 * quarter, quarter), span] = total[i * quarter : (i + 1) * quarter]

    outs = [shape((tokens // 2, width), f32)] * 2
    return call(body, [delta, up_weight], [whole] * 2, outs, [whole] * 2, (), "input_product")


def weight_product(lefts, rights, partial, scale, most, held, name):
    tokens, rows = lefts[0].shape
    columns = rights[0].shape[1]
    tile = tile_of(rows, most)
    count = len(lefts)

    def body(*refs):
        mine = pl.ds(pl.multiple_of(pl.program_id(0) * tile, tile), tile)
        total = contract(refs[0][...], refs[count][...], 0, 0)
        for i in range(1, count):
            total = total + contract(refs[i][...], refs[count + i][...], 0, 0)
        if partial is not None:
            total = total + (refs[2 * count][mine, :] if held else refs[2 * count][...])
        if scale is not None:
            refs[-1][...] = (total * scale).astype(b16)
        elif held:
            refs[-1][mine, :] = total
        else:
            refs[-1][...] = total

    block = pl.BlockSpec((tile, columns), lambda i: (i, 0))
    return call(
        body,
        [*lefts, *rights] + ([] if partial is None else [partial]),
        [pl.BlockSpec((tokens, tile), lambda i: (0, i))] * count
        + [pl.BlockSpec((tokens, columns), lambda i: (0, 0))] * count
        + [whole if held else block] * (partial is not None),
        shape((rows, columns), f32) if held and scale is None else pltpu.HBM((rows, columns), f32 if scale is None else b16),
        whole if held and scale is None else block,
        (rows // tile,),
        name,
        14 * 2**20,
    )


def shards(inputs, up_weight, down_weight, cotangent):
    n_row = lax.axis_size("row")
    replicas = lax.axis_size("dp")
    n_col = lax.axis_size("col")
    assert replicas == 2 and n_col == 4 and n_row % 4 == 0
    rows, width = inputs.shape
    quarter = rows // n_col
    own = lax.axis_index("col")

    def swap_x(a):
        return lax.ppermute(a, "col", [(i, i ^ 1) for i in range(n_col)])

    def swap_y(a):
        return lax.ppermute(a, "col", [(i, i ^ 2) for i in range(n_col)])

    def swap_dp(a):
        return lax.ppermute(a, "dp", [(0, 1), (1, 0)])

    def pass_row(a):
        return lax.ppermute(a, "row", [(i, (i + 1) % n_row) for i in range(n_row)])

    def reorder(a, order):
        blocks = [lax.dynamic_slice_in_dim(a, (own ^ bits) * quarter, quarter, 0) for bits in order]
        return jnp.concatenate(blocks, axis=0)

    x_outer, y_outer = (0, 2, 1, 3), (0, 1, 2, 3)

    def reorder_both():
        def body(own_ref, inputs_ref, cotangent_ref, out_ref):
            for i in range(n_col):
                for ref, order, base in ((inputs_ref, x_outer, 0), (cotangent_ref, y_outer, rows)):
                    source = pl.multiple_of((own_ref[0] ^ order[i]) * quarter, quarter)
                    out_ref[pl.ds(base + i * quarter, quarter), :] = ref[pl.ds(source, quarter), :]

        return call(
            body,
            [own.astype(jnp.int32).reshape(1), inputs, cotangent],
            [pl.BlockSpec(memory_space=pltpu.SMEM), whole, whole],
            shape((2 * rows, width), b16),
            whole,
            (),
            "reorder",
        )

    if quarter % 16 == 0:
        moving = reorder_both()
    else:
        moving = jnp.concatenate([reorder(inputs, x_outer), reorder(cotangent, y_outer)], axis=0)

    group = n_row // 4
    tall = group * rows
    work = [{} for _ in range(4)]
    blocks = {0: [moving]}
    aligned = group == 1 and quarter % 16 == 0

    token = ()

    def after(*values):
        tied = lax.optimization_barrier((*values, *token))[: len(values)]
        return tied if len(values) > 1 else tied[0]

    def fetch(at):
        if at > 0:
            sent = blocks[at - 1][-1]
            if at > 2:
                sent = lax.optimization_barrier((sent, *work[at - 1]["other"]))[0]
            blocks[at] = [pass_row(sent)]
        while len(blocks[at]) < group:
            blocks[at].append(pass_row(blocks[at][-1]))

    def mirror(at):
        w = work[at]
        if at > 0:
            blocks[at][-1] = after(blocks[at][-1])
        w["mine"] = blocks[at][0] if group == 1 else jnp.concatenate(blocks[at])
        w["other"] = [swap_dp(part) for part in (jnp.split(w["mine"], 2) if at > 0 else [w["mine"]])]

    def arrived(at):
        nonlocal token
        token = (*token, blocks[at][-1])

    def build_kernel(mine, *others):
        def body(mine_ref, *refs):
            for part, out in enumerate(refs[-2:]):
                for i in range(n_col):
                    span = pl.ds(part * rows + i * quarter, quarter)
                    out[pl.ds(2 * i * quarter, quarter), :] = mine_ref[span, :]
                    if len(refs) == 3:
                        out[pl.ds((2 * i + 1) * quarter, quarter), :] = refs[0][span, :]
                    else:
                        out[pl.ds((2 * i + 1) * quarter, quarter), :] = refs[part][pl.ds(i * quarter, quarter), :]

        return call(
            body, [mine, *others], [whole] * (1 + len(others)), [shape((2 * rows, width), b16)] * 2, [whole] * 2, (), "build"
        )

    def build(at):
        nonlocal token
        w = work[at]
        mine, *others = after(w["mine"], *w["other"])
        if aligned:
            w["in"], w["cot"] = build_kernel(mine, *others)
        else:
            other = jnp.concatenate(others)
            pair = [a.reshape(group, 2 * n_col, quarter, width).transpose(1, 0, 2, 3) for a in (mine, other)]
            w["in"], w["cot"] = jnp.stack(pair, axis=2).reshape(2, 2 * tall, width)
        token = (w["in"], w["cot"])

    def products(at):
        nonlocal token
        w = work[at]
        w["h_out"], w["h"] = token = first_product(after(w["in"]), up_weight, 0, "hidden_product")
        w["g_out"], w["g"] = token = first_product(after(w["cot"]), down_weight, 1, "delta_act_product")

    def reduce_first(at):
        w = work[at]
        if at < 2:
            w["h_came"], w["g_came"] = swap_x(w["h_out"]), swap_y(w["g_out"])
        else:
            h_out, g_out = after(w["h_out"], w["g_out"])
            w["h_came"], w["g_came"] = swap_x(h_out), swap_y(g_out)

    def reduce_second(at):
        nonlocal token
        w = work[at]
        sent_h, w["h"], sent_g, w["g"] = token = add_halves(*after(w["h"], w["h_came"], w["g"], w["g_came"]))
        w["h_came"], w["g_came"] = swap_y(sent_h), swap_x(sent_g)

    def gather_first(at):
        nonlocal token
        w = work[at]
        w["active"], w["delta"] = token = activate(*after(w["h"], w["h_came"], w["g"], w["g_came"]))
        w["delta_came"], w["active_came"] = swap_y(w["delta"]), swap_x(w["active"])

    def join(at):
        nonlocal token
        w = work[at]
        w["delta"], w["active"] = token = join_pairs(
            *after(w["delta"], w["delta_came"], w["active"], w["active_came"])
        )

    def gather_second(at):
        w = work[at]
        join(at)
        w["delta_came"], w["active_came"] = swap_x(w["delta"]), swap_y(w["active"])

    def add_kernel(dtype, *arrays):
        height = arrays[0].shape[0]
        step = tile_of(height, 128) if height % 128 == 0 else height

        def body(*refs):
            total = refs[0][...]
            for ref in refs[1:-1]:
                total = total + ref[...]
            refs[-1][...] = total.astype(dtype)

        block = pl.BlockSpec((step, tile_of(width, 768)), lambda i, j: (i, j))
        grid = (height // step, width // tile_of(width, 768))
        return call(body, arrays, [block] * len(arrays), shape((height, width), dtype), block, grid, "add")

    def share(at):
        nonlocal token
        w = work[at]
        delta = after(w["delta"])
        if not aligned:
            parts = contract(delta, up_weight, 1, 1).reshape(n_col, group, 2, quarter, width)
            token = (parts,)
            w["part"], w["part_came"] = parts[:, :, 0], swap_dp(parts[:, :, 1])
        else:
            w["part"], sent = token = input_product(delta, up_weight, quarter)
            w["part_came"] = swap_dp(sent)

    running = None

    def share_sum(at):
        nonlocal token, running
        w = work[at]
        if not aligned:
            part = w["part"] + w["part_came"]
            for step in range(at * group, (at + 1) * group):
                one = part[:, step - at * group].reshape(rows, width)
                if step == 0:
                    w["part"] = one
                else:
                    running = pass_row(one if running is None else running + one)
        elif at == 1:
            running = pass_row(add_kernel(f32, w["part"], w["part_came"]))
        else:
            total = add_kernel(b16 if at == 3 else f32, *after(w["part"], w["part_came"], running))
            token = (total,)
            running = pass_row(total)

    def settle():
        nonlocal token
        token = (*token, running)

    def grads(chunks, names, partial, most, held, name):
        nonlocal token
        values = after(*(work[at][k] for k in names for at in chunks))
        count = len(chunks)
        scale = None if partial is None else 1.0 / replicas
        token = (weight_product(values[:count], values[count:], partial, scale, most, held, name),)
        return token[0]

    fetch(0)
    mirror(0)
    fetch(1)
    build(0)
    products(0)
    reduce_first(0)
    mirror(1)
    build(1)
    products(1)
    reduce_first(1)
    reduce_second(0)
    fetch(2)
    reduce_second(1)
    gather_first(0)
    gather_first(1)
    arrived(2)
    mirror(2)
    gather_second(0)
    build(2)
    products(2)
    fetch(3)
    gather_second(1)
    join(0)
    reduce_first(2)
    arrived(3)
    mirror(3)
    build(3)
    products(3)
    share(0)
    if not aligned:
        share_sum(0)
    join(1)
    reduce_first(3)
    share(1)
    share_sum(1)
    up_partial = grads((0, 1), ("in", "delta"), None, 256, True, "up_grad_early")
    reduce_second(2)
    reduce_second(3)
    gather_first(2)
    gather_first(3)
    gather_second(2)
    settle()
    gather_second(3)
    down_partial = grads((0, 1), ("active", "cot"), None, 512, False, "down_grad_early")
    join(2)
    share(2)
    join(3)
    share_sum(2)
    share(3)
    up_grad = grads((2, 3), ("in", "delta"), up_partial, 256, True, "up_grad")
    share_sum(3)
    down_grad = grads((2, 3), ("active", "cot"), down_partial, 512, False, "down_grad")

    def end_kernel(*arrays):
        tile = tile_of(width, 768)

        def body(own_ref, *refs):
            total = refs[0][...]
            for ref in refs[1:-1]:
                total = total + ref[...].astype(f32)
            total = total.astype(b16)
            for i in range(n_col):
                target = pl.multiple_of((own_ref[0] ^ x_outer[i]) * quarter, quarter)
                refs[-1][pl.ds(target, quarter), :] = total[i * quarter : (i + 1) * quarter]

        block = pl.BlockSpec((rows, tile), lambda i: (0, i))
        return call(
            body,
            [own.astype(jnp.int32).reshape(1), *arrays],
            [pl.BlockSpec(memory_space=pltpu.SMEM)] + [block] * len(arrays),
            shape((rows, width), b16),
            block,
            (width // tile,),
            "end",
        )

    if aligned:
        return (end_kernel(work[0]["part"], work[0]["part_came"], running), up_grad, down_grad)
    input_grad = work[0]["part"] + running.astype(f32)
    input_grad = input_grad.astype(b16).reshape(2, 2, quarter, width).transpose(1, 0, 2, 3).reshape(rows, width)
    return (reorder(input_grad, y_outer), up_grad, down_grad)


def solution(mesh):
    tokens = P(("dp", "row"), "col")
    up, down = P("col", ("dp", "row")), P(("dp", "row"), "col")
    return jax.shard_map(
        shards,
        mesh=mesh,
        in_specs=(tokens, up, down, tokens),
        out_specs=(tokens, up, down),
        check_vma=False,
    )
```

```python
import math

import jax
import jax.numpy as jnp
from jax import lax
from jax.experimental import pallas as pl
from jax.experimental.pallas import tpu as pltpu
from jax.sharding import PartitionSpec as P

gelu_const = math.sqrt(2.0 / math.pi)
f32, b16 = jnp.float32, jnp.bfloat16
FIRST_SUM, SECOND_JOIN = 5_000_000_000, 12_000_000_000


def gelu_both(value):
    square = value * value
    tangent = jnp.tanh(gelu_const * (value + 0.044715 * square * value))
    half = 0.5 * (1.0 + tangent)
    slope = half + 0.5 * value * (1.0 - tangent * tangent) * gelu_const * (1.0 + 3.0 * 0.044715 * square)
    return value * half, slope


def contract(left, right, at_left, at_right):
    return lax.dot_general(
        left, right, (((at_left,), (at_right,)), ((), ())), preferred_element_type=f32
    )


def call(body, operands, in_specs, outs, out_specs, grid, name, limit=8 * 2**20, flops=1000):
    return pl.pallas_call(
        body,
        grid=grid,
        in_specs=in_specs,
        out_specs=out_specs,
        out_shape=outs,
        compiler_params=pltpu.CompilerParams(vmem_limit_bytes=limit),
        cost_estimate=pl.CostEstimate(flops=flops, bytes_accessed=1000, transcendentals=0),
        name=name,
    )(*operands)


def shape(dims, dtype):
    return jax.ShapeDtypeStruct(dims, dtype)


def tile_of(size, most):
    return max(t for t in range(128, most + 1, 128) if size % t == 0)


whole = pl.BlockSpec(memory_space=pltpu.VMEM)


def first_product(chunk, weight, weight_dim, name):
    tokens = chunk.shape[0]
    hidden = weight.shape[1 - weight_dim]
    half = tokens // 2
    tile = tile_of(hidden, 512)

    def body(chunk_ref, weight_ref, sent_ref, kept_ref):
        for start in range(0, hidden, tile):
            span = pl.ds(start, tile)
            block = weight_ref[:, span] if weight_dim == 0 else weight_ref[span, :]
            total = contract(chunk_ref[...], block, 1, weight_dim)
            kept_ref[:, span] = total[:half]
            sent_ref[:, span] = total[half:].astype(b16)

    return call(
        body, [chunk, weight], [whole] * 2, [shape((half, hidden), b16), shape((half, hidden), f32)], [whole] * 2, (), name
    )


def add_halves(kept_h, came_h, kept_g, came_g, flops):
    tokens, hidden = kept_h.shape
    half = tokens // 2
    tile = tile_of(hidden, 768)

    def body(kh, ch, kg, cg, sent_h, next_h, sent_g, next_g):
        for kept, came, sent, rest in ((kh, ch, sent_h, next_h), (kg, cg, sent_g, next_g)):
            total = kept[...] + came[...].astype(f32)
            rest[...] = total[:half]
            sent[...] = total[half:].astype(b16)

    block = pl.BlockSpec((tokens, tile), lambda i: (0, i))
    part = pl.BlockSpec((half, tile), lambda i: (0, i))
    return call(
        body,
        [kept_h, came_h, kept_g, came_g],
        [block] * 4,
        [shape((half, hidden), b16), shape((half, hidden), f32)] * 2,
        [part] * 4,
        (hidden // tile,),
        "add_halves",
        flops=flops,
    )


def activate(kept_h, came_h, kept_g, came_g):
    tokens, hidden = kept_h.shape
    tile = tile_of(hidden, 768)

    def body(kh, ch, kg, cg, active_ref, delta_ref):
        value, slope = gelu_both(kh[...] + ch[...].astype(f32))
        active_ref[...] = value.astype(b16)
        delta_ref[...] = ((kg[...] + cg[...].astype(f32)) * slope).astype(b16)

    block = pl.BlockSpec((tokens, tile), lambda i: (0, i))
    return call(
        body, [kept_h, came_h, kept_g, came_g], [block] * 4, [shape((tokens, hidden), b16)] * 2, [block] * 2,
        (hidden // tile,), "activate",
    )


def join_pairs(flops, *arrays):
    rows, columns = arrays[0].shape
    tile = tile_of(columns, 1536)

    def body(*refs):
        for i, out in enumerate(refs[len(arrays):]):
            out[pl.ds(0, rows), :] = refs[2 * i][...]
            out[pl.ds(rows, rows), :] = refs[2 * i + 1][...]

    return call(
        body,
        arrays,
        [pl.BlockSpec((rows, tile), lambda i: (0, i))] * len(arrays),
        [shape((2 * rows, columns), arrays[0].dtype)] * (len(arrays) // 2),
        [pl.BlockSpec((2 * rows, tile), lambda i: (0, i))] * (len(arrays) // 2),
        (columns // tile,),
        "join_pairs",
        flops=flops,
    )


def input_product(delta, up_weight, quarter):
    tokens = delta.shape[0]
    width = up_weight.shape[0]
    tile = tile_of(width, 512)
    pairs = tokens // (2 * quarter)

    def body(delta_ref, weight_ref, kept_ref, *sent_refs):
        for start in range(0, width, tile):
            span = pl.ds(start, tile)
            total = contract(delta_ref[...], weight_ref[span, :], 1, 1)
            for i in range(pairs):
                first, second = 2 * i * quarter, (2 * i + 1) * quarter
                kept_ref[pl.ds(i * quarter, quarter), span] = total[first:second]
                sent_ref = sent_refs[2 * i // pairs]
                sent_ref[pl.ds(i % (pairs // 2) * quarter, quarter), span] = total[second : second + quarter]

    outs = [shape((tokens // 2, width), f32)] + [shape((tokens // 4, width), f32)] * 2
    return call(body, [delta, up_weight], [whole] * 2, outs, [whole] * 3, (), "input_product")


def add_shares(kept_ref, upper_ref, lower_ref, *rest):
    total = kept_ref[...] + jnp.concatenate([upper_ref[...], lower_ref[...]], axis=0)
    for ref in rest:
        total = total + ref[...].astype(f32)
    return total


def weight_product(lefts, rights, partial, scale, most, held, name, flops):
    tokens, rows = lefts[0].shape
    columns = rights[0].shape[1]
    tile = tile_of(rows, most)
    count = len(lefts)

    def body(*refs):
        mine = pl.ds(pl.multiple_of(pl.program_id(0) * tile, tile), tile)
        total = contract(refs[0][...], refs[count][...], 0, 0)
        for i in range(1, count):
            total = total + contract(refs[i][...], refs[count + i][...], 0, 0)
        if partial is not None:
            total = total + (refs[2 * count][mine, :] if held else refs[2 * count][...])
        if scale is not None:
            refs[-1][...] = (total * scale).astype(b16)
        elif held:
            refs[-1][mine, :] = total
        else:
            refs[-1][...] = total

    block = pl.BlockSpec((tile, columns), lambda i: (i, 0))
    return call(
        body,
        [*lefts, *rights] + ([] if partial is None else [partial]),
        [pl.BlockSpec((tokens, tile), lambda i: (0, i))] * count
        + [pl.BlockSpec((tokens, columns), lambda i: (0, 0))] * count
        + [whole if held else block] * (partial is not None),
        shape((rows, columns), f32) if held and scale is None else pltpu.HBM((rows, columns), f32 if scale is None else b16),
        whole if held and scale is None else block,
        (rows // tile,),
        name,
        14 * 2**20,
        flops,
    )


def shards(inputs, up_weight, down_weight, cotangent):
    n_row = lax.axis_size("row")
    replicas = lax.axis_size("dp")
    n_col = lax.axis_size("col")
    assert replicas == 2 and n_col == 4 and n_row % 4 == 0
    rows, width = inputs.shape
    quarter = rows // n_col
    own = lax.axis_index("col")

    def swap_x(a):
        return lax.ppermute(a, "col", [(i, i ^ 1) for i in range(n_col)])

    def swap_y(a):
        return lax.ppermute(a, "col", [(i, i ^ 2) for i in range(n_col)])

    def swap_dp(a):
        return lax.ppermute(a, "dp", [(0, 1), (1, 0)])

    def pass_row(a):
        return lax.ppermute(a, "row", [(i, (i + 1) % n_row) for i in range(n_row)])

    def reorder(a, order):
        blocks = [lax.dynamic_slice_in_dim(a, (own ^ bits) * quarter, quarter, 0) for bits in order]
        return jnp.concatenate(blocks, axis=0)

    x_outer, y_outer = (0, 2, 1, 3), (0, 1, 2, 3)

    def reorder_both():
        def body(own_ref, inputs_ref, cotangent_ref, out_ref):
            for i in range(n_col):
                for ref, order, base in ((inputs_ref, x_outer, 0), (cotangent_ref, y_outer, rows)):
                    source = pl.multiple_of((own_ref[0] ^ order[i]) * quarter, quarter)
                    out_ref[pl.ds(base + i * quarter, quarter), :] = ref[pl.ds(source, quarter), :]

        return call(
            body,
            [own.astype(jnp.int32).reshape(1), inputs, cotangent],
            [pl.BlockSpec(memory_space=pltpu.SMEM), whole, whole],
            shape((2 * rows, width), b16),
            whole,
            (),
            "reorder",
        )

    if quarter % 16 == 0:
        moving = reorder_both()
    else:
        moving = jnp.concatenate([reorder(inputs, x_outer), reorder(cotangent, y_outer)], axis=0)

    group = n_row // 4
    tall = group * rows
    work = [{} for _ in range(4)]
    blocks = {0: [moving]}
    aligned = group == 1 and quarter % 16 == 0

    token = ()

    def after(*values):
        tied = lax.optimization_barrier((*values, *token))[: len(values)]
        return tied if len(values) > 1 else tied[0]

    def fetch(at):
        if at > 0:
            sent = blocks[at - 1][-1]
            if at > 2:
                sent = lax.optimization_barrier((sent, *work[at - 1]["other"]))[0]
            blocks[at] = [pass_row(sent)]
        while len(blocks[at]) < group:
            blocks[at].append(pass_row(blocks[at][-1]))

    def mirror(at):
        w = work[at]
        if at > 0:
            blocks[at][-1] = after(blocks[at][-1])
        w["mine"] = blocks[at][0] if group == 1 else jnp.concatenate(blocks[at])
        w["other"] = [swap_dp(part) for part in (jnp.split(w["mine"], 2) if at > 0 else [w["mine"]])]

    def arrived(at):
        nonlocal token
        token = (*token, blocks[at][-1])

    def build_kernel(mine, *others):
        def body(mine_ref, *refs):
            for part, out in enumerate(refs[-2:]):
                for i in range(n_col):
                    span = pl.ds(part * rows + i * quarter, quarter)
                    out[pl.ds(2 * i * quarter, quarter), :] = mine_ref[span, :]
                    if len(refs) == 3:
                        out[pl.ds((2 * i + 1) * quarter, quarter), :] = refs[0][span, :]
                    else:
                        out[pl.ds((2 * i + 1) * quarter, quarter), :] = refs[part][pl.ds(i * quarter, quarter), :]

        return call(
            body, [mine, *others], [whole] * (1 + len(others)), [shape((2 * rows, width), b16)] * 2, [whole] * 2, (), "build"
        )

    def build(at):
        nonlocal token
        w = work[at]
        mine, *others = after(w["mine"], *w["other"])
        if aligned:
            w["in"], w["cot"] = build_kernel(mine, *others)
        else:
            other = jnp.concatenate(others)
            pair = [a.reshape(group, 2 * n_col, quarter, width).transpose(1, 0, 2, 3) for a in (mine, other)]
            w["in"], w["cot"] = jnp.stack(pair, axis=2).reshape(2, 2 * tall, width)
        token = (w["in"], w["cot"])

    def products(at):
        nonlocal token
        w = work[at]
        w["h_out"], w["h"] = token = first_product(after(w["in"]), up_weight, 0, "hidden_product")
        w["g_out"], w["g"] = token = first_product(after(w["cot"]), down_weight, 1, "delta_act_product")

    def reduce_first(at):
        w = work[at]
        if at < 2:
            w["h_came"], w["g_came"] = swap_x(w["h_out"]), swap_y(w["g_out"])
        else:
            h_out, g_out = after(w["h_out"], w["g_out"])
            w["h_came"], w["g_came"] = swap_x(h_out), swap_y(g_out)

    def reduce_second(at):
        nonlocal token
        w = work[at]
        sent_h, w["h"], sent_g, w["g"] = token = add_halves(
            *after(w["h"], w["h_came"], w["g"], w["g_came"]), FIRST_SUM if at == 0 else 1000
        )
        w["h_came"], w["g_came"] = swap_y(sent_h), swap_x(sent_g)

    def gather_first(at):
        nonlocal token
        w = work[at]
        w["active"], w["delta"] = token = activate(*after(w["h"], w["h_came"], w["g"], w["g_came"]))
        w["delta_came"], w["active_came"] = swap_y(w["delta"]), swap_x(w["active"])

    def join(at, flops=1000):
        nonlocal token
        w = work[at]
        w["delta"], w["active"] = token = join_pairs(
            flops, *after(w["delta"], w["delta_came"], w["active"], w["active_came"])
        )

    def gather_second(at):
        w = work[at]
        join(at, SECOND_JOIN if at == 1 else 1000)
        w["delta_came"], w["active_came"] = swap_x(w["delta"]), swap_y(w["active"])

    def add_kernel(dtype, *arrays):
        tile = tile_of(width, 768)

        def body(*refs):
            refs[-1][...] = add_shares(*refs[:-1]).astype(dtype)

        blocks_of = [pl.BlockSpec((a.shape[0], tile), lambda i: (0, i)) for a in arrays]
        return call(body, arrays, blocks_of, shape((rows, width), dtype), blocks_of[0], (width // tile,), "add")

    def share(at):
        nonlocal token
        w = work[at]
        delta = after(w["delta"])
        if not aligned:
            parts = contract(delta, up_weight, 1, 1).reshape(n_col, group, 2, quarter, width)
            token = (parts,)
            w["part"], w["part_came"] = parts[:, :, 0], swap_dp(parts[:, :, 1])
        else:
            w["part"], *sent = token = input_product(delta, up_weight, quarter)
            w["part_came"] = [swap_dp(part) for part in sent]

    running = None

    def share_sum(at):
        nonlocal token, running
        w = work[at]
        if not aligned:
            part = w["part"] + w["part_came"]
            for step in range(at * group, (at + 1) * group):
                one = part[:, step - at * group].reshape(rows, width)
                if step == 0:
                    w["part"] = one
                else:
                    running = pass_row(one if running is None else running + one)
        elif at == 1:
            running = pass_row(add_kernel(f32, w["part"], *w["part_came"]))
        else:
            total = add_kernel(b16 if at == 3 else f32, *after(w["part"], *w["part_came"], running))
            token = (total,)
            running = pass_row(total)

    def settle():
        nonlocal token
        token = (*token, running)

    def grads(chunks, names, partial, most, held, name, flops=1000):
        nonlocal token
        values = after(*(work[at][k] for k in names for at in chunks))
        count = len(chunks)
        scale = None if partial is None else 1.0 / replicas
        token = (weight_product(values[:count], values[count:], partial, scale, most, held, name, flops),)
        return token[0]

    fetch(0)
    mirror(0)
    fetch(1)
    build(0)
    products(0)
    reduce_first(0)
    mirror(1)
    build(1)
    products(1)
    reduce_first(1)
    reduce_second(0)
    fetch(2)
    reduce_second(1)
    gather_first(0)
    gather_first(1)
    arrived(2)
    mirror(2)
    gather_second(0)
    build(2)
    products(2)
    fetch(3)
    gather_second(1)
    join(0)
    reduce_first(2)
    arrived(3)
    mirror(3)
    build(3)
    products(3)
    share(0)
    if not aligned:
        share_sum(0)
    join(1)
    reduce_first(3)
    share(1)
    share_sum(1)
    up_partial = grads((0, 1), ("in", "delta"), None, 256, True, "up_grad_early")
    reduce_second(2)
    reduce_second(3)
    gather_first(2)
    gather_first(3)
    gather_second(2)
    gather_first(3)
    down_partial = grads((0, 1), ("active", "cot"), None, 512, False, "down_grad_early")
    settle()
    gather_second(3)
    join(2)
    share(2)
    share_sum(2)
    join(3)
    share(3)
    up_grad = grads((2, 3), ("in", "delta"), up_partial, 256, True, "up_grad")
    share_sum(3)
    down_grad = grads((2, 3), ("active", "cot"), down_partial, 512, False, "down_grad")

    def end_kernel(*arrays):
        tile = tile_of(width, 768)

        def body(own_ref, *refs):
            total = add_shares(*refs[:-1]).astype(b16)
            for i in range(n_col):
                target = pl.multiple_of((own_ref[0] ^ x_outer[i]) * quarter, quarter)
                refs[-1][pl.ds(target, quarter), :] = total[i * quarter : (i + 1) * quarter]

        blocks_of = [pl.BlockSpec((a.shape[0], tile), lambda i: (0, i)) for a in arrays]
        return call(
            body,
            [own.astype(jnp.int32).reshape(1), *arrays],
            [pl.BlockSpec(memory_space=pltpu.SMEM)] + blocks_of,
            shape((rows, width), b16),
            blocks_of[0],
            (width // tile,),
            "end",
        )

    if aligned:
        return (end_kernel(work[0]["part"], *work[0]["part_came"], running), up_grad, down_grad)
    input_grad = work[0]["part"] + running.astype(f32)
    input_grad = input_grad.astype(b16).reshape(2, 2, quarter, width).transpose(1, 0, 2, 3).reshape(rows, width)
    return (reorder(input_grad, y_outer), up_grad, down_grad)


def solution(mesh):
    tokens = P(("dp", "row"), "col")
    up, down = P("col", ("dp", "row")), P(("dp", "row"), "col")
    return jax.shard_map(
        shards,
        mesh=mesh,
        in_specs=(tokens, up, down, tokens),
        out_specs=(tokens, up, down),
        check_vma=False,
    )
```

```python
import math

import jax
import jax.numpy as jnp
from jax import lax
from jax.experimental import pallas as pl
from jax.experimental.pallas import tpu as pltpu
from jax.sharding import PartitionSpec as P

gelu_const = math.sqrt(2.0 / math.pi)
f32, b16 = jnp.float32, jnp.bfloat16
FIRST_SUM, SECOND_JOIN = 5_000_000_000, 12_000_000_000


def gelu_both(value):
    square = value * value
    tangent = jnp.tanh(gelu_const * (value + 0.044715 * square * value))
    half = 0.5 * (1.0 + tangent)
    slope = half + 0.5 * value * (1.0 - tangent * tangent) * gelu_const * (1.0 + 3.0 * 0.044715 * square)
    return value * half, slope


def contract(left, right, at_left, at_right):
    return lax.dot_general(
        left, right, (((at_left,), (at_right,)), ((), ())), preferred_element_type=f32
    )


def call(body, operands, in_specs, outs, out_specs, grid, name, limit=8 * 2**20, flops=1000, scratch=()):
    return pl.pallas_call(
        body,
        grid=grid,
        in_specs=in_specs,
        out_specs=out_specs,
        out_shape=outs,
        scratch_shapes=list(scratch),
        compiler_params=pltpu.CompilerParams(vmem_limit_bytes=limit),
        cost_estimate=pl.CostEstimate(flops=flops, bytes_accessed=1000, transcendentals=0),
        name=name,
    )(*operands)


def shape(dims, dtype):
    return jax.ShapeDtypeStruct(dims, dtype)


def tile_of(size, most):
    return max(t for t in range(128, most + 1, 128) if size % t == 0)


whole = pl.BlockSpec(memory_space=pltpu.VMEM)


def first_product(chunk, weight, weight_dim, name):
    tokens = chunk.shape[0]
    hidden = weight.shape[1 - weight_dim]
    half = tokens // 2
    tile = tile_of(hidden, 512)

    def body(chunk_ref, weight_ref, sent_ref, kept_ref):
        for start in range(0, hidden, tile):
            span = pl.ds(start, tile)
            block = weight_ref[:, span] if weight_dim == 0 else weight_ref[span, :]
            total = contract(chunk_ref[...], block, 1, weight_dim)
            kept_ref[:, span] = total[:half]
            sent_ref[:, span] = total[half:].astype(b16)

    return call(
        body, [chunk, weight], [whole] * 2, [shape((half, hidden), b16), shape((half, hidden), f32)], [whole] * 2, (), name
    )


def add_halves(kept_h, came_h, kept_g, came_g, flops):
    tokens, hidden = kept_h.shape
    half = tokens // 2
    tile = tile_of(hidden, 768)

    def body(kh, ch, kg, cg, sent_h, next_h, sent_g, next_g):
        for kept, came, sent, rest in ((kh, ch, sent_h, next_h), (kg, cg, sent_g, next_g)):
            total = kept[...] + came[...].astype(f32)
            rest[...] = total[:half]
            sent[...] = total[half:].astype(b16)

    block = pl.BlockSpec((tokens, tile), lambda i: (0, i))
    part = pl.BlockSpec((half, tile), lambda i: (0, i))
    return call(
        body,
        [kept_h, came_h, kept_g, came_g],
        [block] * 4,
        [shape((half, hidden), b16), shape((half, hidden), f32)] * 2,
        [part] * 4,
        (hidden // tile,),
        "add_halves",
        flops=flops,
    )


def activate(kept_h, came_h, kept_g, came_g):
    tokens, hidden = kept_h.shape
    tile = tile_of(hidden, 768)

    def body(kh, ch, kg, cg, active_ref, delta_ref):
        value, slope = gelu_both(kh[...] + ch[...].astype(f32))
        active_ref[...] = value.astype(b16)
        delta_ref[...] = ((kg[...] + cg[...].astype(f32)) * slope).astype(b16)

    block = pl.BlockSpec((tokens, tile), lambda i: (0, i))
    return call(
        body, [kept_h, came_h, kept_g, came_g], [block] * 4, [shape((tokens, hidden), b16)] * 2, [block] * 2,
        (hidden // tile,), "activate",
    )


def join_pairs(flops, *arrays):
    rows, columns = arrays[0].shape
    tile = tile_of(columns, 1536)

    def body(*refs):
        for i, out in enumerate(refs[len(arrays):]):
            out[pl.ds(0, rows), :] = refs[2 * i][...]
            out[pl.ds(rows, rows), :] = refs[2 * i + 1][...]

    return call(
        body,
        arrays,
        [pl.BlockSpec((rows, tile), lambda i: (0, i))] * len(arrays),
        [shape((2 * rows, columns), arrays[0].dtype)] * (len(arrays) // 2),
        [pl.BlockSpec((2 * rows, tile), lambda i: (0, i))] * (len(arrays) // 2),
        (columns // tile,),
        "join_pairs",
        flops=flops,
    )


def input_product(delta, up_weight, quarter):
    tokens = delta.shape[0]
    width = up_weight.shape[0]
    tile = tile_of(width, 512)
    pairs = tokens // (2 * quarter)

    def body(delta_ref, weight_ref, kept_ref, *sent_refs):
        for start in range(0, width, tile):
            span = pl.ds(start, tile)
            total = contract(delta_ref[...], weight_ref[span, :], 1, 1)
            for i in range(pairs):
                first, second = 2 * i * quarter, (2 * i + 1) * quarter
                kept_ref[pl.ds(i * quarter, quarter), span] = total[first:second]
                sent_ref = sent_refs[2 * i // pairs]
                sent_ref[pl.ds(i % (pairs // 2) * quarter, quarter), span] = total[second : second + quarter]

    outs = [shape((tokens // 2, width), f32)] + [shape((tokens // 4, width), f32)] * 2
    return call(body, [delta, up_weight], [whole] * 2, outs, [whole] * 3, (), "input_product")


def add_shares(kept_ref, upper_ref, lower_ref, *rest):
    total = kept_ref[...] + jnp.concatenate([upper_ref[...], lower_ref[...]], axis=0)
    for ref in rest:
        total = total + ref[...].astype(f32)
    return total


def steps_of(*sizes):
    return max(n for n in range(1, 7) if all(size % (128 * n) == 0 for size in sizes))


def weight_total(lefts, rights, columns):
    total = contract(lefts[0][:, columns], rights[0][...], 0, 0)
    for left, right in zip(lefts[1:], rights[1:]):
        total = total + contract(left[:, columns], right[...], 0, 0)
    return total


def early_grad(lefts, rights, held, name):
    rows, columns = lefts[0].shape[1], rights[0].shape[1]
    steps = steps_of(rows)
    tile = rows // steps
    count = len(lefts)

    def body(*refs):
        mine = pl.ds(pl.multiple_of(pl.program_id(0) * tile, tile), tile)
        total = weight_total(refs[:count], refs[count:-1], mine)
        if held:
            refs[-1][mine, :] = total
        else:
            refs[-1][...] = total

    return call(
        body,
        [*lefts, *rights],
        [whole] * (2 * count),
        shape((rows, columns), f32) if held else pltpu.HBM((rows, columns), f32),
        whole if held else pl.BlockSpec((tile, columns), lambda i: (i, 0)),
        (steps,),
        name,
        14 * 2**20,
    )


def late_grads(inputs, deltas, actives, cotangents, up_partial, down_partial, scale):
    width, hidden = up_partial.shape
    steps = steps_of(width, hidden)
    up_tile, down_tile = width // steps, hidden // steps
    count = len(inputs)

    def body(*refs):
        groups = [refs[i * count : (i + 1) * count] for i in range(4)]
        up_part, down_part, up_ref, down_ref = refs[4 * count :]
        mine = pl.ds(pl.multiple_of(pl.program_id(0) * up_tile, up_tile), up_tile)
        total = weight_total(groups[0], groups[1], mine) + up_part[mine, :]
        up_ref[...] = (total * scale).astype(b16)
        mine = pl.ds(pl.multiple_of(pl.program_id(0) * down_tile, down_tile), down_tile)
        total = weight_total(groups[2], groups[3], mine) + down_part[...]
        down_ref[...] = (total * scale).astype(b16)

    up_block = pl.BlockSpec((up_tile, hidden), lambda i: (i, 0))
    down_block = pl.BlockSpec((down_tile, width), lambda i: (i, 0))
    return call(
        body,
        [*inputs, *deltas, *actives, *cotangents, up_partial, down_partial],
        [whole] * (4 * count + 1) + [down_block],
        [pltpu.HBM((width, hidden), b16), pltpu.HBM((hidden, width), b16)],
        [up_block, down_block],
        (steps,),
        "late_grads",
        26 * 2**20,
    )


def shards(inputs, up_weight, down_weight, cotangent):
    n_row = lax.axis_size("row")
    replicas = lax.axis_size("dp")
    n_col = lax.axis_size("col")
    assert replicas == 2 and n_col == 4 and n_row % 4 == 0
    rows, width = inputs.shape
    quarter = rows // n_col
    own = lax.axis_index("col")

    def swap_x(a):
        return lax.ppermute(a, "col", [(i, i ^ 1) for i in range(n_col)])

    def swap_y(a):
        return lax.ppermute(a, "col", [(i, i ^ 2) for i in range(n_col)])

    def swap_dp(a):
        return lax.ppermute(a, "dp", [(0, 1), (1, 0)])

    def pass_row(a):
        return lax.ppermute(a, "row", [(i, (i + 1) % n_row) for i in range(n_row)])

    def reorder(a, order):
        blocks = [lax.dynamic_slice_in_dim(a, (own ^ bits) * quarter, quarter, 0) for bits in order]
        return jnp.concatenate(blocks, axis=0)

    x_outer, y_outer = (0, 2, 1, 3), (0, 1, 2, 3)

    def reorder_both():
        def body(own_ref, inputs_ref, cotangent_ref, out_ref, done):
            copies = []
            for ref, order, base in ((inputs_ref, x_outer, 0), (cotangent_ref, y_outer, rows)):
                for i in range(n_col):
                    source = pl.multiple_of((own_ref[0] ^ order[i]) * quarter, quarter)
                    copies.append(
                        pltpu.make_async_copy(
                            ref.at[pl.ds(source, quarter), :],
                            out_ref.at[pl.ds(base + i * quarter, quarter), :],
                            done.at[len(copies)],
                        )
                    )
            for copy in copies:
                copy.start()
            for copy in copies:
                copy.wait()

        return call(
            body,
            [own.astype(jnp.int32).reshape(1), inputs, cotangent],
            [pl.BlockSpec(memory_space=pltpu.SMEM)] + [pl.BlockSpec(memory_space=pl.ANY)] * 2,
            shape((2 * rows, width), b16),
            whole,
            (),
            "reorder",
            scratch=[pltpu.SemaphoreType.DMA((2 * n_col,))],
        )

    if quarter % 16 == 0:
        moving = reorder_both()
    else:
        moving = jnp.concatenate([reorder(inputs, x_outer), reorder(cotangent, y_outer)], axis=0)

    group = n_row // 4
    tall = group * rows
    work = [{} for _ in range(4)]
    blocks = {0: [moving]}
    aligned = group == 1 and quarter % 16 == 0

    token = ()

    def after(*values):
        tied = lax.optimization_barrier((*values, *token))[: len(values)]
        return tied if len(values) > 1 else tied[0]

    def fetch(at):
        if at > 0:
            sent = blocks[at - 1][-1]
            if at > 2:
                sent = lax.optimization_barrier((sent, *work[at - 1]["other"]))[0]
            blocks[at] = [pass_row(sent)]
        while len(blocks[at]) < group:
            blocks[at].append(pass_row(blocks[at][-1]))

    def mirror(at):
        w = work[at]
        if at > 0:
            blocks[at][-1] = after(blocks[at][-1])
        w["mine"] = blocks[at][0] if group == 1 else jnp.concatenate(blocks[at])
        w["other"] = [swap_dp(part) for part in (jnp.split(w["mine"], 2) if at > 0 else [w["mine"]])]

    def arrived(at):
        nonlocal token
        token = (*token, blocks[at][-1])

    def build_kernel(mine, *others):
        def body(mine_ref, *refs):
            for part, out in enumerate(refs[-2:]):
                for i in range(n_col):
                    span = pl.ds(part * rows + i * quarter, quarter)
                    out[pl.ds(2 * i * quarter, quarter), :] = mine_ref[span, :]
                    if len(refs) == 3:
                        out[pl.ds((2 * i + 1) * quarter, quarter), :] = refs[0][span, :]
                    else:
                        out[pl.ds((2 * i + 1) * quarter, quarter), :] = refs[part][pl.ds(i * quarter, quarter), :]

        return call(
            body, [mine, *others], [whole] * (1 + len(others)), [shape((2 * rows, width), b16)] * 2, [whole] * 2, (), "build"
        )

    def build(at):
        nonlocal token
        w = work[at]
        mine, *others = after(w["mine"], *w["other"])
        if aligned:
            w["in"], w["cot"] = build_kernel(mine, *others)
        else:
            other = jnp.concatenate(others)
            pair = [a.reshape(group, 2 * n_col, quarter, width).transpose(1, 0, 2, 3) for a in (mine, other)]
            w["in"], w["cot"] = jnp.stack(pair, axis=2).reshape(2, 2 * tall, width)
        token = (w["in"], w["cot"])

    def products(at):
        nonlocal token
        w = work[at]
        w["h_out"], w["h"] = token = first_product(after(w["in"]), up_weight, 0, "hidden_product")
        w["g_out"], w["g"] = token = first_product(after(w["cot"]), down_weight, 1, "delta_act_product")

    def reduce_first(at):
        w = work[at]
        if at < 2:
            w["h_came"], w["g_came"] = swap_x(w["h_out"]), swap_y(w["g_out"])
        else:
            h_out, g_out = after(w["h_out"], w["g_out"])
            w["h_came"], w["g_came"] = swap_x(h_out), swap_y(g_out)

    def reduce_second(at):
        nonlocal token
        w = work[at]
        sent_h, w["h"], sent_g, w["g"] = token = add_halves(
            *after(w["h"], w["h_came"], w["g"], w["g_came"]), FIRST_SUM if at == 0 else 1000
        )
        w["h_came"], w["g_came"] = swap_y(sent_h), swap_x(sent_g)

    def gather_first(at):
        nonlocal token
        w = work[at]
        w["active"], w["delta"] = token = activate(*after(w["h"], w["h_came"], w["g"], w["g_came"]))
        w["delta_came"], w["active_came"] = swap_y(w["delta"]), swap_x(w["active"])

    def join(at, flops=1000):
        nonlocal token
        w = work[at]
        w["delta"], w["active"] = token = join_pairs(
            flops, *after(w["delta"], w["delta_came"], w["active"], w["active_came"])
        )

    def gather_second(at):
        w = work[at]
        join(at, SECOND_JOIN if at == 1 else 1000)
        w["delta_came"], w["active_came"] = swap_x(w["delta"]), swap_y(w["active"])

    def add_kernel(dtype, *arrays):
        tile = tile_of(width, 768)

        def body(*refs):
            refs[-1][...] = add_shares(*refs[:-1]).astype(dtype)

        blocks_of = [pl.BlockSpec((a.shape[0], tile), lambda i: (0, i)) for a in arrays]
        return call(body, arrays, blocks_of, shape((rows, width), dtype), blocks_of[0], (width // tile,), "add")

    def share(at):
        nonlocal token
        w = work[at]
        delta = after(w["delta"])
        if not aligned:
            parts = contract(delta, up_weight, 1, 1).reshape(n_col, group, 2, quarter, width)
            token = (parts,)
            w["part"], w["part_came"] = parts[:, :, 0], swap_dp(parts[:, :, 1])
        else:
            w["part"], *sent = token = input_product(delta, up_weight, quarter)
            w["part_came"] = [swap_dp(part) for part in sent]

    running = None

    def share_sum(at):
        nonlocal token, running
        w = work[at]
        if not aligned:
            part = w["part"] + w["part_came"]
            for step in range(at * group, (at + 1) * group):
                one = part[:, step - at * group].reshape(rows, width)
                if step == 0:
                    w["part"] = one
                else:
                    running = pass_row(one if running is None else running + one)
        elif at == 1:
            running = pass_row(add_kernel(f32, w["part"], *w["part_came"]))
        else:
            total = add_kernel(b16 if at == 3 else f32, *after(w["part"], *w["part_came"], running))
            token = (total,)
            running = pass_row(total)

    def settle():
        nonlocal token
        token = (*token, running)

    def early(names, held, name):
        nonlocal token
        values = after(*(work[at][k] for k in names for at in (0, 1)))
        token = (early_grad(values[:2], values[2:], held, name),)
        return token[0]

    def late(up_partial, down_partial):
        values = after(*(work[at][k] for k in ("in", "delta", "active", "cot") for at in (2, 3)))
        parts = [values[i : i + 2] for i in range(0, 8, 2)]
        return late_grads(*parts, up_partial, down_partial, 1.0 / replicas)

    fetch(0)
    mirror(0)
    fetch(1)
    build(0)
    products(0)
    reduce_first(0)
    mirror(1)
    build(1)
    products(1)
    reduce_first(1)
    reduce_second(0)
    fetch(2)
    reduce_second(1)
    gather_first(0)
    gather_first(1)
    arrived(2)
    mirror(2)
    gather_second(0)
    build(2)
    products(2)
    fetch(3)
    gather_second(1)
    join(0)
    reduce_first(2)
    arrived(3)
    mirror(3)
    build(3)
    products(3)
    share(0)
    if not aligned:
        share_sum(0)
    join(1)
    reduce_first(3)
    share(1)
    share_sum(1)
    up_partial = early(("in", "delta"), True, "up_grad_early")
    reduce_second(2)
    reduce_second(3)
    gather_first(2)
    gather_first(3)
    gather_second(2)
    gather_first(3)
    down_partial = early(("active", "cot"), False, "down_grad_early")
    settle()
    gather_second(3)
    join(2)
    share(2)
    share_sum(2)
    join(3)
    share(3)
    share_sum(3)
    up_grad, down_grad = late(up_partial, down_partial)

    def end_kernel(*arrays):
        tile = tile_of(width, 768)

        def body(own_ref, *refs):
            total = add_shares(*refs[:-1]).astype(b16)
            for i in range(n_col):
                target = pl.multiple_of((own_ref[0] ^ x_outer[i]) * quarter, quarter)
                refs[-1][pl.ds(target, quarter), :] = total[i * quarter : (i + 1) * quarter]

        blocks_of = [pl.BlockSpec((a.shape[0], tile), lambda i: (0, i)) for a in arrays]
        return call(
            body,
            [own.astype(jnp.int32).reshape(1), *arrays],
            [pl.BlockSpec(memory_space=pltpu.SMEM)] + blocks_of,
            shape((rows, width), b16),
            blocks_of[0],
            (width // tile,),
            "end",
        )

    if aligned:
        return (end_kernel(work[0]["part"], *work[0]["part_came"], running), up_grad, down_grad)
    input_grad = work[0]["part"] + running.astype(f32)
    input_grad = input_grad.astype(b16).reshape(2, 2, quarter, width).transpose(1, 0, 2, 3).reshape(rows, width)
    return (reorder(input_grad, y_outer), up_grad, down_grad)


def solution(mesh):
    tokens = P(("dp", "row"), "col")
    up, down = P("col", ("dp", "row")), P(("dp", "row"), "col")
    return jax.shard_map(
        shards,
        mesh=mesh,
        in_specs=(tokens, up, down, tokens),
        out_specs=(tokens, up, down),
        check_vma=False,
    )
```

```python
import math

import jax
import jax.numpy as jnp
from jax import lax
from jax.experimental import pallas as pl
from jax.experimental.pallas import tpu as pltpu
from jax.sharding import PartitionSpec as P

gelu_const = math.sqrt(2.0 / math.pi)
f32, b16 = jnp.float32, jnp.bfloat16
FIRST_SUM, ODD_JOIN = 5_000_000_000, 12_000_000_000


def gelu_both(value):
    square = value * value
    tangent = jnp.tanh(gelu_const * (value + 0.044715 * square * value))
    half = 0.5 * (1.0 + tangent)
    slope = half + 0.5 * value * (1.0 - tangent * tangent) * gelu_const * (1.0 + 3.0 * 0.044715 * square)
    return value * half, slope


def contract(left, right, at_left, at_right):
    return lax.dot_general(
        left, right, (((at_left,), (at_right,)), ((), ())), preferred_element_type=f32
    )


def call(body, operands, in_specs, outs, out_specs, grid, name, limit=8 * 2**20, flops=1000, scratch=()):
    return pl.pallas_call(
        body,
        grid=grid,
        in_specs=in_specs,
        out_specs=out_specs,
        out_shape=outs,
        scratch_shapes=list(scratch),
        compiler_params=pltpu.CompilerParams(vmem_limit_bytes=limit),
        cost_estimate=pl.CostEstimate(flops=flops, bytes_accessed=1000, transcendentals=0),
        name=name,
    )(*operands)


def shape(dims, dtype):
    return jax.ShapeDtypeStruct(dims, dtype)


def tile_of(size, most):
    return max(t for t in range(128, most + 1, 128) if size % t == 0)


whole = pl.BlockSpec(memory_space=pltpu.VMEM)


def first_product(chunk, weight, weight_dim, name):
    tokens = chunk.shape[0]
    hidden = weight.shape[1 - weight_dim]
    half = tokens // 2
    tile = tile_of(hidden, 512)

    def body(chunk_ref, weight_ref, sent_ref, kept_ref):
        for start in range(0, hidden, tile):
            span = pl.ds(start, tile)
            block = weight_ref[:, span] if weight_dim == 0 else weight_ref[span, :]
            total = contract(chunk_ref[...], block, 1, weight_dim)
            kept_ref[:, span] = total[:half]
            sent_ref[:, span] = total[half:].astype(b16)

    return call(
        body, [chunk, weight], [whole] * 2, [shape((half, hidden), b16), shape((half, hidden), f32)], [whole] * 2, (), name
    )


def add_halves(kept_h, came_h, kept_g, came_g, flops):
    tokens, hidden = kept_h.shape
    half = tokens // 2
    tile = tile_of(hidden, 768)

    def body(kh, ch, kg, cg, sent_h, next_h, sent_g, next_g):
        for kept, came, sent, rest in ((kh, ch, sent_h, next_h), (kg, cg, sent_g, next_g)):
            total = kept[...] + came[...].astype(f32)
            rest[...] = total[:half]
            sent[...] = total[half:].astype(b16)

    block = pl.BlockSpec((tokens, tile), lambda i: (0, i))
    part = pl.BlockSpec((half, tile), lambda i: (0, i))
    return call(
        body,
        [kept_h, came_h, kept_g, came_g],
        [block] * 4,
        [shape((half, hidden), b16), shape((half, hidden), f32)] * 2,
        [part] * 4,
        (hidden // tile,),
        "add_halves",
        flops=flops,
    )


def activate(kept_h, came_h, kept_g, came_g):
    tokens, hidden = kept_h.shape
    tile = tile_of(hidden, 768)

    def body(kh, ch, kg, cg, active_ref, delta_ref):
        value, slope = gelu_both(kh[...] + ch[...].astype(f32))
        active_ref[...] = value.astype(b16)
        delta_ref[...] = ((kg[...] + cg[...].astype(f32)) * slope).astype(b16)

    block = pl.BlockSpec((tokens, tile), lambda i: (0, i))
    return call(
        body, [kept_h, came_h, kept_g, came_g], [block] * 4, [shape((tokens, hidden), b16)] * 2, [block] * 2,
        (hidden // tile,), "activate",
    )


def join_pairs(flops, *arrays):
    rows, columns = arrays[0].shape
    tile = tile_of(columns, 1536)

    def body(*refs):
        for i, out in enumerate(refs[len(arrays):]):
            out[pl.ds(0, rows), :] = refs[2 * i][...]
            out[pl.ds(rows, rows), :] = refs[2 * i + 1][...]

    return call(
        body,
        arrays,
        [pl.BlockSpec((rows, tile), lambda i: (0, i))] * len(arrays),
        [shape((2 * rows, columns), arrays[0].dtype)] * (len(arrays) // 2),
        [pl.BlockSpec((2 * rows, tile), lambda i: (0, i))] * (len(arrays) // 2),
        (columns // tile,),
        "join_pairs",
        flops=flops,
    )


def input_product(delta, up_weight, quarter, cuts):
    tokens = delta.shape[0]
    width = up_weight.shape[0]
    tile = tile_of(width, 512)
    pairs = tokens // (2 * quarter)

    def body(delta_ref, weight_ref, kept_ref, *sent_refs):
        for start in range(0, width, tile):
            span = pl.ds(start, tile)
            total = contract(delta_ref[...], weight_ref[span, :], 1, 1)
            for i in range(pairs):
                first, second = 2 * i * quarter, (2 * i + 1) * quarter
                kept_ref[pl.ds(i * quarter, quarter), span] = total[first:second]
                sent_ref = sent_refs[cuts * i // pairs]
                sent_ref[pl.ds(i % (pairs // cuts) * quarter, quarter), span] = total[second : second + quarter]

    outs = [shape((tokens // 2, width), f32)] + [shape((tokens // (2 * cuts), width), f32)] * cuts
    return call(body, [delta, up_weight], [whole] * 2, outs, [whole] * (1 + cuts), (), "input_product")


def add_shares(kept_ref, *rest):
    total, cut = kept_ref[...], kept_ref.shape[0] // 2
    while rest:
        if rest[0].shape[0] == cut:
            total = total + jnp.concatenate([rest[0][...], rest[1][...]], axis=0)
            rest = rest[2:]
        else:
            total = total + rest[0][...].astype(f32)
            rest = rest[1:]
    return total


def steps_of(*sizes):
    return max(n for n in range(1, 7) if all(size % (128 * n) == 0 for size in sizes))


def weight_total(lefts, rights, columns):
    total = contract(lefts[0][:, columns], rights[0][...], 0, 0)
    for left, right in zip(lefts[1:], rights[1:]):
        total = total + contract(left[:, columns], right[...], 0, 0)
    return total


def early_grad(lefts, rights, held, name):
    rows, columns = lefts[0].shape[1], rights[0].shape[1]
    steps = steps_of(rows)
    tile = rows // steps
    count = len(lefts)

    def body(*refs):
        mine = pl.ds(pl.multiple_of(pl.program_id(0) * tile, tile), tile)
        total = weight_total(refs[:count], refs[count:-1], mine)
        if held:
            refs[-1][mine, :] = total
        else:
            refs[-1][...] = total

    return call(
        body,
        [*lefts, *rights],
        [whole] * (2 * count),
        shape((rows, columns), f32) if held else pltpu.HBM((rows, columns), f32),
        whole if held else pl.BlockSpec((tile, columns), lambda i: (i, 0)),
        (steps,),
        name,
        14 * 2**20,
    )


def late_grad(lefts, rights, partial, held, scale, name):
    rows, columns = partial.shape
    steps = steps_of(rows)
    tile = rows // steps
    count = len(lefts)

    def body(*refs):
        mine = pl.ds(pl.multiple_of(pl.program_id(0) * tile, tile), tile)
        total = weight_total(refs[:count], refs[count : 2 * count], mine)
        total = total + (refs[-2][mine, :] if held else refs[-2][...])
        refs[-1][...] = (total * scale).astype(b16)

    block = pl.BlockSpec((tile, columns), lambda i: (i, 0))
    return call(
        body,
        [*lefts, *rights, partial],
        [whole] * (2 * count) + [whole if held else block],
        pltpu.HBM((rows, columns), b16),
        block,
        (steps,),
        name,
        14 * 2**20,
    )


def shards(inputs, up_weight, down_weight, cotangent):
    n_row = lax.axis_size("row")
    replicas = lax.axis_size("dp")
    n_col = lax.axis_size("col")
    assert replicas == 2 and n_col == 4 and n_row % 4 == 0
    rows, width = inputs.shape
    quarter = rows // n_col
    own = lax.axis_index("col")

    def swap_x(a):
        return lax.ppermute(a, "col", [(i, i ^ 1) for i in range(n_col)])

    def swap_y(a):
        return lax.ppermute(a, "col", [(i, i ^ 2) for i in range(n_col)])

    def swap_dp(a):
        return lax.ppermute(a, "dp", [(0, 1), (1, 0)])

    def pass_row(a):
        return lax.ppermute(a, "row", [(i, (i + 1) % n_row) for i in range(n_row)])

    def reorder(a, order):
        blocks = [lax.dynamic_slice_in_dim(a, (own ^ bits) * quarter, quarter, 0) for bits in order]
        return jnp.concatenate(blocks, axis=0)

    x_outer, y_outer = (0, 2, 1, 3), (0, 1, 2, 3)

    def reorder_both():
        def body(own_ref, inputs_ref, cotangent_ref, out_ref, done):
            copies = []
            for ref, order, base in ((inputs_ref, x_outer, 0), (cotangent_ref, y_outer, rows)):
                for i in range(n_col):
                    source = pl.multiple_of((own_ref[0] ^ order[i]) * quarter, quarter)
                    copies.append(
                        pltpu.make_async_copy(
                            ref.at[pl.ds(source, quarter), :],
                            out_ref.at[pl.ds(base + i * quarter, quarter), :],
                            done.at[len(copies)],
                        )
                    )
            for copy in copies:
                copy.start()
            for copy in copies:
                copy.wait()

        return call(
            body,
            [own.astype(jnp.int32).reshape(1)]
            + [pltpu.with_memory_space_constraint(a, pltpu.HBM) for a in (inputs, cotangent)],
            [pl.BlockSpec(memory_space=pltpu.SMEM)] + [pl.BlockSpec(memory_space=pltpu.HBM)] * 2,
            shape((2 * rows, width), b16),
            whole,
            (),
            "reorder",
            scratch=[pltpu.SemaphoreType.DMA((2 * n_col,))],
        )

    if quarter % 16 == 0:
        moving = reorder_both()
    else:
        moving = jnp.concatenate([reorder(inputs, x_outer), reorder(cotangent, y_outer)], axis=0)

    group = n_row // 4
    tall = group * rows
    work = [{} for _ in range(4)]
    blocks = {0: [moving]}
    aligned = group == 1 and quarter % 16 == 0

    token = ()

    def after(*values):
        tied = lax.optimization_barrier((*values, *token))[: len(values)]
        return tied if len(values) > 1 else tied[0]

    def fetch(at):
        if at > 0:
            sent = blocks[at - 1][-1]
            if at > 2:
                sent = lax.optimization_barrier((sent, *work[at - 1]["other"]))[0]
            blocks[at] = [pass_row(sent)]
        while len(blocks[at]) < group:
            blocks[at].append(pass_row(blocks[at][-1]))

    def mirror(at):
        w = work[at]
        if at > 0:
            blocks[at][-1] = after(blocks[at][-1])
        w["mine"] = blocks[at][0] if group == 1 else jnp.concatenate(blocks[at])
        w["other"] = [swap_dp(part) for part in (jnp.split(w["mine"], 2) if at > 0 else [w["mine"]])]

    def arrived(at):
        nonlocal token
        token = (*token, blocks[at][-1])

    def build_kernel(mine, *others):
        def body(mine_ref, *refs):
            for part, out in enumerate(refs[-2:]):
                for i in range(n_col):
                    span = pl.ds(part * rows + i * quarter, quarter)
                    out[pl.ds(2 * i * quarter, quarter), :] = mine_ref[span, :]
                    if len(refs) == 3:
                        out[pl.ds((2 * i + 1) * quarter, quarter), :] = refs[0][span, :]
                    else:
                        out[pl.ds((2 * i + 1) * quarter, quarter), :] = refs[part][pl.ds(i * quarter, quarter), :]

        return call(
            body, [mine, *others], [whole] * (1 + len(others)), [shape((2 * rows, width), b16)] * 2, [whole] * 2, (), "build"
        )

    def build(at):
        nonlocal token
        w = work[at]
        mine, *others = after(w["mine"], *w["other"])
        if aligned:
            w["in"], w["cot"] = build_kernel(mine, *others)
        else:
            other = jnp.concatenate(others)
            pair = [a.reshape(group, 2 * n_col, quarter, width).transpose(1, 0, 2, 3) for a in (mine, other)]
            w["in"], w["cot"] = jnp.stack(pair, axis=2).reshape(2, 2 * tall, width)
        token = (w["in"], w["cot"])

    def products(at):
        nonlocal token
        w = work[at]
        w["h_out"], w["h"] = token = first_product(after(w["in"]), up_weight, 0, "hidden_product")
        w["g_out"], w["g"] = token = first_product(after(w["cot"]), down_weight, 1, "delta_act_product")

    def reduce_first(at):
        w = work[at]
        if at < 2:
            w["h_came"], w["g_came"] = swap_x(w["h_out"]), swap_y(w["g_out"])
        else:
            h_out, g_out = after(w["h_out"], w["g_out"])
            w["h_came"], w["g_came"] = swap_x(h_out), swap_y(g_out)

    def reduce_second(at):
        nonlocal token
        w = work[at]
        sent_h, w["h"], sent_g, w["g"] = token = add_halves(
            *after(w["h"], w["h_came"], w["g"], w["g_came"]), FIRST_SUM if at == 0 else 1000
        )
        w["h_came"], w["g_came"] = swap_y(sent_h), swap_x(sent_g)

    def gather_first(at):
        nonlocal token
        w = work[at]
        w["active"], w["delta"] = token = activate(*after(w["h"], w["h_came"], w["g"], w["g_came"]))
        w["delta_came"], w["active_came"] = swap_y(w["delta"]), swap_x(w["active"])

    def join(at, flops=1000):
        nonlocal token
        w = work[at]
        w["delta"], w["active"] = token = join_pairs(
            flops, *after(w["delta"], w["delta_came"], w["active"], w["active_came"])
        )

    def gather_second(at):
        w = work[at]
        join(at, ODD_JOIN if at % 2 else 1000)
        w["delta_came"], w["active_came"] = swap_x(w["delta"]), swap_y(w["active"])

    def add_kernel(dtype, *arrays):
        tile = tile_of(width, 768)

        def body(*refs):
            refs[-1][...] = add_shares(*refs[:-1]).astype(dtype)

        blocks_of = [pl.BlockSpec((a.shape[0], tile), lambda i: (0, i)) for a in arrays]
        return call(body, arrays, blocks_of, shape((rows, width), dtype), blocks_of[0], (width // tile,), "add")

    def share(at):
        nonlocal token
        w = work[at]
        delta = after(w["delta"])
        if not aligned:
            parts = contract(delta, up_weight, 1, 1).reshape(n_col, group, 2, quarter, width)
            token = (parts,)
            w["part"], w["part_came"] = parts[:, :, 0], swap_dp(parts[:, :, 1])
        else:
            w["part"], *sent = token = input_product(delta, up_weight, quarter, 1 if at < 2 else 2)
            w["part_came"] = [swap_dp(part) for part in sent]

    running = None

    def share_sum(at):
        nonlocal token, running
        w = work[at]
        if not aligned:
            part = w["part"] + w["part_came"]
            for step in range(at * group, (at + 1) * group):
                one = part[:, step - at * group].reshape(rows, width)
                if step == 0:
                    w["part"] = one
                else:
                    running = pass_row(one if running is None else running + one)
        elif at == 1:
            running = pass_row(add_kernel(f32, w["part"], *w["part_came"]))
        else:
            total = add_kernel(b16 if at == 3 else f32, *after(w["part"], *w["part_came"], running))
            token = (total,)
            running = pass_row(total)

    def settle():
        nonlocal token
        token = (*token, running)

    def early(names, held, name):
        nonlocal token
        values = after(*(work[at][k] for k in names for at in (0, 1)))
        token = (early_grad(values[:2], values[2:], held, name),)
        return token[0]

    def late(names, partial, held, name):
        nonlocal token
        values = after(*(work[at][k] for k in names for at in (2, 3)))
        token = (late_grad(values[:2], values[2:], partial, held, 1.0 / replicas, name),)
        return token[0]

    fetch(0)
    mirror(0)
    fetch(1)
    build(0)
    products(0)
    reduce_first(0)
    mirror(1)
    build(1)
    products(1)
    reduce_first(1)
    reduce_second(0)
    fetch(2)
    reduce_second(1)
    gather_first(0)
    gather_first(1)
    arrived(2)
    mirror(2)
    gather_second(0)
    build(2)
    products(2)
    fetch(3)
    gather_second(1)
    join(0)
    reduce_first(2)
    arrived(3)
    mirror(3)
    build(3)
    products(3)
    share(0)
    if not aligned:
        share_sum(0)
    join(1)
    reduce_first(3)
    share(1)
    share_sum(1)
    up_partial = early(("in", "delta"), True, "up_grad_early")
    reduce_second(2)
    reduce_second(3)
    gather_first(2)
    gather_first(3)
    gather_second(2)
    down_partial = early(("active", "cot"), False, "down_grad_early")
    settle()
    gather_second(3)
    join(2)
    share(2)
    share_sum(2)
    join(3)
    share(3)
    up_grad = late(("in", "delta"), up_partial, True, "up_grad")
    share_sum(3)
    down_grad = late(("active", "cot"), down_partial, False, "down_grad")

    def end_kernel(*arrays):
        tile = tile_of(width, 768)

        def body(own_ref, *refs):
            total = add_shares(*refs[:-1]).astype(b16)
            for i in range(n_col):
                target = pl.multiple_of((own_ref[0] ^ x_outer[i]) * quarter, quarter)
                refs[-1][pl.ds(target, quarter), :] = total[i * quarter : (i + 1) * quarter]

        blocks_of = [pl.BlockSpec((a.shape[0], tile), lambda i: (0, i)) for a in arrays]
        return call(
            body,
            [own.astype(jnp.int32).reshape(1), *arrays],
            [pl.BlockSpec(memory_space=pltpu.SMEM)] + blocks_of,
            shape((rows, width), b16),
            blocks_of[0],
            (width // tile,),
            "end",
        )

    if aligned:
        return (end_kernel(work[0]["part"], *work[0]["part_came"], running), up_grad, down_grad)
    input_grad = work[0]["part"] + running.astype(f32)
    input_grad = input_grad.astype(b16).reshape(2, 2, quarter, width).transpose(1, 0, 2, 3).reshape(rows, width)
    return (reorder(input_grad, y_outer), up_grad, down_grad)


def solution(mesh):
    tokens = P(("dp", "row"), "col")
    up, down = P("col", ("dp", "row")), P(("dp", "row"), "col")
    return jax.shard_map(
        shards,
        mesh=mesh,
        in_specs=(tokens, up, down, tokens),
        out_specs=(tokens, up, down),
        check_vma=False,
    )
```

```python
import math

import jax
import jax.numpy as jnp
from jax import lax
from jax.experimental import pallas as pl
from jax.experimental.pallas import tpu as pltpu
from jax.sharding import PartitionSpec as P

gelu_const = math.sqrt(2.0 / math.pi)
f32, b16 = jnp.float32, jnp.bfloat16
FIRST_SUM, ODD_JOIN = 5_000_000_000, 12_000_000_000


def gelu_both(value):
    square = value * value
    tangent = jnp.tanh(gelu_const * (value + 0.044715 * square * value))
    half = 0.5 * (1.0 + tangent)
    slope = half + 0.5 * value * (1.0 - tangent * tangent) * gelu_const * (1.0 + 3.0 * 0.044715 * square)
    return value * half, slope


def contract(left, right, at_left, at_right):
    return lax.dot_general(
        left, right, (((at_left,), (at_right,)), ((), ())), preferred_element_type=f32
    )


def call(body, operands, in_specs, outs, out_specs, grid, name, limit=4 * 2**20, flops=1000, scratch=()):
    return pl.pallas_call(
        body,
        grid=grid,
        in_specs=in_specs,
        out_specs=out_specs,
        out_shape=outs,
        scratch_shapes=list(scratch),
        compiler_params=pltpu.CompilerParams(vmem_limit_bytes=limit),
        cost_estimate=pl.CostEstimate(flops=flops, bytes_accessed=1000, transcendentals=0),
        name=name,
    )(*operands)


def shape(dims, dtype):
    return jax.ShapeDtypeStruct(dims, dtype)


def tile_of(size, most):
    return max(t for t in range(128, most + 1, 128) if size % t == 0)


whole = pl.BlockSpec(memory_space=pltpu.VMEM)


def first_product(chunk, weight, weight_dim, name):
    tokens = chunk.shape[0]
    hidden = weight.shape[1 - weight_dim]
    half = tokens // 2
    tile = tile_of(hidden, 512)

    def body(chunk_ref, weight_ref, sent_ref, kept_ref):
        for start in range(0, hidden, tile):
            span = pl.ds(start, tile)
            block = weight_ref[:, span] if weight_dim == 0 else weight_ref[span, :]
            total = contract(chunk_ref[...], block, 1, weight_dim)
            kept_ref[:, span] = total[:half]
            sent_ref[:, span] = total[half:].astype(b16)

    return call(
        body,
        [chunk, weight],
        [whole] * 2,
        [shape((half, hidden), b16), shape((half, hidden), f32)],
        [whole] * 2,
        (),
        name,
    )


def add_halves(kept_h, came_h, kept_g, came_g, flops):
    tokens, hidden = kept_h.shape
    half = tokens // 2
    tile = tile_of(hidden, 768)

    def body(kh, ch, kg, cg, sent_h, next_h, sent_g, next_g):
        for kept, came, sent, rest in ((kh, ch, sent_h, next_h), (kg, cg, sent_g, next_g)):
            total = kept[...] + came[...].astype(f32)
            rest[...] = total[:half]
            sent[...] = total[half:].astype(b16)

    block = pl.BlockSpec((tokens, tile), lambda i: (0, i))
    part = pl.BlockSpec((half, tile), lambda i: (0, i))
    return call(
        body,
        [kept_h, came_h, kept_g, came_g],
        [block] * 4,
        [shape((half, hidden), b16), shape((half, hidden), f32)] * 2,
        [part] * 4,
        (hidden // tile,),
        "add_halves",
        flops=flops,
    )


def activate(kept_h, came_h, kept_g, came_g):
    tokens, hidden = kept_h.shape
    tile = tile_of(hidden, 768)

    def body(kh, ch, kg, cg, active_ref, delta_ref):
        value, slope = gelu_both(kh[...] + ch[...].astype(f32))
        active_ref[...] = value.astype(b16)
        delta_ref[...] = ((kg[...] + cg[...].astype(f32)) * slope).astype(b16)

    block = pl.BlockSpec((tokens, tile), lambda i: (0, i))
    return call(
        body, [kept_h, came_h, kept_g, came_g], [block] * 4, [shape((tokens, hidden), b16)] * 2, [block] * 2,
        (hidden // tile,), "activate",
    )


def join_pairs(flops, *arrays):
    rows, columns = arrays[0].shape
    tile = tile_of(columns, 1536)

    def body(*refs):
        for i, out in enumerate(refs[len(arrays):]):
            out[pl.ds(0, rows), :] = refs[2 * i][...]
            out[pl.ds(rows, rows), :] = refs[2 * i + 1][...]

    return call(
        body,
        arrays,
        [pl.BlockSpec((rows, tile), lambda i: (0, i))] * len(arrays),
        [shape((2 * rows, columns), arrays[0].dtype)] * (len(arrays) // 2),
        [pl.BlockSpec((2 * rows, tile), lambda i: (0, i))] * (len(arrays) // 2),
        (columns // tile,),
        "join_pairs",
        7 * 2**20,
        flops,
    )


def input_product(delta, up_weight, quarter, cuts):
    tokens = delta.shape[0]
    width = up_weight.shape[0]
    tile = tile_of(width, 512)
    pairs = tokens // (2 * quarter)

    def body(delta_ref, weight_ref, kept_ref, *sent_refs):
        for start in range(0, width, tile):
            span = pl.ds(start, tile)
            total = contract(delta_ref[...], weight_ref[span, :], 1, 1)
            for i in range(pairs):
                first, second = 2 * i * quarter, (2 * i + 1) * quarter
                kept_ref[pl.ds(i * quarter, quarter), span] = total[first:second]
                sent_ref = sent_refs[cuts * i // pairs]
                sent_ref[pl.ds(i % (pairs // cuts) * quarter, quarter), span] = total[second : second + quarter]

    outs = [shape((tokens // 2, width), f32)] + [shape((tokens // (2 * cuts), width), f32)] * cuts
    return call(body, [delta, up_weight], [whole] * 2, outs, [whole] * (1 + cuts), (), "input_product")


def add_shares(kept_ref, *rest):
    total, cut = kept_ref[...], kept_ref.shape[0] // 2
    while rest:
        if rest[0].shape[0] == cut:
            total = total + jnp.concatenate([rest[0][...], rest[1][...]], axis=0)
            rest = rest[2:]
        else:
            total = total + rest[0][...].astype(f32)
            rest = rest[1:]
    return total


def steps_of(*sizes):
    return max(n for n in range(1, 7) if all(size % (128 * n) == 0 for size in sizes))


def weight_total(lefts, rights, columns):
    total = contract(lefts[0][:, columns], rights[0][...], 0, 0)
    for left, right in zip(lefts[1:], rights[1:]):
        total = total + contract(left[:, columns], right[...], 0, 0)
    return total


def early_grad(lefts, rights, held, name):
    rows, columns = lefts[0].shape[1], rights[0].shape[1]
    steps = steps_of(rows)
    tile = rows // steps
    count = len(lefts)

    def body(*refs):
        mine = pl.ds(pl.multiple_of(pl.program_id(0) * tile, tile), tile)
        total = weight_total(refs[:count], refs[count:-1], mine)
        if held:
            refs[-1][mine, :] = total
        else:
            refs[-1][...] = total

    return call(
        body,
        [*lefts, *rights],
        [whole] * (2 * count),
        shape((rows, columns), f32) if held else pltpu.HBM((rows, columns), f32),
        whole if held else pl.BlockSpec((tile, columns), lambda i: (i, 0)),
        (steps,),
        name,
        10 * 2**20,
    )


def late_grad(lefts, rights, partial, held, scale, name):
    rows, columns = partial.shape
    steps = steps_of(rows)
    tile = rows // steps
    count = len(lefts)

    def body(*refs):
        mine = pl.ds(pl.multiple_of(pl.program_id(0) * tile, tile), tile)
        total = weight_total(refs[:count], refs[count : 2 * count], mine)
        total = total + (refs[-2][mine, :] if held else refs[-2][...])
        refs[-1][...] = (total * scale).astype(b16)

    block = pl.BlockSpec((tile, columns), lambda i: (i, 0))
    return call(
        body,
        [*lefts, *rights, partial],
        [whole] * (2 * count) + [whole if held else block],
        pltpu.HBM((rows, columns), b16),
        block,
        (steps,),
        name,
        8 * 2**20,
    )


def shards(inputs, up_weight, down_weight, cotangent):
    n_row = lax.axis_size("row")
    replicas = lax.axis_size("dp")
    n_col = lax.axis_size("col")
    assert replicas == 2 and n_col == 4 and n_row % 4 == 0
    rows, width = inputs.shape
    quarter = rows // n_col
    own = lax.axis_index("col")

    def swap_x(a):
        return lax.ppermute(a, "col", [(i, i ^ 1) for i in range(n_col)])

    def swap_y(a):
        return lax.ppermute(a, "col", [(i, i ^ 2) for i in range(n_col)])

    def swap_dp(a):
        return lax.ppermute(a, "dp", [(0, 1), (1, 0)])

    def pass_row(a):
        return lax.ppermute(a, "row", [(i, (i + 1) % n_row) for i in range(n_row)])

    def reorder(a, order):
        blocks = [lax.dynamic_slice_in_dim(a, (own ^ bits) * quarter, quarter, 0) for bits in order]
        return jnp.concatenate(blocks, axis=0)

    x_outer, y_outer = (0, 2, 1, 3), (0, 1, 2, 3)

    def reorder_both():
        def body(own_ref, inputs_ref, cotangent_ref, out_ref, done):
            copies = []
            for ref, order, base in ((inputs_ref, x_outer, 0), (cotangent_ref, y_outer, rows)):
                for i in range(n_col):
                    source = pl.multiple_of((own_ref[0] ^ order[i]) * quarter, quarter)
                    copies.append(
                        pltpu.make_async_copy(
                            ref.at[pl.ds(source, quarter), :],
                            out_ref.at[pl.ds(base + i * quarter, quarter), :],
                            done.at[len(copies)],
                        )
                    )
            for copy in copies:
                copy.start()
            for copy in copies:
                copy.wait()

        return call(
            body,
            [own.astype(jnp.int32).reshape(1)]
            + [pltpu.with_memory_space_constraint(a, pltpu.HBM) for a in (inputs, cotangent)],
            [pl.BlockSpec(memory_space=pltpu.SMEM)] + [pl.BlockSpec(memory_space=pltpu.HBM)] * 2,
            shape((2 * rows, width), b16),
            whole,
            (),
            "reorder",
            scratch=[pltpu.SemaphoreType.DMA((2 * n_col,))],
        )

    if quarter % 16 == 0:
        moving = reorder_both()
    else:
        moving = jnp.concatenate([reorder(inputs, x_outer), reorder(cotangent, y_outer)], axis=0)

    group = n_row // 4
    tall = group * rows
    work = [{} for _ in range(4)]
    blocks = {0: [moving]}
    aligned = group == 1 and quarter % 16 == 0

    token = ()

    def after(*values):
        tied = lax.optimization_barrier((*values, *token))[: len(values)]
        return tied if len(values) > 1 else tied[0]

    def fetch(at):
        if at > 0:
            sent = blocks[at - 1][-1]
            if at > 2:
                sent = after(sent, *work[at - 1]["other"])[0]
            blocks[at] = [pass_row(sent)]
        while len(blocks[at]) < group:
            blocks[at].append(pass_row(blocks[at][-1]))

    def mirror(at):
        w = work[at]
        if at > 0:
            blocks[at][-1] = after(blocks[at][-1])
        w["mine"] = blocks[at][0] if group == 1 else jnp.concatenate(blocks[at])
        w["other"] = [swap_dp(part) for part in (jnp.split(w["mine"], 2) if at > 0 else [w["mine"]])]

    def arrived(at):
        nonlocal token
        token = (*token, blocks[at][-1])

    def build_kernel(mine, *others):
        def body(mine_ref, *refs):
            for part, out in enumerate(refs[-2:]):
                for i in range(n_col):
                    span = pl.ds(part * rows + i * quarter, quarter)
                    out[pl.ds(2 * i * quarter, quarter), :] = mine_ref[span, :]
                    if len(refs) == 3:
                        out[pl.ds((2 * i + 1) * quarter, quarter), :] = refs[0][span, :]
                    else:
                        out[pl.ds((2 * i + 1) * quarter, quarter), :] = refs[part][pl.ds(i * quarter, quarter), :]

        return call(
            body, [mine, *others], [whole] * (1 + len(others)), [shape((2 * rows, width), b16)] * 2, [whole] * 2, (), "build"
        )

    def build(at):
        nonlocal token
        w = work[at]
        mine, *others = after(w["mine"], *w["other"])
        if aligned:
            w["in"], w["cot"] = build_kernel(mine, *others)
        else:
            other = jnp.concatenate(others)
            pair = [a.reshape(group, 2 * n_col, quarter, width).transpose(1, 0, 2, 3) for a in (mine, other)]
            w["in"], w["cot"] = jnp.stack(pair, axis=2).reshape(2, 2 * tall, width)
        token = (w["in"], w["cot"])

    def products(at):
        nonlocal token
        w = work[at]
        w["h_out"], w["h"] = token = first_product(after(w["in"]), up_weight, 0, "hidden_product")
        w["g_out"], w["g"] = token = first_product(after(w["cot"]), down_weight, 1, "delta_act_product")

    def reduce_first(at):
        w = work[at]
        if at < 2:
            w["h_came"], w["g_came"] = swap_x(w["h_out"]), swap_y(w["g_out"])
        else:
            h_out, g_out = after(w["h_out"], w["g_out"])
            w["h_came"], w["g_came"] = swap_x(h_out), swap_y(g_out)

    def reduce_second(at):
        nonlocal token
        w = work[at]
        sent_h, w["h"], sent_g, w["g"] = token = add_halves(
            *after(w["h"], w["h_came"], w["g"], w["g_came"]), FIRST_SUM if at == 0 else 1000
        )
        w["h_came"], w["g_came"] = swap_y(sent_h), swap_x(sent_g)

    def gather_first(at):
        nonlocal token
        w = work[at]
        w["active"], w["delta"] = token = activate(*after(w["h"], w["h_came"], w["g"], w["g_came"]))
        w["delta_came"], w["active_came"] = swap_y(w["delta"]), swap_x(w["active"])

    def join(at, flops=1000):
        nonlocal token
        w = work[at]
        w["delta"], w["active"] = token = join_pairs(
            flops, *after(w["delta"], w["delta_came"], w["active"], w["active_came"])
        )

    def gather_second(at):
        w = work[at]
        join(at, ODD_JOIN if at % 2 else 1000)
        w["delta_came"], w["active_came"] = swap_x(w["delta"]), swap_y(w["active"])

    def add_kernel(dtype, *arrays):
        tile = tile_of(width, 768)

        def body(*refs):
            refs[-1][...] = add_shares(*refs[:-1]).astype(dtype)

        blocks_of = [pl.BlockSpec((a.shape[0], tile), lambda i: (0, i)) for a in arrays]
        return call(body, arrays, blocks_of, shape((rows, width), dtype), blocks_of[0], (width // tile,), "add")

    def share(at):
        nonlocal token
        w = work[at]
        delta = after(w["delta"])
        if not aligned:
            parts = contract(delta, up_weight, 1, 1).reshape(n_col, group, 2, quarter, width)
            token = (parts,)
            w["part"], w["part_came"] = parts[:, :, 0], swap_dp(parts[:, :, 1])
        else:
            w["part"], *sent = token = input_product(delta, up_weight, quarter, 1 if at < 2 else 2)
            w["part_came"] = [swap_dp(part) for part in sent]

    running = None

    def share_sum(at):
        nonlocal token, running
        w = work[at]
        if not aligned:
            part = w["part"] + w["part_came"]
            for step in range(at * group, (at + 1) * group):
                one = part[:, step - at * group].reshape(rows, width)
                if step == 0:
                    w["part"] = one
                else:
                    running = pass_row(one if running is None else running + one)
        elif at == 1:
            running = pass_row(add_kernel(f32, w["part"], *w["part_came"]))
        else:
            total = add_kernel(b16 if at == 3 else f32, *after(w["part"], *w["part_came"], running))
            token = (total,)
            running = pass_row(total)

    def settle():
        nonlocal token
        token = (*token, running)

    def early(names, held, name):
        nonlocal token
        values = after(*(work[at][k] for k in names for at in (0, 1)))
        token = (early_grad(values[:2], values[2:], held, name),)
        return token[0]

    def late(names, partial, held, name):
        nonlocal token
        values = after(*(work[at][k] for k in names for at in (2, 3)))
        token = (late_grad(values[:2], values[2:], partial, held, 1.0 / replicas, name),)
        return token[0]

    fetch(0)
    mirror(0)
    fetch(1)
    build(0)
    products(0)
    reduce_first(0)
    mirror(1)
    build(1)
    products(1)
    reduce_first(1)
    reduce_second(0)
    fetch(2)
    reduce_second(1)
    gather_first(0)
    gather_first(1)
    arrived(2)
    mirror(2)
    gather_second(0)
    build(2)
    products(2)
    fetch(3)
    gather_second(1)
    join(0)
    reduce_first(2)
    arrived(3)
    mirror(3)
    build(3)
    products(3)
    share(0)
    if not aligned:
        share_sum(0)
    join(1)
    reduce_first(3)
    share(1)
    share_sum(1)
    up_partial = early(("in", "delta"), True, "up_grad_early")
    reduce_second(2)
    reduce_second(3)
    gather_first(2)
    gather_first(3)
    gather_second(2)
    down_partial = early(("active", "cot"), False, "down_grad_early")
    settle()
    gather_second(3)
    join(2)
    share(2)
    share_sum(2)
    join(3)
    share(3)
    up_grad = late(("in", "delta"), up_partial, True, "up_grad")
    share_sum(3)
    down_grad = late(("active", "cot"), down_partial, False, "down_grad")

    def end_kernel(*arrays):
        tile = tile_of(width, 768)

        def body(own_ref, *refs):
            total = add_shares(*refs[:-1]).astype(b16)
            for i in range(n_col):
                target = pl.multiple_of((own_ref[0] ^ x_outer[i]) * quarter, quarter)
                refs[-1][pl.ds(target, quarter), :] = total[i * quarter : (i + 1) * quarter]

        blocks_of = [pl.BlockSpec((a.shape[0], tile), lambda i: (0, i)) for a in arrays]
        return call(
            body,
            [own.astype(jnp.int32).reshape(1), *arrays],
            [pl.BlockSpec(memory_space=pltpu.SMEM)] + blocks_of,
            shape((rows, width), b16),
            blocks_of[0],
            (width // tile,),
            "end",
        )

    if aligned:
        return (end_kernel(work[0]["part"], *work[0]["part_came"], running), up_grad, down_grad)
    input_grad = work[0]["part"] + running.astype(f32)
    input_grad = input_grad.astype(b16).reshape(2, 2, quarter, width).transpose(1, 0, 2, 3).reshape(rows, width)
    return (reorder(input_grad, y_outer), up_grad, down_grad)


def solution(mesh):
    tokens = P(("dp", "row"), "col")
    up, down = P("col", ("dp", "row")), P(("dp", "row"), "col")
    return jax.shard_map(
        shards,
        mesh=mesh,
        in_specs=(tokens, up, down, tokens),
        out_specs=(tokens, up, down),
        check_vma=False,
    )
```

```python
import math

import jax
import jax.numpy as jnp
from jax import lax
from jax.experimental import pallas as pl
from jax.experimental.pallas import tpu as pltpu
from jax.sharding import PartitionSpec as P

gelu_const = math.sqrt(2.0 / math.pi)
f32, b16 = jnp.float32, jnp.bfloat16
FIRST_SUM, ODD_JOIN = 14_000_000_000, 12_000_000_000


def gelu_both(value):
    square = value * value
    tangent = jnp.tanh(gelu_const * (value + 0.044715 * square * value))
    half = 0.5 * (1.0 + tangent)
    slope = half + 0.5 * value * (1.0 - tangent * tangent) * gelu_const * (1.0 + 3.0 * 0.044715 * square)
    return value * half, slope


def contract(left, right, at_left, at_right):
    return lax.dot_general(
        left, right, (((at_left,), (at_right,)), ((), ())), preferred_element_type=f32
    )


def call(body, operands, in_specs, outs, out_specs, grid, name, limit=4 * 2**20, flops=1000, scratch=()):
    return pl.pallas_call(
        body,
        grid=grid,
        in_specs=in_specs,
        out_specs=out_specs,
        out_shape=outs,
        scratch_shapes=list(scratch),
        compiler_params=pltpu.CompilerParams(vmem_limit_bytes=limit),
        cost_estimate=pl.CostEstimate(flops=flops, bytes_accessed=1000, transcendentals=0),
        name=name,
    )(*operands)


def shape(dims, dtype):
    return jax.ShapeDtypeStruct(dims, dtype)


def tile_of(size, most):
    return max(t for t in range(128, most + 1, 128) if size % t == 0)


whole = pl.BlockSpec(memory_space=pltpu.VMEM)


def cut_of(hidden):
    return hidden // 256 * 128


def first_product(chunk, weight, weight_dim, cut, name):
    tokens = chunk.shape[0]
    hidden = weight.shape[1 - weight_dim]
    half, quarter = tokens // 2, tokens // 4
    widths = [cut] + [hidden - cut] * (cut < hidden)

    def body(chunk_ref, weight_ref, kept_ref, *sent_refs):
        for start in range(0, hidden, tile_of(hidden, 512) if cut == hidden else 128 if cut % 512 else 512):
            tile = min(hidden, start + (tile_of(hidden, 512) if cut == hidden else 128 if cut % 512 else 512)) - start
            span = pl.ds(start, tile)
            block = weight_ref[:, span] if weight_dim == 0 else weight_ref[span, :]
            total = contract(chunk_ref[...], block, 1, weight_dim)
            if start < cut:
                kept, sent = total[:half], total[half:]
            else:
                q = [total[i * quarter : (i + 1) * quarter] for i in range(4)]
                kept, sent = jnp.concatenate([q[0], q[2]], axis=0), jnp.concatenate([q[1], q[3]], axis=0)
            kept_ref[:, span] = kept
            sent_refs[start >= cut][:, pl.ds(start - cut * (start >= cut), tile)] = sent.astype(b16)

    return call(
        body,
        [chunk, weight],
        [whole] * 2,
        [shape((half, hidden), f32)] + [shape((half, w), b16) for w in widths],
        [whole] * (1 + len(widths)),
        (),
        name,
    )


def add_halves(kept_h, came_h, kept_g, came_g, flops):
    tokens, hidden = kept_h.shape
    half = tokens // 2
    tile = tile_of(hidden, 768)

    def body(kh, ch, kg, cg, sent_h, next_h, sent_g, next_g):
        for kept, came, sent, rest in ((kh, ch, sent_h, next_h), (kg, cg, sent_g, next_g)):
            total = kept[...] + came[...].astype(f32)
            rest[...] = total[:half]
            sent[...] = total[half:].astype(b16)

    block = pl.BlockSpec((tokens, tile), lambda i: (0, i))
    part = pl.BlockSpec((half, tile), lambda i: (0, i))
    return call(
        body,
        [kept_h, came_h, kept_g, came_g],
        [block] * 4,
        [shape((half, hidden), b16), shape((half, hidden), f32)] * 2,
        [part] * 4,
        (hidden // tile,),
        "add_halves",
        flops=flops,
    )


def add_crossed(kept_h, came_h, kept_g, came_g, cut, flops):
    tokens, hidden = kept_h.shape
    half = tokens // 2

    def body(kh, h0, h1, kg, g0, g1, sent_hg, next_h, sent_gh, next_g):
        for kept, came, rest, sents in ((kh, (h0, h1), next_h, (sent_hg, sent_gh)), (kg, (g0, g1), next_g, (sent_gh, sent_hg))):
            for side in range(2):
                span = pl.ds(cut * side, (cut, hidden - cut)[side])
                total = kept[:, span] + came[side][...].astype(f32)
                rest[:, span] = total[:half]
                sents[side][:, span] = total[half:].astype(b16)

    return call(
        body,
        [kept_h, *came_h, kept_g, *came_g],
        [whole] * 6,
        [shape((half, hidden), b16), shape((half, hidden), f32)] * 2,
        [whole] * 4,
        (),
        "add_crossed",
        flops=flops,
    )


def activate(kept_h, came_h, kept_g, came_g, cut):
    tokens, hidden = kept_h.shape
    tile = tile_of(cut, 768) if hidden % cut == 0 else 128

    def body(kh, ch, kg, cg, active_ref, delta_ref):
        came_h, came_g = ch[...].astype(f32), cg[...].astype(f32)
        if cut < hidden:
            straight = pl.program_id(0) < cut // tile
            came_h, came_g = jnp.where(straight, came_h, came_g), jnp.where(straight, came_g, came_h)
        value, slope = gelu_both(kh[...] + came_h)
        active_ref[...] = value.astype(b16)
        delta_ref[...] = ((kg[...] + came_g) * slope).astype(b16)

    block = pl.BlockSpec((tokens, tile), lambda i: (0, i))
    return call(
        body, [kept_h, came_h, kept_g, came_g], [block] * 4, [shape((tokens, hidden), b16)] * 2, [block] * 2,
        (hidden // tile,), "activate",
    )


def join_pairs(flops, *arrays):
    rows, columns = arrays[0].shape
    tile = tile_of(columns, 1536)

    def body(*refs):
        for i, out in enumerate(refs[len(arrays):]):
            out[pl.ds(0, rows), :] = refs[2 * i][...]
            out[pl.ds(rows, rows), :] = refs[2 * i + 1][...]

    return call(
        body,
        arrays,
        [pl.BlockSpec((rows, tile), lambda i: (0, i))] * len(arrays),
        [shape((2 * rows, columns), arrays[0].dtype)] * (len(arrays) // 2),
        [pl.BlockSpec((2 * rows, tile), lambda i: (0, i))] * (len(arrays) // 2),
        (columns // tile,),
        "join_pairs",
        7 * 2**20,
        flops,
    )


def input_product(delta, up_weight, quarter, cuts):
    tokens = delta.shape[0]
    width = up_weight.shape[0]
    tile = tile_of(width, 512)
    pairs = tokens // (2 * quarter)

    def body(delta_ref, weight_ref, kept_ref, *sent_refs):
        for start in range(0, width, tile):
            span = pl.ds(start, tile)
            total = contract(delta_ref[...], weight_ref[span, :], 1, 1)
            for i in range(pairs):
                first, second = 2 * i * quarter, (2 * i + 1) * quarter
                kept_ref[pl.ds(i * quarter, quarter), span] = total[first:second]
                sent_ref = sent_refs[cuts * i // pairs]
                sent_ref[pl.ds(i % (pairs // cuts) * quarter, quarter), span] = total[second : second + quarter]

    outs = [shape((tokens // 2, width), f32)] + [shape((tokens // (2 * cuts), width), f32)] * cuts
    return call(body, [delta, up_weight], [whole] * 2, outs, [whole] * (1 + cuts), (), "input_product")


def add_shares(kept_ref, *rest):
    total, cut = kept_ref[...], kept_ref.shape[0] // 2
    while rest:
        if rest[0].shape[0] == cut:
            total = total + jnp.concatenate([rest[0][...], rest[1][...]], axis=0)
            rest = rest[2:]
        else:
            total = total + rest[0][...].astype(f32)
            rest = rest[1:]
    return total


def steps_of(*sizes):
    return max(n for n in range(1, 7) if all(size % (128 * n) == 0 for size in sizes))


def weight_total(lefts, rights, columns):
    total = contract(lefts[0][:, columns], rights[0][...], 0, 0)
    for left, right in zip(lefts[1:], rights[1:]):
        total = total + contract(left[:, columns], right[...], 0, 0)
    return total


def early_grad(lefts, rights, held, name):
    rows, columns = lefts[0].shape[1], rights[0].shape[1]
    steps = steps_of(rows)
    tile = rows // steps
    count = len(lefts)

    def body(*refs):
        mine = pl.ds(pl.multiple_of(pl.program_id(0) * tile, tile), tile)
        total = weight_total(refs[:count], refs[count:-1], mine)
        if held:
            refs[-1][mine, :] = total
        else:
            refs[-1][...] = total

    return call(
        body,
        [*lefts, *rights],
        [whole] * (2 * count),
        shape((rows, columns), f32) if held else pltpu.HBM((rows, columns), f32),
        whole if held else pl.BlockSpec((tile, columns), lambda i: (i, 0)),
        (steps,),
        name,
        10 * 2**20,
    )


def late_grad(lefts, rights, partial, held, scale, name):
    rows, columns = partial.shape
    steps = steps_of(rows)
    tile = rows // steps
    count = len(lefts)

    def body(*refs):
        mine = pl.ds(pl.multiple_of(pl.program_id(0) * tile, tile), tile)
        total = weight_total(refs[:count], refs[count : 2 * count], mine)
        total = total + (refs[-2][mine, :] if held else refs[-2][...])
        refs[-1][...] = (total * scale).astype(b16)

    block = pl.BlockSpec((tile, columns), lambda i: (i, 0))
    return call(
        body,
        [*lefts, *rights, partial],
        [whole] * (2 * count) + [whole if held else block],
        pltpu.HBM((rows, columns), b16),
        block,
        (steps,),
        name,
        8 * 2**20,
    )


def shards(inputs, up_weight, down_weight, cotangent):
    n_row = lax.axis_size("row")
    replicas = lax.axis_size("dp")
    n_col = lax.axis_size("col")
    assert replicas == 2 and n_col == 4 and n_row % 4 == 0
    rows, width = inputs.shape
    quarter = rows // n_col
    own = lax.axis_index("col")

    def swap_x(a):
        return lax.ppermute(a, "col", [(i, i ^ 1) for i in range(n_col)])

    def swap_y(a):
        return lax.ppermute(a, "col", [(i, i ^ 2) for i in range(n_col)])

    def swap_dp(a):
        return lax.ppermute(a, "dp", [(0, 1), (1, 0)])

    def pass_row(a):
        return lax.ppermute(a, "row", [(i, (i + 1) % n_row) for i in range(n_row)])

    def reorder(a, order):
        blocks = [lax.dynamic_slice_in_dim(a, (own ^ bits) * quarter, quarter, 0) for bits in order]
        return jnp.concatenate(blocks, axis=0)

    x_outer, y_outer = (0, 2, 1, 3), (0, 1, 2, 3)

    def reorder_both():
        def body(own_ref, inputs_ref, cotangent_ref, out_ref, done):
            copies = []
            for ref, order, base in ((inputs_ref, x_outer, 0), (cotangent_ref, y_outer, rows)):
                for i in range(n_col):
                    source = pl.multiple_of((own_ref[0] ^ order[i]) * quarter, quarter)
                    copies.append(
                        pltpu.make_async_copy(
                            ref.at[pl.ds(source, quarter), :],
                            out_ref.at[pl.ds(base + i * quarter, quarter), :],
                            done.at[len(copies)],
                        )
                    )
            for copy in copies:
                copy.start()
            for copy in copies:
                copy.wait()

        return call(
            body,
            [own.astype(jnp.int32).reshape(1)]
            + [pltpu.with_memory_space_constraint(a, pltpu.HBM) for a in (inputs, cotangent)],
            [pl.BlockSpec(memory_space=pltpu.SMEM)] + [pl.BlockSpec(memory_space=pltpu.HBM)] * 2,
            shape((2 * rows, width), b16),
            whole,
            (),
            "reorder",
            scratch=[pltpu.SemaphoreType.DMA((2 * n_col,))],
        )

    if quarter % 16 == 0:
        moving = reorder_both()
    else:
        moving = jnp.concatenate([reorder(inputs, x_outer), reorder(cotangent, y_outer)], axis=0)

    group = n_row // 4
    tall = group * rows
    work = [{} for _ in range(4)]
    blocks = {0: [moving]}
    aligned = group == 1 and quarter % 16 == 0

    token = ()

    def after(*values):
        tied = lax.optimization_barrier((*values, *token))[: len(values)]
        return tied if len(values) > 1 else tied[0]

    def fetch(at):
        if at > 0:
            sent = blocks[at - 1][-1]
            if at > 2:
                sent = after(sent, *work[at - 1]["other"])[0]
            blocks[at] = [pass_row(sent)]
        while len(blocks[at]) < group:
            blocks[at].append(pass_row(blocks[at][-1]))

    def mirror(at):
        w = work[at]
        if at == 1:
            blocks[at][-1], *work[0]["h_came"] = after(blocks[at][-1], *work[0]["h_came"])
        elif at > 1:
            blocks[at][-1] = after(blocks[at][-1])
        w["mine"] = blocks[at][0] if group == 1 else jnp.concatenate(blocks[at])
        eighth = w["mine"].shape[0] // (2 * n_col)
        bounds = [0, *((), (3, 6), (4,), (4,))[at], 2 * n_col]
        w["other"] = [swap_dp(w["mine"][i * eighth : j * eighth]) for i, j in zip(bounds[:-1], bounds[1:])]

    def arrived(at):
        nonlocal token
        token = (*token, blocks[at][-1])

    def build_kernel(mine, *others):
        def body(mine_ref, *refs):
            pieces = [(ref, k) for ref in refs[:-2] for k in range(ref.shape[0] // quarter)]
            for part, out in enumerate(refs[-2:]):
                for i in range(n_col):
                    ref, k = pieces[part * n_col + i]
                    out[pl.ds(2 * i * quarter, quarter), :] = mine_ref[pl.ds(part * rows + i * quarter, quarter), :]
                    out[pl.ds((2 * i + 1) * quarter, quarter), :] = ref[pl.ds(k * quarter, quarter), :]

        return call(
            body, [mine, *others], [whole] * (1 + len(others)), [shape((2 * rows, width), b16)] * 2, [whole] * 2, (), "build"
        )

    def build(at):
        nonlocal token
        w = work[at]
        mine, *others = after(w["mine"], *w["other"])
        if aligned:
            w["in"], w["cot"] = build_kernel(mine, *others)
        else:
            other = jnp.concatenate(others)
            pair = [a.reshape(group, 2 * n_col, quarter, width).transpose(1, 0, 2, 3) for a in (mine, other)]
            w["in"], w["cot"] = jnp.stack(pair, axis=2).reshape(2, 2 * tall, width)
        token = (w["in"], w["cot"])

    hidden_of = up_weight.shape[1]
    cuts = [cut_of(hidden_of), hidden_of, hidden_of, hidden_of]

    def products(at):
        nonlocal token
        w = work[at]
        w["h"], *w["h_out"] = token = first_product(after(w["in"]), up_weight, 0, cuts[at], "hidden_product")
        w["g"], *w["g_out"] = token = first_product(after(w["cot"]), down_weight, 1, cuts[at], "delta_act_product")

    def reduce_first(at):
        w = work[at]
        if at == 0:
            w["h_came"] = [swap_x(w["h_out"][0]), swap_y(w["h_out"][1])]
            w["g_came"] = [swap_y(w["g_out"][0]), swap_x(w["g_out"][1])]
            return
        h_out, g_out = w["h_out"][0], w["g_out"][0]
        if at > 1:
            h_out, g_out = after(h_out, g_out)
        w["h_came"], w["g_came"] = swap_x(h_out), swap_y(g_out)

    def reduce_second(at):
        nonlocal token
        w = work[at]
        if at == 0:
            h, h0, h1, g, g0, g1 = after(w["h"], *w["h_came"], w["g"], *w["g_came"])
            sent_h, w["h"], sent_g, w["g"] = token = add_crossed(h, (h0, h1), g, (g0, g1), cuts[0], FIRST_SUM)
        else:
            sent_h, w["h"], sent_g, w["g"] = token = add_halves(*after(w["h"], w["h_came"], w["g"], w["g_came"]), 1000)
        w["h_came"], w["g_came"] = swap_y(sent_h), swap_x(sent_g)

    def gather_first(at):
        nonlocal token
        w = work[at]
        w["active"], w["delta"] = token = activate(*after(w["h"], w["h_came"], w["g"], w["g_came"]), cuts[at])
        w["delta_came"], w["active_came"] = swap_y(w["delta"]), swap_x(w["active"])

    def join(at, flops=1000):
        nonlocal token
        w = work[at]
        w["delta"], w["active"] = token = join_pairs(
            flops, *after(w["delta"], w["delta_came"], w["active"], w["active_came"])
        )

    def gather_second(at):
        w = work[at]
        join(at, ODD_JOIN if at % 2 else 1000)
        w["delta_came"], w["active_came"] = swap_x(w["delta"]), swap_y(w["active"])

    def add_kernel(dtype, *arrays):
        tile = tile_of(width, 768)

        def body(*refs):
            refs[-1][...] = add_shares(*refs[:-1]).astype(dtype)

        blocks_of = [pl.BlockSpec((a.shape[0], tile), lambda i: (0, i)) for a in arrays]
        return call(body, arrays, blocks_of, shape((rows, width), dtype), blocks_of[0], (width // tile,), "add")

    def share(at):
        nonlocal token
        w = work[at]
        delta = after(w["delta"])
        if not aligned:
            parts = contract(delta, up_weight, 1, 1).reshape(n_col, group, 2, quarter, width)
            token = (parts,)
            w["part"], w["part_came"] = parts[:, :, 0], swap_dp(parts[:, :, 1])
        else:
            w["part"], *sent = token = input_product(delta, up_weight, quarter, 1 if at < 2 else 2)
            w["part_came"] = [swap_dp(part) for part in sent]

    running = None

    def share_sum(at):
        nonlocal token, running
        w = work[at]
        if not aligned:
            part = w["part"] + w["part_came"]
            for step in range(at * group, (at + 1) * group):
                one = part[:, step - at * group].reshape(rows, width)
                if step == 0:
                    w["part"] = one
                else:
                    running = pass_row(one if running is None else running + one)
        elif at == 1:
            running = pass_row(add_kernel(f32, w["part"], *w["part_came"]))
        else:
            total = add_kernel(b16 if at == 3 else f32, *after(w["part"], *w["part_came"], running))
            token = (total,)
            running = pass_row(total)

    def settle():
        nonlocal token
        token = (*token, running)

    def early(names, held, name):
        nonlocal token
        values = after(*(work[at][k] for k in names for at in (0, 1)))
        token = (early_grad(values[:2], values[2:], held, name),)
        return token[0]

    def late(names, partial, held, name):
        nonlocal token
        values = after(*(work[at][k] for k in names for at in (2, 3)))
        token = (late_grad(values[:2], values[2:], partial, held, 1.0 / replicas, name),)
        return token[0]

    fetch(0)
    mirror(0)
    fetch(1)
    build(0)
    products(0)
    reduce_first(0)
    mirror(1)
    build(1)
    products(1)
    reduce_first(1)
    reduce_second(0)
    fetch(2)
    reduce_second(1)
    gather_first(0)
    gather_first(1)
    arrived(2)
    mirror(2)
    gather_second(0)
    build(2)
    products(2)
    fetch(3)
    gather_second(1)
    join(0)
    reduce_first(2)
    arrived(3)
    mirror(3)
    build(3)
    products(3)
    share(0)
    if not aligned:
        share_sum(0)
    join(1)
    reduce_first(3)
    share(1)
    share_sum(1)
    up_partial = early(("in", "delta"), True, "up_grad_early")
    reduce_second(2)
    reduce_second(3)
    gather_first(2)
    gather_first(3)
    gather_second(2)
    down_partial = early(("active", "cot"), False, "down_grad_early")
    settle()
    gather_second(3)
    join(2)
    share(2)
    share_sum(2)
    join(3)
    share(3)
    up_grad = late(("in", "delta"), up_partial, True, "up_grad")
    share_sum(3)
    down_grad = late(("active", "cot"), down_partial, False, "down_grad")

    def end_kernel(*arrays):
        tile = tile_of(width, 768)

        def body(own_ref, *refs):
            total = add_shares(*refs[:-1]).astype(b16)
            for i in range(n_col):
                target = pl.multiple_of((own_ref[0] ^ x_outer[i]) * quarter, quarter)
                refs[-1][pl.ds(target, quarter), :] = total[i * quarter : (i + 1) * quarter]

        blocks_of = [pl.BlockSpec((a.shape[0], tile), lambda i: (0, i)) for a in arrays]
        return call(
            body,
            [own.astype(jnp.int32).reshape(1), *arrays],
            [pl.BlockSpec(memory_space=pltpu.SMEM)] + blocks_of,
            shape((rows, width), b16),
            blocks_of[0],
            (width // tile,),
            "end",
        )

    if aligned:
        return (end_kernel(work[0]["part"], *work[0]["part_came"], running), up_grad, down_grad)
    input_grad = work[0]["part"] + running.astype(f32)
    input_grad = input_grad.astype(b16).reshape(2, 2, quarter, width).transpose(1, 0, 2, 3).reshape(rows, width)
    return (reorder(input_grad, y_outer), up_grad, down_grad)


def solution(mesh):
    tokens = P(("dp", "row"), "col")
    up, down = P("col", ("dp", "row")), P(("dp", "row"), "col")
    return jax.shard_map(
        shards,
        mesh=mesh,
        in_specs=(tokens, up, down, tokens),
        out_specs=(tokens, up, down),
        check_vma=False,
    )
```

```python
import math

import jax
import jax.numpy as jnp
from jax import lax
from jax.experimental import pallas as pl
from jax.experimental.pallas import tpu as pltpu
from jax.sharding import PartitionSpec as P

gelu_const = math.sqrt(2.0 / math.pi)
f32, b16 = jnp.float32, jnp.bfloat16
FIRST_SUM, ODD_JOIN = 14_000_000_000, 12_000_000_000


def gelu_both(value):
    square = value * value
    tangent = jnp.tanh(gelu_const * (value + 0.044715 * square * value))
    half = 0.5 * (1.0 + tangent)
    slope = half + 0.5 * value * (1.0 - tangent * tangent) * gelu_const * (1.0 + 3.0 * 0.044715 * square)
    return value * half, slope


def contract(left, right, at_left, at_right):
    return lax.dot_general(
        left, right, (((at_left,), (at_right,)), ((), ())), preferred_element_type=f32
    )


def call(body, operands, in_specs, outs, out_specs, grid, name, limit=4 * 2**20, flops=1000, scratch=()):
    return pl.pallas_call(
        body,
        grid=grid,
        in_specs=in_specs,
        out_specs=out_specs,
        out_shape=outs,
        scratch_shapes=list(scratch),
        compiler_params=pltpu.CompilerParams(vmem_limit_bytes=limit),
        cost_estimate=pl.CostEstimate(flops=flops, bytes_accessed=1000, transcendentals=0),
        name=name,
    )(*operands)


def shape(dims, dtype):
    return jax.ShapeDtypeStruct(dims, dtype)


def tile_of(size, most):
    return max(t for t in range(128, most + 1, 128) if size % t == 0)


whole = pl.BlockSpec(memory_space=pltpu.VMEM)


def cut_of(hidden):
    return hidden // 256 * 128


def first_product(chunk, weight, weight_dim, cut, name):
    tokens = chunk.shape[0]
    hidden = weight.shape[1 - weight_dim]
    half, quarter = tokens // 2, tokens // 4
    widths = [cut] + [hidden - cut] * (cut < hidden)

    def body(chunk_ref, weight_ref, kept_ref, *sent_refs):
        for start in range(0, hidden, tile_of(hidden, 512) if cut == hidden else 128 if cut % 512 else 512):
            tile = min(hidden, start + (tile_of(hidden, 512) if cut == hidden else 128 if cut % 512 else 512)) - start
            span = pl.ds(start, tile)
            block = weight_ref[:, span] if weight_dim == 0 else weight_ref[span, :]
            total = contract(chunk_ref[...], block, 1, weight_dim)
            if start < cut:
                kept, sent = total[:half], total[half:]
            else:
                q = [total[i * quarter : (i + 1) * quarter] for i in range(4)]
                kept, sent = jnp.concatenate([q[0], q[2]], axis=0), jnp.concatenate([q[1], q[3]], axis=0)
            kept_ref[:, span] = kept
            sent_refs[start >= cut][:, pl.ds(start - cut * (start >= cut), tile)] = sent.astype(b16)

    return call(
        body,
        [chunk, weight],
        [whole] * 2,
        [shape((half, hidden), f32)] + [shape((half, w), b16) for w in widths],
        [whole] * (1 + len(widths)),
        (),
        name,
    )


def add_halves(kept_h, came_h, kept_g, came_g, flops):
    tokens, hidden = kept_h.shape
    half = tokens // 2
    tile = tile_of(hidden, 768)

    def body(kh, ch, kg, cg, sent_h, next_h, sent_g, next_g):
        for kept, came, sent, rest in ((kh, ch, sent_h, next_h), (kg, cg, sent_g, next_g)):
            total = kept[...] + came[...].astype(f32)
            rest[...] = total[:half]
            sent[...] = total[half:].astype(b16)

    block = pl.BlockSpec((tokens, tile), lambda i: (0, i))
    part = pl.BlockSpec((half, tile), lambda i: (0, i))
    return call(
        body,
        [kept_h, came_h, kept_g, came_g],
        [block] * 4,
        [shape((half, hidden), b16), shape((half, hidden), f32)] * 2,
        [part] * 4,
        (hidden // tile,),
        "add_halves",
        flops=flops,
    )


def add_crossed(kept_h, came_h, kept_g, came_g, cut, flops):
    tokens, hidden = kept_h.shape
    half = tokens // 2

    def body(kh, h0, h1, kg, g0, g1, sent_hg, next_h, sent_gh, next_g):
        for kept, came, rest, sents in ((kh, (h0, h1), next_h, (sent_hg, sent_gh)), (kg, (g0, g1), next_g, (sent_gh, sent_hg))):
            for side in range(2):
                span = pl.ds(cut * side, (cut, hidden - cut)[side])
                total = kept[:, span] + came[side][...].astype(f32)
                rest[:, span] = total[:half]
                sents[side][:, span] = total[half:].astype(b16)

    return call(
        body,
        [kept_h, *came_h, kept_g, *came_g],
        [whole] * 6,
        [shape((half, hidden), b16), shape((half, hidden), f32)] * 2,
        [whole] * 4,
        (),
        "add_crossed",
        flops=flops,
    )


def activate(kept_h, came_h, kept_g, came_g, cut):
    tokens, hidden = kept_h.shape
    tile = tile_of(cut, 768) if hidden % cut == 0 else 128

    def body(kh, ch, kg, cg, active_ref, delta_ref):
        came_h, came_g = ch[...].astype(f32), cg[...].astype(f32)
        if cut < hidden:
            straight = pl.program_id(0) < cut // tile
            came_h, came_g = jnp.where(straight, came_h, came_g), jnp.where(straight, came_g, came_h)
        value, slope = gelu_both(kh[...] + came_h)
        active_ref[...] = value.astype(b16)
        delta_ref[...] = ((kg[...] + came_g) * slope).astype(b16)

    block = pl.BlockSpec((tokens, tile), lambda i: (0, i))
    return call(
        body, [kept_h, came_h, kept_g, came_g], [block] * 4, [shape((tokens, hidden), b16)] * 2, [block] * 2,
        (hidden // tile,), "activate",
    )


def join_pairs(flops, *arrays):
    rows, columns = arrays[0].shape
    tile = tile_of(columns, 1536)

    def body(*refs):
        for i, out in enumerate(refs[len(arrays):]):
            out[pl.ds(0, rows), :] = refs[2 * i][...]
            out[pl.ds(rows, rows), :] = refs[2 * i + 1][...]

    return call(
        body,
        arrays,
        [pl.BlockSpec((rows, tile), lambda i: (0, i))] * len(arrays),
        [shape((2 * rows, columns), arrays[0].dtype)] * (len(arrays) // 2),
        [pl.BlockSpec((2 * rows, tile), lambda i: (0, i))] * (len(arrays) // 2),
        (columns // tile,),
        "join_pairs",
        7 * 2**20,
        flops,
    )


def input_product(delta, up_weight, quarter, cuts):
    tokens = delta.shape[0]
    width = up_weight.shape[0]
    tile = tile_of(width, 512)
    pairs = tokens // (2 * quarter)

    def body(delta_ref, weight_ref, kept_ref, *sent_refs):
        for start in range(0, width, tile):
            span = pl.ds(start, tile)
            total = contract(delta_ref[...], weight_ref[span, :], 1, 1)
            for i in range(pairs):
                first, second = 2 * i * quarter, (2 * i + 1) * quarter
                kept_ref[pl.ds(i * quarter, quarter), span] = total[first:second]
                sent_ref = sent_refs[cuts * i // pairs]
                sent_ref[pl.ds(i % (pairs // cuts) * quarter, quarter), span] = total[second : second + quarter]

    outs = [shape((tokens // 2, width), f32)] + [shape((tokens // (2 * cuts), width), f32)] * cuts
    return call(body, [delta, up_weight], [whole] * 2, outs, [whole] * (1 + cuts), (), "input_product")


def add_shares(kept_ref, *rest):
    total, cut = kept_ref[...], kept_ref.shape[0] // 2
    while rest:
        if rest[0].shape[0] == cut:
            total = total + jnp.concatenate([rest[0][...], rest[1][...]], axis=0)
            rest = rest[2:]
        else:
            total = total + rest[0][...].astype(f32)
            rest = rest[1:]
    return total


def steps_of(*sizes):
    return max(n for n in range(1, 7) if all(size % (128 * n) == 0 for size in sizes))


def weight_total(lefts, rights, columns):
    total = contract(lefts[0][:, columns], rights[0][...], 0, 0)
    for left, right in zip(lefts[1:], rights[1:]):
        total = total + contract(left[:, columns], right[...], 0, 0)
    return total


def early_grad(lefts, rights, held, name):
    rows, columns = lefts[0].shape[1], rights[0].shape[1]
    steps = steps_of(rows)
    tile = rows // steps
    count = len(lefts)

    def body(*refs):
        mine = pl.ds(pl.multiple_of(pl.program_id(0) * tile, tile), tile)
        total = weight_total(refs[:count], refs[count:-1], mine)
        if held:
            refs[-1][mine, :] = total
        else:
            refs[-1][...] = total

    return call(
        body,
        [*lefts, *rights],
        [whole] * (2 * count),
        shape((rows, columns), f32) if held else pltpu.HBM((rows, columns), f32),
        whole if held else pl.BlockSpec((tile, columns), lambda i: (i, 0)),
        (steps,),
        name,
        10 * 2**20,
    )


def late_grad(lefts, rights, partial, held, scale, name):
    rows, columns = partial.shape
    steps = steps_of(rows)
    tile = rows // steps
    count = len(lefts)

    def body(*refs):
        mine = pl.ds(pl.multiple_of(pl.program_id(0) * tile, tile), tile)
        total = weight_total(refs[:count], refs[count : 2 * count], mine)
        total = total + (refs[-2][mine, :] if held else refs[-2][...])
        refs[-1][...] = (total * scale).astype(b16)

    block = pl.BlockSpec((tile, columns), lambda i: (i, 0))
    return call(
        body,
        [*lefts, *rights, partial],
        [whole] * (2 * count) + [whole if held else block],
        pltpu.HBM((rows, columns), b16),
        block,
        (steps,),
        name,
        8 * 2**20,
    )


def shards(inputs, up_weight, down_weight, cotangent):
    n_row = lax.axis_size("row")
    replicas = lax.axis_size("dp")
    n_col = lax.axis_size("col")
    assert replicas == 2 and n_col == 4 and n_row % 4 == 0
    rows, width = inputs.shape
    quarter = rows // n_col
    own = lax.axis_index("col")

    def swap_x(a):
        return lax.ppermute(a, "col", [(i, i ^ 1) for i in range(n_col)])

    def swap_y(a):
        return lax.ppermute(a, "col", [(i, i ^ 2) for i in range(n_col)])

    def swap_dp(a):
        return lax.ppermute(a, "dp", [(0, 1), (1, 0)])

    def pass_row(a):
        return lax.ppermute(a, "row", [(i, (i + 1) % n_row) for i in range(n_row)])

    def reorder(a, order):
        blocks = [lax.dynamic_slice_in_dim(a, (own ^ bits) * quarter, quarter, 0) for bits in order]
        return jnp.concatenate(blocks, axis=0)

    x_outer, y_outer = (0, 2, 1, 3), (0, 1, 2, 3)

    def reorder_both():
        def body(own_ref, inputs_ref, cotangent_ref, out_ref, done):
            copies = []
            for ref, order, base in ((inputs_ref, x_outer, 0), (cotangent_ref, y_outer, rows)):
                for i in range(n_col):
                    source = pl.multiple_of((own_ref[0] ^ order[i]) * quarter, quarter)
                    copies.append(
                        pltpu.make_async_copy(
                            ref.at[pl.ds(source, quarter), :],
                            out_ref.at[pl.ds(base + i * quarter, quarter), :],
                            done.at[len(copies)],
                        )
                    )
            for copy in copies:
                copy.start()
            for copy in copies:
                copy.wait()

        return call(
            body,
            [own.astype(jnp.int32).reshape(1)]
            + [pltpu.with_memory_space_constraint(a, pltpu.HBM) for a in (inputs, cotangent)],
            [pl.BlockSpec(memory_space=pltpu.SMEM)] + [pl.BlockSpec(memory_space=pltpu.HBM)] * 2,
            shape((2 * rows, width), b16),
            whole,
            (),
            "reorder",
            scratch=[pltpu.SemaphoreType.DMA((2 * n_col,))],
        )

    if quarter % 16 == 0:
        moving = reorder_both()
    else:
        moving = jnp.concatenate([reorder(inputs, x_outer), reorder(cotangent, y_outer)], axis=0)

    group = n_row // 4
    tall = group * rows
    work = [{} for _ in range(4)]
    blocks = {0: [moving]}
    aligned = group == 1 and quarter % 16 == 0

    token = ()

    def after(*values):
        tied = lax.optimization_barrier((*values, *token))[: len(values)]
        return tied if len(values) > 1 else tied[0]

    def fetch(at):
        if at > 0:
            sent = blocks[at - 1][-1]
            if at > 1:
                sent = after(sent, *work[at - 1]["other"])[0]
            blocks[at] = [pass_row(sent)]
        while len(blocks[at]) < group:
            blocks[at].append(pass_row(blocks[at][-1]))

    def mirror(at):
        w = work[at]
        if at == 1:
            blocks[at][-1], *work[0]["h_came"] = after(blocks[at][-1], *work[0]["h_came"])
        elif at > 1:
            blocks[at][-1] = after(blocks[at][-1])
        w["mine"] = blocks[at][0] if group == 1 else jnp.concatenate(blocks[at])
        eighth = w["mine"].shape[0] // (2 * n_col)
        bounds = [0, *((), (3, 6), (4,), (4,))[at], 2 * n_col]
        w["other"] = [swap_dp(w["mine"][i * eighth : j * eighth]) for i, j in zip(bounds[:-1], bounds[1:])]

    def arrived(at):
        nonlocal token
        token = (*token, blocks[at][-1])

    def build_kernel(mine, *others):
        def body(mine_ref, *refs):
            pieces = [(ref, k) for ref in refs[:-2] for k in range(ref.shape[0] // quarter)]
            for part, out in enumerate(refs[-2:]):
                for i in range(n_col):
                    ref, k = pieces[part * n_col + i]
                    out[pl.ds(2 * i * quarter, quarter), :] = mine_ref[pl.ds(part * rows + i * quarter, quarter), :]
                    out[pl.ds((2 * i + 1) * quarter, quarter), :] = ref[pl.ds(k * quarter, quarter), :]

        return call(
            body, [mine, *others], [whole] * (1 + len(others)), [shape((2 * rows, width), b16)] * 2, [whole] * 2, (), "build"
        )

    def build(at):
        nonlocal token
        w = work[at]
        mine, *others = after(w["mine"], *w["other"])
        if aligned:
            w["in"], w["cot"] = build_kernel(mine, *others)
        else:
            other = jnp.concatenate(others)
            pair = [a.reshape(group, 2 * n_col, quarter, width).transpose(1, 0, 2, 3) for a in (mine, other)]
            w["in"], w["cot"] = jnp.stack(pair, axis=2).reshape(2, 2 * tall, width)
        token = (w["in"], w["cot"])

    hidden_of = up_weight.shape[1]
    cuts = [cut_of(hidden_of), hidden_of, hidden_of, hidden_of]

    def products(at):
        nonlocal token
        w = work[at]
        w["h"], *w["h_out"] = token = first_product(after(w["in"]), up_weight, 0, cuts[at], "hidden_product")
        w["g"], *w["g_out"] = token = first_product(after(w["cot"]), down_weight, 1, cuts[at], "delta_act_product")

    def reduce_first(at):
        w = work[at]
        if at == 0:
            w["h_came"] = [swap_x(w["h_out"][0]), swap_y(w["h_out"][1])]
            w["g_came"] = [swap_y(w["g_out"][0]), swap_x(w["g_out"][1])]
            return
        h_out, g_out = w["h_out"][0], w["g_out"][0]
        if at > 1:
            h_out, g_out = after(h_out, g_out)
        w["h_came"], w["g_came"] = swap_x(h_out), swap_y(g_out)

    def reduce_second(at):
        nonlocal token
        w = work[at]
        if at == 0:
            h, h0, h1, g, g0, g1 = after(w["h"], *w["h_came"], w["g"], *w["g_came"])
            sent_h, w["h"], sent_g, w["g"] = token = add_crossed(h, (h0, h1), g, (g0, g1), cuts[0], FIRST_SUM)
        else:
            sent_h, w["h"], sent_g, w["g"] = token = add_halves(*after(w["h"], w["h_came"], w["g"], w["g_came"]), 1000)
        w["h_came"], w["g_came"] = swap_y(sent_h), swap_x(sent_g)

    def gather_first(at):
        nonlocal token
        w = work[at]
        w["active"], w["delta"] = token = activate(*after(w["h"], w["h_came"], w["g"], w["g_came"]), cuts[at])
        w["delta_came"], w["active_came"] = swap_y(w["delta"]), swap_x(w["active"])

    def join(at, flops=1000):
        nonlocal token
        w = work[at]
        w["delta"], w["active"] = token = join_pairs(
            flops, *after(w["delta"], w["delta_came"], w["active"], w["active_came"])
        )

    def gather_second(at):
        w = work[at]
        join(at, ODD_JOIN if at % 2 else 1000)
        w["delta_came"], w["active_came"] = swap_x(w["delta"]), swap_y(w["active"])

    def add_kernel(dtype, *arrays):
        tile = tile_of(width, 768)

        def body(*refs):
            refs[-1][...] = add_shares(*refs[:-1]).astype(dtype)

        blocks_of = [pl.BlockSpec((a.shape[0], tile), lambda i: (0, i)) for a in arrays]
        return call(body, arrays, blocks_of, shape((rows, width), dtype), blocks_of[0], (width // tile,), "add")

    def share(at):
        nonlocal token
        w = work[at]
        delta = after(w["delta"])
        if not aligned:
            parts = contract(delta, up_weight, 1, 1).reshape(n_col, group, 2, quarter, width)
            token = (parts,)
            w["part"], w["part_came"] = parts[:, :, 0], swap_dp(parts[:, :, 1])
        else:
            w["part"], *sent = token = input_product(delta, up_weight, quarter, 1 if at < 2 else 2)
            w["part_came"] = [swap_dp(part) for part in sent]

    running = None

    def share_sum(at):
        nonlocal token, running
        w = work[at]
        if not aligned:
            part = w["part"] + w["part_came"]
            for step in range(at * group, (at + 1) * group):
                one = part[:, step - at * group].reshape(rows, width)
                if step == 0:
                    w["part"] = one
                else:
                    running = pass_row(one if running is None else running + one)
        elif at == 1:
            running = pass_row(add_kernel(f32, w["part"], *w["part_came"]))
        else:
            total = add_kernel(b16 if at == 3 else f32, *after(w["part"], *w["part_came"], running))
            token = (total,)
            running = pass_row(total)

    def settle():
        nonlocal token
        token = (*token, running)

    def early(names, held, name):
        nonlocal token
        values = after(*(work[at][k] for k in names for at in (0, 1)))
        token = (early_grad(values[:2], values[2:], held, name),)
        return token[0]

    def late(names, partial, held, name):
        nonlocal token
        values = after(*(work[at][k] for k in names for at in (2, 3)))
        token = (late_grad(values[:2], values[2:], partial, held, 1.0 / replicas, name),)
        return token[0]

    fetch(0)
    mirror(0)
    fetch(1)
    build(0)
    products(0)
    reduce_first(0)
    mirror(1)
    build(1)
    products(1)
    reduce_first(1)
    fetch(2)
    reduce_second(0)
    reduce_second(1)
    gather_first(0)
    gather_first(1)
    arrived(2)
    mirror(2)
    gather_second(0)
    build(2)
    products(2)
    fetch(3)
    gather_second(1)
    join(0)
    reduce_first(2)
    arrived(3)
    mirror(3)
    build(3)
    products(3)
    share(0)
    if not aligned:
        share_sum(0)
    join(1)
    reduce_first(3)
    share(1)
    share_sum(1)
    up_partial = early(("in", "delta"), True, "up_grad_early")
    reduce_second(2)
    reduce_second(3)
    gather_first(2)
    gather_first(3)
    gather_second(2)
    down_partial = early(("active", "cot"), False, "down_grad_early")
    settle()
    gather_second(3)
    join(2)
    share(2)
    share_sum(2)
    join(3)
    share(3)
    up_grad = late(("in", "delta"), up_partial, True, "up_grad")
    share_sum(3)
    down_grad = late(("active", "cot"), down_partial, False, "down_grad")

    def end_kernel(*arrays):
        tile = tile_of(width, 768)

        def body(own_ref, *refs):
            total = add_shares(*refs[:-1]).astype(b16)
            for i in range(n_col):
                target = pl.multiple_of((own_ref[0] ^ x_outer[i]) * quarter, quarter)
                refs[-1][pl.ds(target, quarter), :] = total[i * quarter : (i + 1) * quarter]

        blocks_of = [pl.BlockSpec((a.shape[0], tile), lambda i: (0, i)) for a in arrays]
        return call(
            body,
            [own.astype(jnp.int32).reshape(1), *arrays],
            [pl.BlockSpec(memory_space=pltpu.SMEM)] + blocks_of,
            shape((rows, width), b16),
            blocks_of[0],
            (width // tile,),
            "end",
        )

    if aligned:
        return (end_kernel(work[0]["part"], *work[0]["part_came"], running), up_grad, down_grad)
    input_grad = work[0]["part"] + running.astype(f32)
    input_grad = input_grad.astype(b16).reshape(2, 2, quarter, width).transpose(1, 0, 2, 3).reshape(rows, width)
    return (reorder(input_grad, y_outer), up_grad, down_grad)


def solution(mesh):
    tokens = P(("dp", "row"), "col")
    up, down = P("col", ("dp", "row")), P(("dp", "row"), "col")
    return jax.shard_map(
        shards,
        mesh=mesh,
        in_specs=(tokens, up, down, tokens),
        out_specs=(tokens, up, down),
        check_vma=False,
    )
```

```python
import math

import jax
import jax.numpy as jnp
from jax import lax
from jax.experimental import pallas as pl
from jax.experimental.pallas import tpu as pltpu
from jax.sharding import PartitionSpec as P

gelu_const = math.sqrt(2.0 / math.pi)
f32, b16 = jnp.float32, jnp.bfloat16
FIRST_SUM, ODD_JOIN = 14_000_000_000, 12_000_000_000


def gelu_both(value):
    square = value * value
    tangent = jnp.tanh(gelu_const * (value + 0.044715 * square * value))
    half = 0.5 * (1.0 + tangent)
    slope = half + 0.5 * value * (1.0 - tangent * tangent) * gelu_const * (1.0 + 3.0 * 0.044715 * square)
    return value * half, slope


def contract(left, right, at_left, at_right):
    return lax.dot_general(
        left, right, (((at_left,), (at_right,)), ((), ())), preferred_element_type=f32
    )


def call(body, operands, in_specs, outs, out_specs, grid, name, limit=4 * 2**20, flops=1000, scratch=()):
    return pl.pallas_call(
        body,
        grid=grid,
        in_specs=in_specs,
        out_specs=out_specs,
        out_shape=outs,
        scratch_shapes=list(scratch),
        compiler_params=pltpu.CompilerParams(vmem_limit_bytes=limit),
        cost_estimate=pl.CostEstimate(flops=flops, bytes_accessed=1000, transcendentals=0),
        name=name,
    )(*operands)


def shape(dims, dtype):
    return jax.ShapeDtypeStruct(dims, dtype)


def tile_of(size, most):
    return max(t for t in range(128, most + 1, 128) if size % t == 0)


whole = pl.BlockSpec(memory_space=pltpu.VMEM)


def cut_of(hidden):
    return hidden // 256 * 128


def first_product(chunk, weight, weight_dim, cut, name):
    tokens = chunk.shape[0]
    hidden = weight.shape[1 - weight_dim]
    half, quarter = tokens // 2, tokens // 4
    widths = [cut] + [hidden - cut] * (cut < hidden)

    def body(chunk_ref, weight_ref, kept_ref, *sent_refs):
        for start in range(0, hidden, tile_of(hidden, 512) if cut == hidden else 128 if cut % 512 else 512):
            tile = min(hidden, start + (tile_of(hidden, 512) if cut == hidden else 128 if cut % 512 else 512)) - start
            span = pl.ds(start, tile)
            block = weight_ref[:, span] if weight_dim == 0 else weight_ref[span, :]
            total = contract(chunk_ref[...], block, 1, weight_dim)
            if start < cut:
                kept, sent = total[:half], total[half:]
            else:
                q = [total[i * quarter : (i + 1) * quarter] for i in range(4)]
                kept, sent = jnp.concatenate([q[0], q[2]], axis=0), jnp.concatenate([q[1], q[3]], axis=0)
            kept_ref[:, span] = kept
            sent_refs[start >= cut][:, pl.ds(start - cut * (start >= cut), tile)] = sent.astype(b16)

    return call(
        body,
        [chunk, weight],
        [whole] * 2,
        [shape((half, hidden), f32)] + [shape((half, w), b16) for w in widths],
        [whole] * (1 + len(widths)),
        (),
        name,
    )


def add_halves(kept_h, came_h, kept_g, came_g, flops):
    tokens, hidden = kept_h.shape
    half = tokens // 2
    tile = tile_of(hidden, 768)

    def body(kh, ch, kg, cg, sent_h, next_h, sent_g, next_g):
        for kept, came, sent, rest in ((kh, ch, sent_h, next_h), (kg, cg, sent_g, next_g)):
            total = kept[...] + came[...].astype(f32)
            rest[...] = total[:half]
            sent[...] = total[half:].astype(b16)

    block = pl.BlockSpec((tokens, tile), lambda i: (0, i))
    part = pl.BlockSpec((half, tile), lambda i: (0, i))
    return call(
        body,
        [kept_h, came_h, kept_g, came_g],
        [block] * 4,
        [shape((half, hidden), b16), shape((half, hidden), f32)] * 2,
        [part] * 4,
        (hidden // tile,),
        "add_halves",
        flops=flops,
    )


def add_crossed(kept_h, came_h, kept_g, came_g, cut, flops):
    tokens, hidden = kept_h.shape
    half = tokens // 2

    def body(kh, h0, h1, kg, g0, g1, sent_hg, next_h, sent_gh, next_g):
        for kept, came, rest, sents in ((kh, (h0, h1), next_h, (sent_hg, sent_gh)), (kg, (g0, g1), next_g, (sent_gh, sent_hg))):
            for side in range(2):
                span = pl.ds(cut * side, (cut, hidden - cut)[side])
                total = kept[:, span] + came[side][...].astype(f32)
                rest[:, span] = total[:half]
                sents[side][:, span] = total[half:].astype(b16)

    return call(
        body,
        [kept_h, *came_h, kept_g, *came_g],
        [whole] * 6,
        [shape((half, hidden), b16), shape((half, hidden), f32)] * 2,
        [whole] * 4,
        (),
        "add_crossed",
        flops=flops,
    )


def activate(kept_h, came_h, kept_g, came_g, cut):
    tokens, hidden = kept_h.shape
    tile = tile_of(cut, 768) if hidden % cut == 0 else 128

    def body(kh, ch, kg, cg, active_ref, delta_ref):
        came_h, came_g = ch[...].astype(f32), cg[...].astype(f32)
        if cut < hidden:
            straight = pl.program_id(0) < cut // tile
            came_h, came_g = jnp.where(straight, came_h, came_g), jnp.where(straight, came_g, came_h)
        value, slope = gelu_both(kh[...] + came_h)
        active_ref[...] = value.astype(b16)
        delta_ref[...] = ((kg[...] + came_g) * slope).astype(b16)

    block = pl.BlockSpec((tokens, tile), lambda i: (0, i))
    return call(
        body, [kept_h, came_h, kept_g, came_g], [block] * 4, [shape((tokens, hidden), b16)] * 2, [block] * 2,
        (hidden // tile,), "activate",
    )


def join_pairs(flops, *arrays):
    rows, columns = arrays[0].shape
    tile = tile_of(columns, 1536)

    def body(*refs):
        for i, out in enumerate(refs[len(arrays):]):
            out[pl.ds(0, rows), :] = refs[2 * i][...]
            out[pl.ds(rows, rows), :] = refs[2 * i + 1][...]

    return call(
        body,
        arrays,
        [pl.BlockSpec((rows, tile), lambda i: (0, i))] * len(arrays),
        [shape((2 * rows, columns), arrays[0].dtype)] * (len(arrays) // 2),
        [pl.BlockSpec((2 * rows, tile), lambda i: (0, i))] * (len(arrays) // 2),
        (columns // tile,),
        "join_pairs",
        7 * 2**20,
        flops,
    )


def input_product(delta, up_weight, quarter, cuts):
    tokens = delta.shape[0]
    width = up_weight.shape[0]
    tile = tile_of(width, 512)
    pairs = tokens // (2 * quarter)

    def body(delta_ref, weight_ref, kept_ref, *sent_refs):
        for start in range(0, width, tile):
            span = pl.ds(start, tile)
            total = contract(delta_ref[...], weight_ref[span, :], 1, 1)
            for i in range(pairs):
                first, second = 2 * i * quarter, (2 * i + 1) * quarter
                kept_ref[pl.ds(i * quarter, quarter), span] = total[first:second]
                sent_ref = sent_refs[cuts * i // pairs]
                sent_ref[pl.ds(i % (pairs // cuts) * quarter, quarter), span] = total[second : second + quarter]

    outs = [shape((tokens // 2, width), f32)] + [shape((tokens // (2 * cuts), width), f32)] * cuts
    return call(body, [delta, up_weight], [whole] * 2, outs, [whole] * (1 + cuts), (), "input_product")


def add_shares(kept_ref, *rest):
    total, cut = kept_ref[...], kept_ref.shape[0] // 2
    while rest:
        if rest[0].shape[0] == cut:
            total = total + jnp.concatenate([rest[0][...], rest[1][...]], axis=0)
            rest = rest[2:]
        else:
            total = total + rest[0][...].astype(f32)
            rest = rest[1:]
    return total


def steps_of(*sizes):
    return max(n for n in range(1, 7) if all(size % (128 * n) == 0 for size in sizes))


def weight_total(lefts, rights, columns):
    total = contract(lefts[0][:, columns], rights[0][...], 0, 0)
    for left, right in zip(lefts[1:], rights[1:]):
        total = total + contract(left[:, columns], right[...], 0, 0)
    return total


def early_grad(lefts, rights, held, name):
    rows, columns = lefts[0].shape[1], rights[0].shape[1]
    steps = steps_of(rows)
    tile = rows // steps
    count = len(lefts)

    def body(*refs):
        mine = pl.ds(pl.multiple_of(pl.program_id(0) * tile, tile), tile)
        total = weight_total(refs[:count], refs[count:-1], mine)
        if held:
            refs[-1][mine, :] = total
        else:
            refs[-1][...] = total

    return call(
        body,
        [*lefts, *rights],
        [whole] * (2 * count),
        shape((rows, columns), f32) if held else pltpu.HBM((rows, columns), f32),
        whole if held else pl.BlockSpec((tile, columns), lambda i: (i, 0)),
        (steps,),
        name,
        10 * 2**20,
    )


def late_grad(lefts, rights, partial, held, scale, name):
    rows, columns = partial.shape
    steps = steps_of(rows)
    tile = rows // steps
    count = len(lefts)

    def body(*refs):
        mine = pl.ds(pl.multiple_of(pl.program_id(0) * tile, tile), tile)
        total = weight_total(refs[:count], refs[count : 2 * count], mine)
        total = total + (refs[-2][mine, :] if held else refs[-2][...])
        refs[-1][...] = (total * scale).astype(b16)

    block = pl.BlockSpec((tile, columns), lambda i: (i, 0))
    return call(
        body,
        [*lefts, *rights, partial],
        [whole] * (2 * count) + [whole if held else block],
        pltpu.HBM((rows, columns), b16),
        block,
        (steps,),
        name,
        8 * 2**20,
    )


def shards(inputs, up_weight, down_weight, cotangent):
    n_row = lax.axis_size("row")
    replicas = lax.axis_size("dp")
    n_col = lax.axis_size("col")
    assert replicas == 2 and n_col == 4 and n_row % 4 == 0
    rows, width = inputs.shape
    quarter = rows // n_col
    own = lax.axis_index("col")

    def swap_x(a):
        return lax.ppermute(a, "col", [(i, i ^ 1) for i in range(n_col)])

    def swap_y(a):
        return lax.ppermute(a, "col", [(i, i ^ 2) for i in range(n_col)])

    def swap_dp(a):
        return lax.ppermute(a, "dp", [(0, 1), (1, 0)])

    def pass_row(a):
        return lax.ppermute(a, "row", [(i, (i + 1) % n_row) for i in range(n_row)])

    def reorder(a, order):
        blocks = [lax.dynamic_slice_in_dim(a, (own ^ bits) * quarter, quarter, 0) for bits in order]
        return jnp.concatenate(blocks, axis=0)

    x_outer, y_outer = (0, 2, 1, 3), (0, 1, 2, 3)

    def reorder_both():
        def body(own_ref, inputs_ref, cotangent_ref, out_ref, done):
            copies = []
            for ref, order, base in ((inputs_ref, x_outer, 0), (cotangent_ref, y_outer, rows)):
                for i in range(n_col):
                    source = pl.multiple_of((own_ref[0] ^ order[i]) * quarter, quarter)
                    copies.append(
                        pltpu.make_async_copy(
                            ref.at[pl.ds(source, quarter), :],
                            out_ref.at[pl.ds(base + i * quarter, quarter), :],
                            done.at[len(copies)],
                        )
                    )
            for copy in copies:
                copy.start()
            for copy in copies:
                copy.wait()

        return call(
            body,
            [own.astype(jnp.int32).reshape(1)]
            + [pltpu.with_memory_space_constraint(a, pltpu.HBM) for a in (inputs, cotangent)],
            [pl.BlockSpec(memory_space=pltpu.SMEM)] + [pl.BlockSpec(memory_space=pltpu.HBM)] * 2,
            shape((2 * rows, width), b16),
            whole,
            (),
            "reorder",
            scratch=[pltpu.SemaphoreType.DMA((2 * n_col,))],
        )

    if quarter % 16 == 0:
        moving = reorder_both()
    else:
        moving = jnp.concatenate([reorder(inputs, x_outer), reorder(cotangent, y_outer)], axis=0)

    group = n_row // 4
    tall = group * rows
    work = [{} for _ in range(4)]
    blocks = {0: [moving]}
    aligned = group == 1 and quarter % 16 == 0

    token = ()

    def after(*values):
        tied = lax.optimization_barrier((*values, *token))[: len(values)]
        return tied if len(values) > 1 else tied[0]

    def fetch(at):
        if at > 0:
            sent = blocks[at - 1][-1]
            if at > 2:
                sent = after(sent, *work[at - 1]["other"])[0]
            blocks[at] = [pass_row(sent)]
        while len(blocks[at]) < group:
            blocks[at].append(pass_row(blocks[at][-1]))

    def mirror(at):
        w = work[at]
        if at == 1:
            blocks[at][-1], *work[0]["h_came"] = after(blocks[at][-1], *work[0]["h_came"])
        elif at > 1:
            blocks[at][-1] = after(blocks[at][-1])
        w["mine"] = blocks[at][0] if group == 1 else jnp.concatenate(blocks[at])
        eighth = w["mine"].shape[0] // (2 * n_col)
        bounds = [0, *((), (3, 6), (4,), (4,))[at], 2 * n_col]
        w["other"] = [swap_dp(w["mine"][i * eighth : j * eighth]) for i, j in zip(bounds[:-1], bounds[1:])]

    def arrived(at):
        nonlocal token
        token = (*token, blocks[at][-1])

    def build_kernel(mine, *others):
        def body(mine_ref, *refs):
            pieces = [(ref, k) for ref in refs[:-2] for k in range(ref.shape[0] // quarter)]
            for part, out in enumerate(refs[-2:]):
                for i in range(n_col):
                    ref, k = pieces[part * n_col + i]
                    out[pl.ds(2 * i * quarter, quarter), :] = mine_ref[pl.ds(part * rows + i * quarter, quarter), :]
                    out[pl.ds((2 * i + 1) * quarter, quarter), :] = ref[pl.ds(k * quarter, quarter), :]

        return call(
            body, [mine, *others], [whole] * (1 + len(others)), [shape((2 * rows, width), b16)] * 2, [whole] * 2, (), "build"
        )

    def build(at):
        nonlocal token
        w = work[at]
        mine, *others = after(w["mine"], *w["other"])
        if aligned:
            w["in"], w["cot"] = build_kernel(mine, *others)
        else:
            other = jnp.concatenate(others)
            pair = [a.reshape(group, 2 * n_col, quarter, width).transpose(1, 0, 2, 3) for a in (mine, other)]
            w["in"], w["cot"] = jnp.stack(pair, axis=2).reshape(2, 2 * tall, width)
        token = (w["in"], w["cot"])

    hidden_of = up_weight.shape[1]
    cuts = [cut_of(hidden_of), hidden_of, hidden_of, hidden_of]

    def products(at):
        nonlocal token
        w = work[at]
        w["h"], *w["h_out"] = token = first_product(after(w["in"]), up_weight, 0, cuts[at], "hidden_product")
        w["g"], *w["g_out"] = token = first_product(after(w["cot"]), down_weight, 1, cuts[at], "delta_act_product")

    def reduce_first(at):
        w = work[at]
        if at == 0:
            w["h_came"] = [swap_x(w["h_out"][0]), swap_y(w["h_out"][1])]
            w["g_came"] = [swap_y(w["g_out"][0]), swap_x(w["g_out"][1])]
            return
        h_out, g_out = w["h_out"][0], w["g_out"][0]
        if at > 1:
            h_out, g_out = after(h_out, g_out)
        w["h_came"], w["g_came"] = swap_x(h_out), swap_y(g_out)

    def reduce_second(at):
        nonlocal token
        w = work[at]
        if at == 0:
            h, h0, h1, g, g0, g1 = after(w["h"], *w["h_came"], w["g"], *w["g_came"])
            sent_h, w["h"], sent_g, w["g"] = token = add_crossed(h, (h0, h1), g, (g0, g1), cuts[0], FIRST_SUM)
        else:
            sent_h, w["h"], sent_g, w["g"] = token = add_halves(*after(w["h"], w["h_came"], w["g"], w["g_came"]), 1000)
        w["h_came"], w["g_came"] = swap_y(sent_h), swap_x(sent_g)

    def gather_first(at):
        nonlocal token
        w = work[at]
        w["active"], w["delta"] = token = activate(*after(w["h"], w["h_came"], w["g"], w["g_came"]), cuts[at])
        w["delta_came"], w["active_came"] = swap_y(w["delta"]), swap_x(w["active"])

    def join(at, flops=1000):
        nonlocal token
        w = work[at]
        w["delta"], w["active"] = token = join_pairs(
            flops, *after(w["delta"], w["delta_came"], w["active"], w["active_came"])
        )

    def gather_second(at):
        w = work[at]
        join(at, ODD_JOIN if at % 2 else 1000)
        w["delta_came"], w["active_came"] = swap_x(w["delta"]), swap_y(w["active"])

    def add_kernel(dtype, *arrays):
        tile = tile_of(width, 768)

        def body(*refs):
            refs[-1][...] = add_shares(*refs[:-1]).astype(dtype)

        blocks_of = [pl.BlockSpec((a.shape[0], tile), lambda i: (0, i)) for a in arrays]
        return call(body, arrays, blocks_of, shape((rows, width), dtype), blocks_of[0], (width // tile,), "add")

    def share(at):
        nonlocal token
        w = work[at]
        delta = after(w["delta"])
        if not aligned:
            parts = contract(delta, up_weight, 1, 1).reshape(n_col, group, 2, quarter, width)
            token = (parts,)
            w["part"], w["part_came"] = parts[:, :, 0], swap_dp(parts[:, :, 1])
        else:
            w["part"], *sent = token = input_product(delta, up_weight, quarter, 1 if at < 2 else 2)
            w["part_came"] = [swap_dp(part) for part in sent]

    running = None

    def share_sum(at):
        nonlocal token, running
        w = work[at]
        if not aligned:
            part = w["part"] + w["part_came"]
            for step in range(at * group, (at + 1) * group):
                one = part[:, step - at * group].reshape(rows, width)
                if step == 0:
                    w["part"] = one
                else:
                    running = pass_row(one if running is None else running + one)
        elif at == 1:
            running = pass_row(add_kernel(f32, w["part"], *w["part_came"]))
        else:
            total = add_kernel(b16, *after(w["part"], *w["part_came"], running))
            token = (total,)
            running = pass_row(total)

    def settle():
        nonlocal token
        token = (*token, running)

    def early(names, held, name):
        nonlocal token
        values = after(*(work[at][k] for k in names for at in (0, 1)))
        token = (early_grad(values[:2], values[2:], held, name),)
        return token[0]

    def late(names, partial, held, name):
        nonlocal token
        values = after(*(work[at][k] for k in names for at in (2, 3)))
        token = (late_grad(values[:2], values[2:], partial, held, 1.0 / replicas, name),)
        return token[0]

    fetch(0)
    mirror(0)
    fetch(1)
    build(0)
    products(0)
    reduce_first(0)
    mirror(1)
    build(1)
    products(1)
    reduce_first(1)
    reduce_second(0)
    fetch(2)
    reduce_second(1)
    gather_first(0)
    gather_first(1)
    arrived(2)
    mirror(2)
    gather_second(0)
    build(2)
    products(2)
    fetch(3)
    gather_second(1)
    join(0)
    reduce_first(2)
    arrived(3)
    mirror(3)
    build(3)
    products(3)
    share(0)
    if not aligned:
        share_sum(0)
    join(1)
    reduce_first(3)
    share(1)
    share_sum(1)
    up_partial = early(("in", "delta"), True, "up_grad_early")
    reduce_second(2)
    reduce_second(3)
    gather_first(2)
    gather_first(3)
    gather_second(2)
    down_partial = early(("active", "cot"), False, "down_grad_early")
    settle()
    gather_second(3)
    join(2)
    share(2)
    share_sum(2)
    join(3)
    share(3)
    share_sum(3)
    up_grad = late(("in", "delta"), up_partial, True, "up_grad")
    down_grad = late(("active", "cot"), down_partial, False, "down_grad")

    def end_kernel(*arrays):
        tile = tile_of(width, 768)

        def body(own_ref, *refs):
            total = add_shares(*refs[:-1]).astype(b16)
            for i in range(n_col):
                target = pl.multiple_of((own_ref[0] ^ x_outer[i]) * quarter, quarter)
                refs[-1][pl.ds(target, quarter), :] = total[i * quarter : (i + 1) * quarter]

        blocks_of = [pl.BlockSpec((a.shape[0], tile), lambda i: (0, i)) for a in arrays]
        return call(
            body,
            [own.astype(jnp.int32).reshape(1), *arrays],
            [pl.BlockSpec(memory_space=pltpu.SMEM)] + blocks_of,
            shape((rows, width), b16),
            blocks_of[0],
            (width // tile,),
            "end",
        )

    if aligned:
        return (end_kernel(work[0]["part"], *work[0]["part_came"], running), up_grad, down_grad)
    input_grad = work[0]["part"] + running.astype(f32)
    input_grad = input_grad.astype(b16).reshape(2, 2, quarter, width).transpose(1, 0, 2, 3).reshape(rows, width)
    return (reorder(input_grad, y_outer), up_grad, down_grad)


def solution(mesh):
    tokens = P(("dp", "row"), "col")
    up, down = P("col", ("dp", "row")), P(("dp", "row"), "col")
    return jax.shard_map(
        shards,
        mesh=mesh,
        in_specs=(tokens, up, down, tokens),
        out_specs=(tokens, up, down),
        check_vma=False,
    )
```
